512 devices in a mesh: dom: 64 (over z_lo, y, core), sub: 8 (over z_hi, x).
Axes of the slice: x: 4, y: 8, z: 8 (z_hi: 2, z_lo: 4; z = z_hi * 4 + z_lo), core: 2. Of those that a mesh axis runs over, the one named last changes fastest.
Arguments:
- embeddings: float32 [131072, 256], P(('dom', 'sub')), may hold values from -1.5 to 1.5
- row_accum: float32 [131072], P(('dom', 'sub')), may hold values from 0.05 to 5
- relations: float32 [8, 256, 256], replicated, may hold values from -0.375 to 0.375
- rel_accum: float32 [8, 256], replicated, may hold values from 0.05 to 5
- matching: int32 [64], replicated, may hold values from 0 to 63, each once
- src_rows: int32 [262144], P(('dom', 'sub')), may hold values from 0 to 255
- dst_rows: int32 [262144], P(('dom', 'sub')), may hold values from 0 to 2047
- rel_ids: int32 [262144], P(('dom', 'sub')), may hold values from 0 to 7
- neg_rows: int32 [512, 512], P(('dom', 'sub')), may hold values from 0 to 2047
Outputs:
- new_embeddings: float32 [131072, 256], P(('dom', 'sub'))
- new_row_accum: float32 [131072], P(('dom', 'sub'))
- new_relations: float32 [8, 256, 256], replicated
- new_rel_accum: float32 [8, 256], replicated
The draws below stay inside these ranges and needn't reach their ends.
Inputs may be any that keep to these rules, and one draw needn't show every extreme that they name: matching is a permutation of the partitions 0 to 64 - 1.
All inputs are finite; a program needn't handle non-finite values.
Results may differ from the reference program's by a relative error of at most 0.0073.
Values may be sent and summed in bfloat16 or wider, within the bound.
No kernel may reach another device: no remote copies, remote signals or barrier semaphores. Data moves between devices by JAX's collectives and lax.ppermute only.
A program may use at most 64 MiB of HBM per device.

```python
import math
import jax
import jax.numpy as jnp
from jax import lax

D = 256
NREL = 8
NEG = 512
ROWS_DEV = 256
EDGES_DEV = 512
PROWS = 2048
SPANS_DEV = 1
N_DOM = 64
N_SUB = 8


def set_ends(values, rng, smallest, top_value):
    longest = values.shape.index(max(values.shape))
    spots = []
    for shift in (0, 1):
        where = [jax.random.randint(jax.random.fold_in(rng, axis), (), 0, length) for axis, length in enumerate(values.shape)]
        where[longest] = (where[longest] + shift) % values.shape[longest]
        spots.append(tuple(where))
    return values.at[spots[0]].set(smallest).at[spots[1]].set(top_value)


def level_of(rng, shape, split, smallest, largest):
    gain, own = 1.0, jax.random.fold_in(rng, 6)
    for dim, parts in split:
        heights = jnp.exp(jax.random.uniform(jax.random.fold_in(own, dim), (parts,), jnp.float32, smallest / len(split), largest / len(split)))
        gain = gain * jnp.repeat(heights, shape[dim] // parts).reshape([-1 if axis == dim else 1 for axis in range(len(shape))])
    return gain


def normal_values(stream_key, shape, spread, reach, split=(), kind=jnp.bfloat16):
    result = jax.random.normal(stream_key, shape, jnp.float32) * spread
    if len(split) > 0:
        result = level_of(stream_key, shape, split, -0.22, 0.18) * result
    return jnp.clip(result, min=-reach, max=reach).astype(kind)


def setup_inputs(seed: int = 0) -> dict:
    key_of = jax.random.split(jax.random.key(seed), 10)
    embeddings = normal_values(key_of[0], (N_DOM * PROWS, D), 0.25, 1.5, ((0, 512),), jnp.float32)
    row_accum = jnp.clip(jnp.exp(math.log(5.0) - 4.6051702 * jax.random.uniform(key_of[1], (N_DOM * PROWS,), jnp.float32) ** level_of(key_of[1], (N_DOM * PROWS,), ((0, 512),), -0.2, 0.2)), 0.05, 5.0)
    relations = normal_values(key_of[2], (NREL, D, D), D ** -0.5, 0.375, (), jnp.float32)
    rel_accum = jnp.clip(jnp.exp(jax.random.uniform(key_of[3], (NREL, D), jnp.float32, math.log(0.05), math.log(5.0))), 0.05, 5.0)
    matching = jax.random.permutation(key_of[4], N_DOM).astype(jnp.int32)
    src_rows = set_ends(jax.random.randint(key_of[5], (N_DOM * N_SUB * EDGES_DEV,), 0, ROWS_DEV), jax.random.fold_in(key_of[5], 1), 0, ROWS_DEV - 1).astype(jnp.int32)
    dst_rows = set_ends(jax.random.randint(key_of[6], (N_DOM * N_SUB * EDGES_DEV,), 0, PROWS), jax.random.fold_in(key_of[6], 1), 0, PROWS - 1).astype(jnp.int32)
    rel_ids = set_ends(jax.random.randint(key_of[7], (N_DOM * N_SUB * EDGES_DEV,), 0, NREL), jax.random.fold_in(key_of[7], 1), 0, NREL - 1).astype(jnp.int32)
    neg_rows = set_ends(jax.random.randint(key_of[8], (N_DOM * N_SUB * SPANS_DEV, NEG), 0, PROWS), jax.random.fold_in(key_of[8], 1), 0, PROWS - 1).astype(jnp.int32)
    return dict(embeddings=embeddings, row_accum=row_accum, relations=relations, rel_accum=rel_accum, matching=matching, src_rows=src_rows, dst_rows=dst_rows, rel_ids=rel_ids, neg_rows=neg_rows)


learn_rate = 0.1

def reference(embeddings, row_accum, relations, rel_accum, matching, src_rows, dst_rows, rel_ids, neg_rows):
    devices_all = N_DOM * N_SUB
    span_total = devices_all * SPANS_DEV
    emb_b = embeddings.astype(jnp.bfloat16)
    rel_b = relations.astype(jnp.bfloat16)
    edge_device = (jnp.arange(devices_all * EDGES_DEV, dtype=jnp.int32) // EDGES_DEV).astype(jnp.int32)
    partner = matching[edge_device // N_SUB]
    src_global = (edge_device * ROWS_DEV + src_rows).astype(jnp.int32)
    dst_global = (partner * PROWS + dst_rows).astype(jnp.int32)
    span_device = (jnp.arange(span_total, dtype=jnp.int32) // SPANS_DEV).astype(jnp.int32)
    neg_global = ((matching[span_device // N_SUB] * PROWS)[:, None] + neg_rows).astype(jnp.int32)
    slots = jnp.arange(NREL, dtype=jnp.int32)

    def step(rel_total, inputs):
        src_idx, dst_idx, rel_idx, neg_idx = inputs
        src_b = emb_b[src_idx]
        dst_b = emb_b[dst_idx]
        negs_b = emb_b[neg_idx]
        per_edge = rel_b[rel_idx].astype(jnp.float32)
        trans = jnp.einsum('cij,cj->ci', per_edge, src_b.astype(jnp.float32)).astype(jnp.bfloat16)
        pos_score = lax.optimization_barrier(jnp.sum(trans.astype(jnp.float32) * dst_b.astype(jnp.float32), axis=-1))
        neg_score = jnp.einsum('ni,mi->nm', trans.astype(jnp.float32), negs_b.astype(jnp.float32))
        g_pos = -jax.nn.sigmoid(-pos_score)
        g_neg = jax.nn.sigmoid(neg_score).astype(jnp.bfloat16)
        g_trans = (g_pos[:, None] * dst_b.astype(jnp.float32) + jnp.dot(g_neg, negs_b, preferred_element_type=jnp.float32)).astype(jnp.bfloat16)
        g_dst = (g_pos[:, None] * trans.astype(jnp.float32)).astype(jnp.bfloat16)
        g_negrow = jnp.einsum('nm,ni->mi', g_neg.astype(jnp.float32), trans.astype(jnp.float32)).astype(jnp.bfloat16)
        g_src = jnp.einsum('cij,ci->cj', per_edge, g_trans.astype(jnp.float32)).astype(jnp.bfloat16)
        rel_mask = (rel_idx[:, None] == slots[None, :]).astype(jnp.bfloat16)
        masked = (rel_mask[:, :, None] * g_trans[:, None, :]).reshape(NEG, NREL * D)
        rel_term = lax.dot_general(masked, src_b, (((0,), (0,)), ((), ())), preferred_element_type=jnp.float32)
        return (rel_total + rel_term, (g_src, g_dst, g_negrow))
    init = jnp.zeros((NREL * D, D), jnp.float32)
    rel_grad, (g_src, g_dst, g_negrow) = lax.scan(step, init, (src_global.reshape(span_total, NEG), dst_global.reshape(span_total, NEG), rel_ids.reshape(span_total, NEG), neg_global))
    total_rows = N_DOM * PROWS
    row_grad = jax.ops.segment_sum(g_src.reshape(-1, D).astype(jnp.float32), src_global, num_segments=total_rows)
    row_grad = row_grad + jax.ops.segment_sum(g_dst.reshape(-1, D).astype(jnp.float32), dst_global, num_segments=total_rows)
    row_grad = row_grad + jax.ops.segment_sum(g_negrow.reshape(-1, D).astype(jnp.float32), neg_global.reshape(-1), num_segments=total_rows)
    new_row_accum = row_accum + lax.optimization_barrier(jnp.mean(row_grad * row_grad, axis=-1))
    new_embeddings = embeddings - learn_rate * row_grad / jnp.sqrt(new_row_accum)[:, None]
    rel_flat = relations.reshape(NREL * D, D)
    accum_flat = rel_accum.reshape(NREL * D) + lax.optimization_barrier(jnp.mean(rel_grad * rel_grad, axis=-1))
    new_relations = rel_flat - learn_rate * rel_grad / jnp.sqrt(accum_flat)[:, None]
    return (new_embeddings, new_row_accum, new_relations.reshape(NREL, D, D), accum_flat.reshape(NREL, D))
```

```python
import jax
import jax.numpy as jnp
from jax import lax
from jax.sharding import Mesh, PartitionSpec as P

learn_rate = 0.1
AXES = ("zlo", "y", "core", "zhi", "x")
DOM = ("zlo", "y", "core")
SUB = ("zhi", "x")
bf16 = jnp.bfloat16
f32 = jnp.float32


def swap(value, axis):
    return lax.ppermute(value, axis, [(0, 1), (1, 0)])


def spread(value, axis):
    return lax.all_to_all(value, axis, split_axis=0, concat_axis=0, tiled=True)


def to_pieces(block):
    return block.reshape(32, 8, 2, 128).transpose(2, 0, 1, 3).reshape(64, 8, 128)


def from_pieces(pieces):
    return pieces.reshape(2, 32, 8, 128).transpose(1, 2, 0, 3).reshape(256, 256)


def body(
    embeddings, row_accum, relations, rel_accum, matching, src_rows, dst_rows, rel_ids, neg_rows
):
    core = lax.axis_index("core")
    zhi = lax.axis_index("zhi")
    own_b = embeddings.astype(bf16)
    index = jnp.stack([src_rows, rel_ids, dst_rows, neg_rows.reshape(-1)])
    other_b = swap(own_b, "zhi")
    other_index = swap(index, "zhi")

    arrived = spread(to_pieces(own_b), DOM)
    routed = jnp.take(arrived, matching, axis=0)
    partner_slice = spread(routed, DOM)
    rows4 = spread(jnp.broadcast_to(partner_slice[None], (4, 64, 8, 128)), "x")
    rows = rows4.reshape(4, 2, 256, 128).transpose(0, 2, 1, 3).reshape(1024, 256)

    rel_b = relations.astype(bf16)
    both = jnp.stack([index, other_index])
    src_i, rel_i = both[:, 0], both[:, 1]
    dst_i, neg_i = both[:, 2] - zhi * 1024, both[:, 3] - zhi * 1024
    local = lax.iota(jnp.int32, 256)
    src_hot = (src_i[:, :, None] == local).astype(bf16)
    source = jnp.einsum(
        "ser,srj->sej", src_hot, jnp.stack([own_b, other_b]), preferred_element_type=f32
    ).astype(bf16)
    slots = lax.iota(jnp.int32, 8)
    mask = (rel_i[:, :, None] == slots).astype(bf16)
    masked_src = (mask[:, :, :, None] * source[:, :, None, :]).reshape(1024, 2048)
    trans = jnp.dot(
        masked_src, rel_b.transpose(0, 2, 1).reshape(2048, 256), preferred_element_type=f32
    ).astype(bf16)
    wide = lax.iota(jnp.int32, 1024)
    counts = jnp.sum((neg_i[:, :, None] == wide).astype(f32), axis=1)

    score = jnp.dot(trans, rows.T, preferred_element_type=f32).reshape(2, 512, 1024)
    sig = jax.nn.sigmoid(score)
    hit = dst_i[:, :, None] == wide
    weight = counts[:, None, :] * sig + jnp.where(hit, sig - 1.0, 0.0)
    weight = weight.astype(bf16).reshape(1024, 1024)
    g_trans = jnp.dot(weight, rows, preferred_element_type=f32).astype(bf16)
    g_rows = lax.dot_general(weight, trans, (((0,), (0,)), ((), ())), preferred_element_type=f32)
    masked_g = (mask.reshape(1024, 8)[:, :, None] * g_trans[:, None, :]).reshape(1024, 2048)
    rel_grad = lax.dot_general(
        masked_g, source.reshape(1024, 256), (((0,), (0,)), ((), ())), preferred_element_type=f32
    ).reshape(2, 1024, 256)
    g_src = jnp.dot(masked_g, rel_b.reshape(2048, 256), preferred_element_type=f32)
    own = jnp.einsum(
        "ser,sej->srj", src_hot, g_src.astype(bf16).reshape(2, 512, 256), preferred_element_type=f32
    )
    own_here = own[0] + swap(own[1].astype(bf16), "zhi").astype(f32)

    kept = lax.dynamic_index_in_dim(rel_grad, core, 0, keepdims=False)
    given = lax.dynamic_index_in_dim(rel_grad, 1 - core, 0, keepdims=False)
    half = (kept + swap(given.astype(bf16), "core").astype(f32)).astype(bf16)
    out = jnp.stack(
        [g_rows.astype(bf16).reshape(4, 256, 256), half.reshape(4, 256, 256)], axis=1
    )
    got = jnp.sum(spread(out, "x").astype(f32), axis=0).astype(bf16)
    pieces = jnp.concatenate([to_pieces(got[0]), to_pieces(got[1])], axis=1)
    mid = spread(pieces, DOM)
    spots = lax.iota(jnp.int32, 64)
    inverse = jnp.sum(jnp.where(matching[None, :] == spots[:, None], spots[None, :], 0), axis=1)
    row_mid = jnp.take(mid[:, :8], inverse, axis=0)
    rel_mid = jnp.sum(mid[:, 8:].astype(f32).reshape(32, 2, 8, 128), axis=0)
    rel_mid = (rel_mid + swap(rel_mid, "zhi")).astype(bf16)
    rel_out = jnp.broadcast_to(rel_mid[None], (32, 2, 8, 128)).reshape(64, 8, 128)
    last = spread(jnp.concatenate([row_mid, rel_out], axis=1), DOM)
    returned = from_pieces(last[:, :8]).astype(f32)
    rel_one = from_pieces(last[:, 8:])
    rel_four = spread(jnp.broadcast_to(rel_one[None], (4, 256, 256)), "x")
    rel_rest = swap(rel_four, "core")
    first = jnp.where(core == 0, rel_four, rel_rest)
    second = jnp.where(core == 0, rel_rest, rel_four)
    total = jnp.concatenate([first, second], axis=0).astype(f32)

    row_grad = own_here + returned
    new_row_accum = row_accum + jnp.mean(row_grad * row_grad, axis=-1)
    new_embeddings = embeddings - learn_rate * row_grad / jnp.sqrt(new_row_accum)[:, None]
    new_rel_accum = rel_accum + jnp.mean(total * total, axis=-1)
    new_relations = relations - learn_rate * total / jnp.sqrt(new_rel_accum)[:, :, None]
    return new_embeddings, new_row_accum, new_relations, new_rel_accum


def solution(mesh):
    fine = Mesh(mesh.devices.reshape(4, 8, 2, 2, 4), AXES)
    placed = (
        P(AXES, None),
        P(AXES),
        P(),
        P(),
        P(),
        P(AXES),
        P(AXES),
        P(AXES),
        P(AXES, None),
    )
    return jax.shard_map(
        body,
        mesh=fine,
        in_specs=placed,
        out_specs=(P(AXES, None), P(AXES), P(), P()),
        check_vma=False,
    )
```

```python
import functools

import jax
import jax.numpy as jnp
from jax import lax
from jax.experimental import pallas as pl
from jax.experimental.pallas import tpu as pltpu
from jax.sharding import Mesh, PartitionSpec as P

learn_rate = 0.1
AXES = ("zlo", "y", "core", "zhi", "x")
DOM = ("zlo", "y", "core")
bf16 = jnp.bfloat16
f32 = jnp.float32
VMEM = pl.BlockSpec(memory_space=pltpu.VMEM)
SMEM = pl.BlockSpec(memory_space=pltpu.SMEM)
NN = (((1,), (0,)), ((), ()))
NT = (((1,), (1,)), ((), ()))


def shape(dims, dtype):
    return jax.ShapeDtypeStruct(dims, dtype)


def dot(a, b, dims=NN):
    return lax.dot_general(a, b, dims, preferred_element_type=f32)


def call(kernel, outs, scalars, args, flops=0, moved=0, scratch=()):
    return pl.pallas_call(
        kernel,
        out_shape=outs,
        in_specs=[SMEM] * scalars + [VMEM] * (len(args) - scalars),
        out_specs=jax.tree.map(lambda _: VMEM, outs),
        scratch_shapes=list(scratch),
        compiler_params=pltpu.CompilerParams(vmem_limit_bytes=40 * 1024 * 1024),
        cost_estimate=pl.CostEstimate(flops=flops, bytes_accessed=moved, transcendentals=0),
    )(*args)


def swap(value, axis):
    return lax.ppermute(value, axis, [(0, 1), (1, 0)])


def spread(value, axis):
    return lax.all_to_all(value, axis, split_axis=0, concat_axis=0, tiled=True)


def pack_kernel(emb, src, rel, dst, neg, pieces, pack):
    for h in range(2):
        pieces[h * 32 : (h + 1) * 32] = emb[:, h * 128 : (h + 1) * 128].reshape(32, 8, 128).astype(bf16)
    pack[0:256, :] = emb[...].astype(bf16)
    wide = jnp.concatenate([src[...], rel[...], dst[...], neg[...]], axis=0)
    high = wide // 256
    low = (wide - high * 256).astype(f32)
    both = jnp.concatenate([high.astype(f32), low], axis=0)
    pack[256:272, :] = jnp.concatenate([both[:, :256], both[:, 256:]], axis=0).astype(bf16)


def indices(pack):
    part = pack[256:272, :].astype(f32)
    both = jnp.concatenate([part[0:8], part[8:16]], axis=1)
    return both[0:4] * 256.0 + both[4:8]


def columns(value):
    return jnp.concatenate([value, value], axis=0).T


def lane_ids(rows, width):
    return lax.broadcasted_iota(jnp.int32, (rows, width), 1).astype(f32)


def trans_kernel(zhi, own, other, rel, trans, source, rel_b, counts):
    for r in range(8):
        rel_b[r] = rel[r].astype(bf16)
    base = (zhi[0] * 1024).astype(f32)
    ids = lane_ids(512, 256)
    for s, pack in enumerate((own, other)):
        index = indices(pack)
        column = columns(index)
        hot = (column[:, 0:1] == ids).astype(f32).astype(bf16)
        rows = dot(hot, pack[0:256, :])
        source[s * 512 : (s + 1) * 512, :] = rows.astype(bf16)
        total = jnp.zeros((512, 256), f32)
        for r in range(8):
            masked = jnp.where(column[:, 1:2] == float(r), rows, 0.0).astype(bf16)
            total = total + dot(masked, rel_b[r], NT)
        trans[s * 512 : (s + 1) * 512, :] = total.astype(bf16)
        hits = (column[:, 3:4] - base == lane_ids(512, 1024)).astype(f32)
        counts[s : s + 1, :] = jnp.sum(hits, axis=0, keepdims=True)
    counts[2:8, :] = jnp.zeros((6, 1024), f32)


def score_kernel(
    place, rows4, trans, source, counts, own, other, weight, g_trans, kept, given, rows
):
    core = place[0]
    base = (place[1] * 1024).astype(f32)
    for k in range(4):
        rows[k * 256 : (k + 1) * 256, :] = jnp.concatenate([rows4[k, 0], rows4[k, 1]], axis=1)
    index = [indices(own), indices(other)]
    ids = lane_ids(256, 1024)
    for b in range(4):
        s = b // 2
        column = columns(index[s])[(b % 2) * 256 : (b % 2 + 1) * 256]
        span = slice(b * 256, (b + 1) * 256)
        score = dot(trans[span, :], rows[...], NT)
        sig = 1.0 / (1.0 + jnp.exp(-score))
        count = counts[s : s + 1, :]
        hit = column[:, 2:3] - base == ids
        part = jnp.where(hit, (count + 1.0) * sig - 1.0, count * sig).astype(bf16)
        weight[span, :] = part
        g_trans[span, :] = dot(part, rows[...]).astype(bf16)
    turned = g_trans[...].astype(f32).T
    kinds = jnp.concatenate([index[0][1:2], index[1][1:2]], axis=1)
    for r in range(8):
        wanted = r + 4 * core if r < 4 else r - 4 * core
        masked = jnp.where(kinds == wanted.astype(f32), turned, 0.0).astype(bf16)
        grad = dot(masked, source[...]).astype(bf16)
        if r < 4:
            kept[r * 256 : (r + 1) * 256, :] = grad
        else:
            given[(r - 4) * 256 : (r - 3) * 256, :] = grad


def back_kernel(weight, trans, g_trans, rel_b, own, other, g_rows, own_here, own_there):
    turned = trans[...].astype(f32).T.astype(bf16)
    for k in range(4):
        part = dot(turned, weight[:, k * 256 : (k + 1) * 256])
        g_rows[k] = part.T.astype(bf16)
    sub_ids = lax.broadcasted_iota(jnp.int32, (256, 512), 0).astype(f32)
    for s, pack in enumerate((own, other)):
        index = indices(pack)
        column = columns(index)
        grad = g_trans[s * 512 : (s + 1) * 512, :].astype(f32)
        total = jnp.zeros((512, 256), f32)
        for r in range(8):
            masked = jnp.where(column[:, 1:2] == float(r), grad, 0.0).astype(bf16)
            total = total + dot(masked, rel_b[r])
        hot = (index[0:1, :] == sub_ids).astype(f32).astype(bf16)
        mine = dot(hot, total.astype(bf16))
        if s == 0:
            own_here[...] = mine
        else:
            own_there[...] = mine.astype(bf16)


def join_kernel(g_rows, kept, came, out):
    for k in range(4):
        out[k, 0:256, :] = g_rows[k]
        span = slice(k * 256, (k + 1) * 256)
        out[k, 256:512, :] = (kept[span, :].astype(f32) + came[span, :].astype(f32)).astype(bf16)


def pieces_kernel(got, out):
    for h in range(2):
        half = slice(h * 128, (h + 1) * 128)
        total = got[0, :, half].astype(f32)
        for k in range(1, 4):
            total = total + got[k, :, half].astype(f32)
        both = total.reshape(2, 32, 8, 128)
        out[h * 32 : (h + 1) * 32] = jnp.concatenate([both[0], both[1]], axis=1).astype(bf16)


def middle_kernel(mid, rel_sum):
    for c in range(2):
        total = jnp.zeros((8, 128), f32)
        for k in range(32):
            total = total + mid[2 * k + c].astype(f32)[8:16]
        rel_sum[c] = total


def route_kernel(matching, mid, rel_sum, rel_came, out):
    rel = [rel_sum[c] + rel_came[c] for c in range(2)]
    for d in range(64):
        target = matching[d]
        tail = jnp.where(target % 2 == 0, rel[0], rel[1])
        out[target] = jnp.concatenate([mid[d].astype(f32)[0:8], tail], axis=0).astype(bf16)


def rel_kernel(last, out):
    for h in range(2):
        part = last[h * 32 : (h + 1) * 32].astype(f32)[:, 8:16].reshape(256, 128).astype(bf16)
        for k in range(4):
            out[k, :, h * 128 : (h + 1) * 128] = part


def to_row(column):
    return jnp.broadcast_to(column, (256, 128)).T[0:1]


def to_column(row):
    return jnp.broadcast_to(row, (128, 256)).T[:, 0:1]


def rows_kernel(emb, accum, own_here, own_came, last, new_emb, new_accum):
    halves = [
        last[h * 32 : (h + 1) * 32].astype(f32)[:, 0:8].reshape(256, 128) for h in range(2)
    ]
    grad = own_here[...] + own_came[...].astype(f32) + jnp.concatenate(halves, axis=1)
    total = to_column(accum[...]) + jnp.mean(grad * grad, axis=1, keepdims=True)
    new_emb[...] = emb[...] - learn_rate * grad / jnp.sqrt(total)
    new_accum[...] = to_row(total)


def update_kernel(place, rel, accum, four, rest, new_rel, new_accum):
    core = place[0]
    old = jnp.concatenate([accum[...], accum[...]], axis=0)
    ordered = jnp.where(core == 0, old[0:8], old[4:12])
    column = ordered.T
    totals = []
    for r in range(8):
        target = r + 4 * core if r < 4 else r - 4 * core
        grad = (four[r] if r < 4 else rest[r - 4]).astype(f32)
        total = column[:, r : r + 1] + jnp.mean(grad * grad, axis=1, keepdims=True)
        new_rel[target] = rel[target] - learn_rate * grad / jnp.sqrt(total)
        totals.append(total)
    rows = jnp.concatenate(totals, axis=1).T
    twice = jnp.concatenate([rows, rows], axis=0)
    new_accum[...] = jnp.where(core == 0, twice[0:8], twice[4:12])


def body(
    embeddings, row_accum, relations, rel_accum, matching, src_rows, dst_rows, rel_ids, neg_rows
):
    core = lax.axis_index("core").astype(jnp.int32)
    zhi = lax.axis_index("zhi").astype(jnp.int32)
    place = jnp.stack([core, zhi])
    line = lambda v: v.reshape(1, 512)
    pieces, pack = call(
        pack_kernel,
        (shape((64, 8, 128), bf16), shape((272, 256), bf16)),
        0,
        (embeddings, line(src_rows), line(rel_ids), line(dst_rows), line(neg_rows)),
    )
    arrived = spread(pieces, DOM)
    routed = jnp.take(arrived, matching, axis=0)
    other = swap(pack, "zhi")
    partner_slice = spread(routed, DOM)
    other, routed = lax.optimization_barrier((other, routed))
    trans, source, rel_b, counts = call(
        trans_kernel,
        (
            shape((1024, 256), bf16),
            shape((1024, 256), bf16),
            shape((8, 256, 256), bf16),
            shape((8, 1024), f32),
        ),
        1,
        (zhi.reshape(1), pack, other, relations),
        flops=1_300_000_000,
        moved=4_000_000,
    )
    rows4 = spread(jnp.broadcast_to(partner_slice[None], (4, 64, 8, 128)), "x")
    weight, g_trans, kept, given = call(
        score_kernel,
        (
            shape((1024, 1024), bf16),
            shape((1024, 256), bf16),
            shape((1024, 256), bf16),
            shape((1024, 256), bf16),
        ),
        1,
        (place, rows4.reshape(4, 2, 256, 128), trans, source, counts, pack, other),
        flops=2_200_000_000,
        moved=4_000_000,
        scratch=[pltpu.VMEM((1024, 256), bf16)],
    )
    came = swap(given, "core")
    g_rows, own_here, own_there = call(
        back_kernel,
        (shape((4, 256, 256), bf16), shape((256, 256), f32), shape((256, 256), bf16)),
        0,
        (weight, trans, g_trans, rel_b, pack, other),
        flops=1_700_000_000,
        moved=4_000_000,
    )
    own_came = swap(own_there, "zhi")
    joined = call(join_kernel, shape((4, 512, 256), bf16), 0, (g_rows, kept, came), moved=2_000_000)
    got = spread(joined, "x")
    mid = spread(call(pieces_kernel, shape((64, 16, 128), bf16), 0, (got,), moved=1_000_000), DOM)
    rel_sum = call(middle_kernel, shape((2, 8, 128), f32), 0, (mid,), moved=256_000)
    rel_came = swap(rel_sum, "zhi")
    routed_back = call(
        route_kernel,
        shape((64, 16, 128), bf16),
        1,
        (matching, mid, rel_sum, rel_came),
        moved=512_000,
    )
    last = spread(routed_back, DOM)
    rel_four = spread(call(rel_kernel, shape((4, 256, 256), bf16), 0, (last,), moved=512_000), "x")
    new_embeddings, new_row_accum = call(
        rows_kernel,
        (shape((256, 256), f32), shape((1, 256), f32)),
        0,
        (embeddings, row_accum.reshape(1, 256), own_here, own_came, last),
        flops=1_000_000,
        moved=1_000_000,
    )
    rel_rest = swap(rel_four, "core")
    new_relations, new_rel_accum = call(
        update_kernel,
        (shape((8, 256, 256), f32), shape((8, 256), f32)),
        1,
        (place, relations, rel_accum, rel_four, rel_rest),
        moved=5_000_000,
    )
    return new_embeddings, new_row_accum.reshape(256), new_relations, new_rel_accum


def solution(mesh):
    fine = Mesh(mesh.devices.reshape(4, 8, 2, 2, 4), AXES)
    placed = (
        P(AXES, None),
        P(AXES),
        P(),
        P(),
        P(),
        P(AXES),
        P(AXES),
        P(AXES),
        P(AXES, None),
    )
    return jax.shard_map(
        body,
        mesh=fine,
        in_specs=placed,
        out_specs=(P(AXES, None), P(AXES), P(), P()),
        check_vma=False,
    )
```

```python
import functools

import jax
import jax.numpy as jnp
from jax import lax
from jax.experimental import pallas as pl
from jax.experimental.pallas import tpu as pltpu
from jax.sharding import Mesh, PartitionSpec as P

learn_rate = 0.1
AXES = ("zlo", "y", "core", "zhi", "x")
DOM = ("zlo", "y", "core")
bf16 = jnp.bfloat16
f32 = jnp.float32
VMEM = pl.BlockSpec(memory_space=pltpu.VMEM)
SMEM = pl.BlockSpec(memory_space=pltpu.SMEM)
NN = (((1,), (0,)), ((), ()))
NT = (((1,), (1,)), ((), ()))


def shape(dims, dtype):
    return jax.ShapeDtypeStruct(dims, dtype)


def dot(a, b, dims=NN):
    return lax.dot_general(a, b, dims, preferred_element_type=f32)


def call(kernel, outs, scalars, args, flops=0, moved=0, scratch=(), space=8):
    return pl.pallas_call(
        kernel,
        out_shape=outs,
        in_specs=[SMEM] * scalars + [VMEM] * (len(args) - scalars),
        out_specs=jax.tree.map(lambda _: VMEM, outs),
        scratch_shapes=list(scratch),
        compiler_params=pltpu.CompilerParams(vmem_limit_bytes=space * 1024 * 1024),
        cost_estimate=pl.CostEstimate(flops=flops, bytes_accessed=moved, transcendentals=0),
    )(*args)


def swap(value, axis):
    return lax.ppermute(value, axis, [(0, 1), (1, 0)])


def spread(value, axis):
    return lax.all_to_all(value, axis, split_axis=0, concat_axis=0, tiled=True)


def first_kernel(emb, pieces):
    for h in range(2):
        pieces[h * 32 : (h + 1) * 32] = emb[:, h * 128 : (h + 1) * 128].reshape(32, 8, 128).astype(bf16)


def pack_kernel(emb, src, rel, dst, neg, pack):
    pack[0:256, :] = emb[...].astype(bf16)
    wide = jnp.concatenate([src[...], rel[...], dst[...], neg[...]], axis=0)
    high = wide // 256
    low = (wide - high * 256).astype(f32)
    both = jnp.concatenate([high.astype(f32), low], axis=0)
    pack[256:272, :] = jnp.concatenate([both[:, :256], both[:, 256:]], axis=0).astype(bf16)


def take_kernel(matching, arrived, routed):
    for d in range(64):
        routed[d] = arrived[matching[d]]


def indices(pack):
    part = pack[256:272, :].astype(f32)
    both = jnp.concatenate([part[0:8], part[8:16]], axis=1)
    return both[0:4] * 256.0 + both[4:8]


def columns(value):
    return jnp.concatenate([value, value], axis=0).T


def lane_ids(rows, width):
    return lax.broadcasted_iota(jnp.int32, (rows, width), 1).astype(f32)


def trans_kernel(zhi, own, other, rel, trans, source, rel_b, counts):
    for r in range(8):
        rel_b[r] = rel[r].astype(bf16)
    base = (zhi[0] * 1024).astype(f32)
    ids = lane_ids(512, 256)
    for s, pack in enumerate((own, other)):
        index = indices(pack)
        column = columns(index)
        hot = (column[:, 0:1] == ids).astype(f32).astype(bf16)
        rows = dot(hot, pack[0:256, :])
        source[s * 512 : (s + 1) * 512, :] = rows.astype(bf16)
        total = jnp.zeros((512, 256), f32)
        for r in range(8):
            masked = jnp.where(column[:, 1:2] == float(r), rows, 0.0).astype(bf16)
            total = total + dot(masked, rel_b[r], NT)
        trans[s * 512 : (s + 1) * 512, :] = total.astype(bf16)
        hits = (column[:, 3:4] - base == lane_ids(512, 1024)).astype(f32)
        counts[s : s + 1, :] = jnp.sum(hits, axis=0, keepdims=True)
    counts[2:8, :] = jnp.zeros((6, 1024), f32)


def score_kernel(
    place, rows4, trans, source, counts, own, other, weight, g_trans, kept, given, rows
):
    core = place[0]
    base = (place[1] * 1024).astype(f32)
    for k in range(4):
        rows[k * 256 : (k + 1) * 256, :] = jnp.concatenate([rows4[k, 0], rows4[k, 1]], axis=1)
    index = [indices(own), indices(other)]
    ids = lane_ids(256, 1024)
    for b in range(4):
        s = b // 2
        column = columns(index[s])[(b % 2) * 256 : (b % 2 + 1) * 256]
        span = slice(b * 256, (b + 1) * 256)
        score = dot(trans[span, :], rows[...], NT)
        sig = 1.0 / (1.0 + jnp.exp(-score))
        count = counts[s : s + 1, :]
        hit = column[:, 2:3] - base == ids
        part = jnp.where(hit, (count + 1.0) * sig - 1.0, count * sig).astype(bf16)
        weight[span, :] = part
        g_trans[span, :] = dot(part, rows[...]).astype(bf16)
    turned = g_trans[...].astype(f32).T
    kinds = jnp.concatenate([index[0][1:2], index[1][1:2]], axis=1)
    for r in range(8):
        wanted = r + 4 * core if r < 4 else r - 4 * core
        masked = jnp.where(kinds == wanted.astype(f32), turned, 0.0).astype(bf16)
        grad = dot(masked, source[...]).astype(bf16)
        if r < 4:
            kept[r * 256 : (r + 1) * 256, :] = grad
        else:
            given[(r - 4) * 256 : (r - 3) * 256, :] = grad


def back_kernel(weight, trans, g_trans, rel_b, own, other, g_rows, own_here, own_there):
    turned = trans[...].astype(f32).T.astype(bf16)
    for k in range(4):
        part = dot(turned, weight[:, k * 256 : (k + 1) * 256])
        g_rows[k] = part.T.astype(bf16)
    sub_ids = lax.broadcasted_iota(jnp.int32, (256, 512), 0).astype(f32)
    for s, pack in enumerate((own, other)):
        index = indices(pack)
        column = columns(index)
        grad = g_trans[s * 512 : (s + 1) * 512, :].astype(f32)
        total = jnp.zeros((512, 256), f32)
        for r in range(8):
            masked = jnp.where(column[:, 1:2] == float(r), grad, 0.0).astype(bf16)
            total = total + dot(masked, rel_b[r])
        hot = (index[0:1, :] == sub_ids).astype(f32).astype(bf16)
        mine = dot(hot, total.astype(bf16))
        if s == 0:
            own_here[...] = mine
        else:
            own_there[...] = mine.astype(bf16)


def join_kernel(g_rows, kept, came, out):
    for k in range(4):
        out[k, 0:256, :] = g_rows[k]
        span = slice(k * 256, (k + 1) * 256)
        out[k, 256:512, :] = (kept[span, :].astype(f32) + came[span, :].astype(f32)).astype(bf16)


def pieces_kernel(got, out):
    for h in range(2):
        half = slice(h * 128, (h + 1) * 128)
        total = got[0, :, half].astype(f32)
        for k in range(1, 4):
            total = total + got[k, :, half].astype(f32)
        both = total.reshape(2, 32, 8, 128)
        out[h * 32 : (h + 1) * 32] = jnp.concatenate([both[0], both[1]], axis=1).astype(bf16)


def middle_kernel(mid, rel_sum):
    for c in range(2):
        total = jnp.zeros((8, 128), f32)
        for k in range(32):
            total = total + mid[2 * k + c].astype(f32)[8:16]
        rel_sum[c] = total


def route_kernel(matching, mid, rel_sum, rel_came, out):
    rel = [rel_sum[c] + rel_came[c] for c in range(2)]
    for d in range(64):
        target = matching[d]
        tail = jnp.where(target % 2 == 0, rel[0], rel[1])
        out[target] = jnp.concatenate([mid[d].astype(f32)[0:8], tail], axis=0).astype(bf16)


def rel_kernel(last, out):
    for h in range(2):
        part = last[h * 32 : (h + 1) * 32].astype(f32)[:, 8:16].reshape(256, 128).astype(bf16)
        for k in range(4):
            out[k, :, h * 128 : (h + 1) * 128] = part


def to_row(column):
    return jnp.broadcast_to(column, (256, 128)).T[0:1]


def to_column(row):
    return jnp.broadcast_to(row, (128, 256)).T[:, 0:1]


def rows_kernel(emb, accum, own_here, own_came, last, new_emb, new_accum):
    halves = [
        last[h * 32 : (h + 1) * 32].astype(f32)[:, 0:8].reshape(256, 128) for h in range(2)
    ]
    grad = own_here[...] + own_came[...].astype(f32) + jnp.concatenate(halves, axis=1)
    total = to_column(accum[...]) + jnp.mean(grad * grad, axis=1, keepdims=True)
    new_emb[...] = emb[...] - grad * (learn_rate / jnp.sqrt(total))
    new_accum[...] = to_row(total)


def update_kernel(place, rel, accum, grads, *rest):
    if len(rest) == 6:
        core, (seen, held, new_rel, new_accum, block, sem) = 1 - place[0], rest
    else:
        core, (new_rel, new_accum, block, sem) = place[0], rest
    old = jnp.concatenate([accum[...], accum[...]], axis=0)
    column = jnp.where(core == 0, old[0:8], old[4:12]).T
    totals = []
    for r in range(4):
        grad = grads[r].astype(f32)
        total = column[:, r : r + 1] + jnp.mean(grad * grad, axis=1, keepdims=True)
        block[r] = rel[4 * core + r] - grad * (learn_rate / jnp.sqrt(total))
        totals.append(total)
    copy = pltpu.make_async_copy(block, new_rel.at[pl.ds(4 * core, 4)], sem)
    copy.start()
    rows = jnp.concatenate(totals + totals, axis=1).T
    if len(rest) == 6:
        first = jnp.concatenate([held[...], held[...]], axis=0)
        mixed = jnp.concatenate([rows[0:4], first[0:4]], axis=0)
        turned = jnp.concatenate([first[0:4], rows[0:4]], axis=0)
        new_accum[...] = jnp.where(core == 0, mixed, turned)
    else:
        new_accum[...] = rows
    copy.wait()


def update_half(place, relations, rel_accum, grads, before=None):
    given = (place, relations, rel_accum, grads) + (before or ())
    specs = [SMEM, VMEM, VMEM, VMEM] + ([pl.BlockSpec(memory_space=pl.ANY), VMEM] if before else [])
    return pl.pallas_call(
        update_kernel,
        out_shape=(shape((8, 256, 256), f32), shape((8, 256), f32)),
        in_specs=specs,
        out_specs=(pl.BlockSpec(memory_space=pl.ANY), VMEM),
        scratch_shapes=[pltpu.VMEM((4, 256, 256), f32), pltpu.SemaphoreType.DMA],
        input_output_aliases={4: 0} if before else {},
        compiler_params=pltpu.CompilerParams(vmem_limit_bytes=8 * 1024 * 1024),
        cost_estimate=pl.CostEstimate(flops=0, bytes_accessed=3_000_000, transcendentals=0),
    )(*given)


def body(
    embeddings, row_accum, relations, rel_accum, matching, src_rows, dst_rows, rel_ids, neg_rows
):
    core = lax.axis_index("core").astype(jnp.int32)
    zhi = lax.axis_index("zhi").astype(jnp.int32)
    place = jnp.stack([core, zhi])
    line = lambda v: v.reshape(1, 512)
    pieces = call(first_kernel, shape((64, 8, 128), bf16), 0, (embeddings,), moved=400_000)
    arrived = spread(pieces, DOM)
    pack = call(
        pack_kernel,
        shape((272, 256), bf16),
        0,
        (embeddings, line(src_rows), line(rel_ids), line(dst_rows), line(neg_rows)),
        flops=2_000_000_000,
        moved=400_000,
    )
    other = swap(pack, "zhi")
    routed = call(take_kernel, shape((64, 8, 128), bf16), 1, (matching, arrived), moved=400_000)
    other, routed = lax.optimization_barrier((other, routed))
    partner_slice = spread(routed, DOM)
    trans, source, rel_b, counts = call(
        trans_kernel,
        (
            shape((1024, 256), bf16),
            shape((1024, 256), bf16),
            shape((8, 256, 256), bf16),
            shape((8, 1024), f32),
        ),
        1,
        (zhi.reshape(1), pack, other, relations),
        flops=1_300_000_000,
        space=16,
        moved=4_000_000,
    )
    rows4 = spread(jnp.broadcast_to(partner_slice[None], (4, 64, 8, 128)), "x")
    weight, g_trans, kept, given = call(
        score_kernel,
        (
            shape((1024, 1024), bf16),
            shape((1024, 256), bf16),
            shape((1024, 256), bf16),
            shape((1024, 256), bf16),
        ),
        1,
        (place, rows4.reshape(4, 2, 256, 128), trans, source, counts, pack, other),
        flops=2_200_000_000,
        space=20,
        moved=4_000_000,
        scratch=[pltpu.VMEM((1024, 256), bf16)],
    )
    came = swap(given, "core")
    g_rows, own_here, own_there = call(
        back_kernel,
        (shape((4, 256, 256), bf16), shape((256, 256), f32), shape((256, 256), bf16)),
        0,
        (weight, trans, g_trans, rel_b, pack, other),
        flops=1_700_000_000,
        space=16,
        moved=4_000_000,
    )
    own_came = swap(own_there, "zhi")
    joined = call(join_kernel, shape((4, 512, 256), bf16), 0, (g_rows, kept, came), moved=2_000_000)
    got = spread(joined, "x")
    own_came, got = lax.optimization_barrier((own_came, got))
    mid = spread(call(pieces_kernel, shape((64, 16, 128), bf16), 0, (got,), moved=1_000_000), DOM)
    rel_sum = call(middle_kernel, shape((2, 8, 128), f32), 0, (mid,), moved=256_000)
    rel_came = swap(rel_sum, "zhi")
    routed_back = call(
        route_kernel,
        shape((64, 16, 128), bf16),
        1,
        (matching, mid, rel_sum, rel_came),
        moved=512_000,
    )
    last = spread(routed_back, DOM)
    rel_four = spread(call(rel_kernel, shape((4, 256, 256), bf16), 0, (last,), moved=512_000), "x")
    new_embeddings, new_row_accum = call(
        rows_kernel,
        (shape((256, 256), f32), shape((1, 256), f32)),
        0,
        (embeddings, row_accum.reshape(1, 256), own_here, own_came, last),
        flops=1_000_000,
        moved=1_000_000,
    )
    rel_rest = swap(rel_four, "core")
    half = update_half(place, relations, rel_accum, rel_four)
    new_relations, new_rel_accum = update_half(place, relations, rel_accum, rel_rest, half)
    return new_embeddings, new_row_accum.reshape(256), new_relations, new_rel_accum


def solution(mesh):
    fine = Mesh(mesh.devices.reshape(4, 8, 2, 2, 4), AXES)
    placed = (
        P(AXES, None),
        P(AXES),
        P(),
        P(),
        P(),
        P(AXES),
        P(AXES),
        P(AXES),
        P(AXES, None),
    )
    return jax.shard_map(
        body,
        mesh=fine,
        in_specs=placed,
        out_specs=(P(AXES, None), P(AXES), P(), P()),
        check_vma=False,
    )
```

```python
import jax
import jax.numpy as jnp
from jax import lax
from jax.experimental import pallas as pl
from jax.experimental.pallas import tpu as pltpu
from jax.sharding import Mesh, PartitionSpec as P

learn_rate = 0.1
AXES = ("zlo", "y", "core", "zhi", "x")
DOM = ("zlo", "y", "core")
DOM_Z = DOM + ("zhi",)
bf16 = jnp.bfloat16
f32 = jnp.float32
VMEM = pl.BlockSpec(memory_space=pltpu.VMEM)
SMEM = pl.BlockSpec(memory_space=pltpu.SMEM)
NN = (((1,), (0,)), ((), ()))
NT = (((1,), (1,)), ((), ()))


def shape(dims, dtype):
    return jax.ShapeDtypeStruct(dims, dtype)


def dot(a, b, dims=NN):
    return lax.dot_general(a, b, dims, preferred_element_type=f32)


def call(kernel, outs, scalars, args, flops=0, moved=0, scratch=(), space=8):
    return pl.pallas_call(
        kernel,
        out_shape=outs,
        in_specs=[SMEM] * scalars + [VMEM] * (len(args) - scalars),
        out_specs=jax.tree.map(lambda _: VMEM, outs),
        scratch_shapes=list(scratch),
        compiler_params=pltpu.CompilerParams(vmem_limit_bytes=space * 1024 * 1024),
        cost_estimate=pl.CostEstimate(flops=flops, bytes_accessed=moved, transcendentals=0),
    )(*args)


def swap(value, axis):
    return lax.ppermute(value, axis, [(0, 1), (1, 0)])


def spread(value, axis):
    return lax.all_to_all(value, axis, split_axis=0, concat_axis=0, tiled=True)


def first_kernel(emb, pieces):
    for h in range(2):
        pieces[h * 32 : (h + 1) * 32] = emb[:, h * 128 : (h + 1) * 128].reshape(32, 8, 128).astype(bf16)


def pack_kernel(emb, src, rel, dst, neg, out):
    wide = jnp.concatenate([src[...], rel[...], dst[...], neg[...]], axis=0)
    high = wide // 256
    low = (wide - high * 256).astype(f32)
    both = jnp.concatenate([high.astype(f32), low], axis=0)
    index = jnp.concatenate([both[:, :256], both[:, 256:]], axis=0).astype(bf16)
    out[0:256, :] = emb[...].astype(bf16)
    out[256:272, :] = index


def take_kernel(matching, arrived, routed):
    for d in range(64):
        piece = arrived[matching[d]]
        routed[d, 0] = piece
        routed[d, 1] = piece


def indices(part):
    part = part.astype(f32)
    both = jnp.concatenate([part[0:8], part[8:16]], axis=1)
    return both[0:4] * 256.0 + both[4:8]


def columns(value):
    return jnp.concatenate([value, value], axis=0).T


def lane_ids(rows, width):
    return lax.broadcasted_iota(jnp.int32, (rows, width), 1)


def row_ids(x, rows):
    ids = lane_ids(rows, 512)
    return (ids + jnp.where(ids >= 256, 768, 0) + x * 256).astype(f32)


def trans_kernel(place, pack0, pack1, pack2, pack3, rel, trans, source, rel_b, counts, known):
    packs = (pack0, pack1, pack2, pack3)
    for r in range(8):
        rel_b[r] = rel[r].astype(bf16)
    ids = lane_ids(512, 256).astype(f32)
    wide = row_ids(place[2], 512)
    for s in range(4):
        index = indices(packs[s][256:272, :])
        known[s * 4 : (s + 1) * 4, :] = index
        column = columns(index)
        hot = (column[:, 0:1] == ids).astype(f32).astype(bf16)
        rows = dot(hot, packs[s][0:256, :])
        source[s * 512 : (s + 1) * 512, :] = rows.astype(bf16)
        total = jnp.zeros((512, 256), f32)
        for r in range(8):
            masked = jnp.where(column[:, 1:2] == float(r), rows, 0.0).astype(bf16)
            total = total + dot(masked, rel_b[r], NT)
        trans[s * 512 : (s + 1) * 512, :] = total.astype(bf16)
        hits = (column[:, 3:4] == wide).astype(f32)
        counts[s : s + 1, :] = jnp.sum(hits, axis=0, keepdims=True)
    counts[4:8, :] = jnp.zeros((4, 512), f32)


def score_kernel(
    place, rows_in, trans, source, counts, known, weight, g_trans, kept, given, rows
):
    core = place[0]
    for z in range(2):
        both = rows_in[:, z].reshape(2, 256, 128)
        rows[z * 256 : (z + 1) * 256, :] = jnp.concatenate([both[0], both[1]], axis=1)
    index = [known[s * 4 : (s + 1) * 4, :] for s in range(4)]
    ids = row_ids(place[2], 256)
    for b in range(8):
        s = b // 2
        column = columns(index[s])[(b % 2) * 256 : (b % 2 + 1) * 256]
        span = slice(b * 256, (b + 1) * 256)
        score = dot(trans[span, :], rows[...], NT)
        sig = 1.0 / (1.0 + jnp.exp(-score))
        count = counts[s : s + 1, :]
        hit = column[:, 2:3] == ids
        part = jnp.where(hit, (count + 1.0) * sig - 1.0, count * sig).astype(bf16)
        weight[span, :] = part
        g_trans[span, :] = dot(part, rows[...]).astype(bf16)
    turned = g_trans[...].astype(f32).T
    kinds = jnp.concatenate([part[1:2] for part in index], axis=1)
    for r in range(8):
        wanted = r + 4 * core if r < 4 else r - 4 * core
        masked = jnp.where(kinds == wanted.astype(f32), turned, 0.0).astype(bf16)
        grad = dot(masked, source[...]).astype(bf16)
        if r < 4:
            kept[r * 256 : (r + 1) * 256, :] = grad
        else:
            given[(r - 4) * 256 : (r - 3) * 256, :] = grad


def back_kernel(place, weight, trans, g_trans, rel_b, known, g_rows, own):
    turned = trans[...].astype(f32).T.astype(bf16)
    for z in range(2):
        part = dot(turned, weight[:, z * 256 : (z + 1) * 256])
        g_rows[z] = part.T.astype(bf16)
    sub_ids = lax.broadcasted_iota(jnp.int32, (256, 512), 0).astype(f32)
    for s in range(4):
        index = known[s * 4 : (s + 1) * 4, :]
        column = columns(index)
        grad = g_trans[s * 512 : (s + 1) * 512, :].astype(f32)
        total = jnp.zeros((512, 256), f32)
        for r in range(8):
            masked = jnp.where(column[:, 1:2] == float(r), grad, 0.0).astype(bf16)
            total = total + dot(masked, rel_b[r])
        hot = (index[0:1, :] == sub_ids).astype(f32).astype(bf16)
        own[(place[2] + s) % 4] = dot(hot, total.astype(bf16)).astype(bf16)


def join_kernel(own, kept, came, out):
    for k in range(4):
        out[k, 0:256, :] = own[k]
        span = slice(k * 256, (k + 1) * 256)
        out[k, 256:512, :] = (kept[span, :].astype(f32) + came[span, :].astype(f32)).astype(bf16)


def upper(tiles):
    return lax.broadcasted_iota(jnp.int32, tiles, len(tiles) - 2) % 8 < 4


def halves_swapped(tiles):
    return jnp.concatenate([tiles[:, 4:8], tiles[:, 0:4]], axis=1)


def pieces_kernel(got, g_rows, out, own_here):
    first = upper((32, 8, 128))
    for h in range(2):
        half = slice(h * 128, (h + 1) * 128)
        total = got[0, :, half].astype(f32)
        for k in range(1, 4):
            total = total + got[k, :, half].astype(f32)
        own_here[:, half] = total[0:256]
        rel = total[256:512].reshape(32, 8, 128)
        turned = halves_swapped(rel)
        near = g_rows[0, :, half].astype(f32).reshape(32, 8, 128)
        far = g_rows[1, :, half].astype(f32).reshape(32, 8, 128)
        span = slice(h * 32, (h + 1) * 32)
        out[span, 0] = jnp.concatenate(
            [jnp.where(first, near, far), jnp.where(first, rel, turned)], axis=1
        ).astype(bf16)
        out[span, 1] = jnp.concatenate(
            [jnp.where(first, far, near), jnp.where(first, turned, rel)], axis=1
        ).astype(bf16)


def route_kernel(place, matching, mid, out, sums):
    rel = [jnp.zeros((8, 128), f32), jnp.zeros((8, 128), f32)]
    for d in range(64):
        both = mid[d, 0].astype(f32) + mid[d, 1].astype(f32)
        sums[d] = both[0:8]
        rel[d % 2] = rel[d % 2] + both[8:16]
    first = upper((8, 128))
    near = first == (place[1] == 0)
    for d in range(64):
        target = matching[d]
        tail = jnp.where(target % 2 == 0, rel[0], rel[1])
        out[target, 0] = jnp.where(near, sums[d], tail).astype(bf16)
        out[target, 1] = jnp.where(near, tail, sums[d]).astype(bf16)


def rel_kernel(place, last, out):
    first = upper((32, 8, 128))
    for h in range(2):
        even = last[h * 32 : (h + 1) * 32, 0].astype(f32)
        odd = last[h * 32 : (h + 1) * 32, 1].astype(f32)
        straight = jnp.where(first, even, odd)
        crossed = halves_swapped(jnp.where(first, odd, even))
        part = jnp.where(place[1] == 0, crossed, straight).reshape(256, 128).astype(bf16)
        for k in range(4):
            out[k, :, h * 128 : (h + 1) * 128] = part


def to_row(column):
    return jnp.broadcast_to(column, (256, 128)).T[0:1]


def to_column(row):
    return jnp.broadcast_to(row, (128, 256)).T[:, 0:1]


def rows_kernel(place, emb, accum, own_here, last, new_emb, new_accum):
    first = upper((64, 8, 128)) == (place[1] == 0)
    rows = jnp.where(first, last[:, 0].astype(f32), last[:, 1].astype(f32))
    halves = [rows[h * 32 : (h + 1) * 32].reshape(256, 128) for h in range(2)]
    grad = own_here[...] + jnp.concatenate(halves, axis=1)
    total = to_column(accum[...]) + jnp.mean(grad * grad, axis=1, keepdims=True)
    new_emb[...] = emb[...] - grad * (learn_rate / jnp.sqrt(total))
    new_accum[...] = to_row(total)


def update_kernel(place, rel, accum, grads, *rest):
    if len(rest) == 6:
        core, (seen, held, new_rel, new_accum, block, sem) = 1 - place[0], rest
    else:
        core, (new_rel, new_accum, block, sem) = place[0], rest
    old = jnp.concatenate([accum[...], accum[...]], axis=0)
    column = jnp.where(core == 0, old[0:8], old[4:12]).T
    totals = []
    for r in range(4):
        grad = grads[r].astype(f32)
        total = column[:, r : r + 1] + jnp.mean(grad * grad, axis=1, keepdims=True)
        block[r] = rel[4 * core + r] - grad * (learn_rate / jnp.sqrt(total))
        totals.append(total)
    copy = pltpu.make_async_copy(block, new_rel.at[pl.ds(4 * core, 4)], sem)
    copy.start()
    rows = jnp.concatenate(totals + totals, axis=1).T
    if len(rest) == 6:
        first = jnp.concatenate([held[...], held[...]], axis=0)
        mixed = jnp.concatenate([rows[0:4], first[0:4]], axis=0)
        turned = jnp.concatenate([first[0:4], rows[0:4]], axis=0)
        new_accum[...] = jnp.where(core == 0, mixed, turned)
    else:
        new_accum[...] = rows
    copy.wait()


def update_half(place, relations, rel_accum, grads, before=None):
    given = (place, relations, rel_accum, grads) + (before or ())
    specs = [SMEM, VMEM, VMEM, VMEM] + ([pl.BlockSpec(memory_space=pl.ANY), VMEM] if before else [])
    return pl.pallas_call(
        update_kernel,
        out_shape=(shape((8, 256, 256), f32), shape((8, 256), f32)),
        in_specs=specs,
        out_specs=(pl.BlockSpec(memory_space=pl.ANY), VMEM),
        scratch_shapes=[pltpu.VMEM((4, 256, 256), f32), pltpu.SemaphoreType.DMA],
        input_output_aliases={4: 0} if before else {},
        compiler_params=pltpu.CompilerParams(vmem_limit_bytes=8 * 1024 * 1024),
        cost_estimate=pl.CostEstimate(flops=0, bytes_accessed=3_000_000, transcendentals=0),
    )(*given)


def body(
    embeddings, row_accum, relations, rel_accum, matching, src_rows, dst_rows, rel_ids, neg_rows
):
    place = jnp.stack([lax.axis_index(name) for name in ("core", "zhi", "x")]).astype(jnp.int32)
    line = lambda v: v.reshape(1, 512)
    pieces = call(first_kernel, shape((64, 8, 128), bf16), 0, (embeddings,), moved=400_000)
    arrived = spread(pieces, DOM)
    pack = call(
        pack_kernel,
        shape((272, 256), bf16),
        0,
        (embeddings, line(src_rows), line(rel_ids), line(dst_rows), line(neg_rows)),
        flops=2_000_000_000,
        moved=400_000,
    )
    packs = [pack] + [
        lax.ppermute(pack, "x", [(i, (i - k) % 4) for i in range(4)]) for k in range(1, 4)
    ]
    packs[1], packs[3], arrived = lax.optimization_barrier((packs[1], packs[3], arrived))
    routed = call(take_kernel, shape((64, 2, 8, 128), bf16), 1, (matching, arrived), moved=400_000)
    rows_in = spread(routed.reshape(128, 8, 128), DOM_Z).reshape(64, 2, 8, 128)
    trans, source, rel_b, counts, known = call(
        trans_kernel,
        (
            shape((2048, 256), bf16),
            shape((2048, 256), bf16),
            shape((8, 256, 256), bf16),
            shape((8, 512), f32),
            shape((16, 512), f32),
        ),
        1,
        (place, *packs, relations),
        flops=2_500_000_000,
        moved=6_000_000,
        space=16,
    )
    weight, g_trans, kept, given = call(
        score_kernel,
        (
            shape((2048, 512), bf16),
            shape((2048, 256), bf16),
            shape((1024, 256), bf16),
            shape((1024, 256), bf16),
        ),
        1,
        (place, rows_in, trans, source, counts, known),
        flops=3_200_000_000,
        moved=6_000_000,
        scratch=[pltpu.VMEM((512, 256), bf16)],
        space=20,
    )
    came = swap(given, "core")
    g_rows, own = call(
        back_kernel,
        (shape((2, 256, 256), bf16), shape((4, 256, 256), bf16)),
        1,
        (place, weight, trans, g_trans, rel_b, known),
        flops=3_000_000_000,
        moved=6_000_000,
        space=16,
    )
    joined = call(join_kernel, shape((4, 512, 256), bf16), 0, (own, kept, came), moved=2_000_000)
    got = spread(joined, "x")
    out, own_here = call(
        pieces_kernel,
        (shape((64, 2, 16, 128), bf16), shape((256, 256), f32)),
        0,
        (got, g_rows),
        moved=2_000_000,
    )
    mid = spread(out.reshape(128, 16, 128), DOM_Z).reshape(64, 2, 16, 128)
    routed_back = call(
        route_kernel,
        shape((64, 2, 8, 128), bf16),
        2,
        (place, matching, mid),
        moved=512_000,
        scratch=[pltpu.VMEM((64, 8, 128), f32)],
    )
    last = spread(routed_back.reshape(128, 8, 128), DOM_Z).reshape(64, 2, 8, 128)
    rel_four = spread(
        call(rel_kernel, shape((4, 256, 256), bf16), 1, (place, last), moved=512_000), "x"
    )
    new_embeddings, new_row_accum = call(
        rows_kernel,
        (shape((256, 256), f32), shape((1, 256), f32)),
        1,
        (place, embeddings, row_accum.reshape(1, 256), own_here, last),
        flops=1_000_000,
        moved=1_000_000,
    )
    rel_rest = swap(rel_four, "core")
    half = update_half(place, relations, rel_accum, rel_four)
    new_relations, new_rel_accum = update_half(place, relations, rel_accum, rel_rest, half)
    return new_embeddings, new_row_accum.reshape(256), new_relations, new_rel_accum


def solution(mesh):
    fine = Mesh(mesh.devices.reshape(4, 8, 2, 2, 4), AXES)
    placed = (
        P(AXES, None),
        P(AXES),
        P(),
        P(),
        P(),
        P(AXES),
        P(AXES),
        P(AXES),
        P(AXES, None),
    )
    return jax.shard_map(
        body,
        mesh=fine,
        in_specs=placed,
        out_specs=(P(AXES, None), P(AXES), P(), P()),
        check_vma=False,
    )
```

```python
import jax
import jax.numpy as jnp
from jax import lax
from jax.experimental import pallas as pl
from jax.experimental.pallas import tpu as pltpu
from jax.sharding import Mesh, PartitionSpec as P

learn_rate = 0.1
AXES = ("zlo", "y", "core", "zhi", "x")
DOM = ("zlo", "y", "core")
DOM_Z = DOM + ("zhi",)
bf16 = jnp.bfloat16
f32 = jnp.float32
VMEM = pl.BlockSpec(memory_space=pltpu.VMEM)
ANY = pl.BlockSpec(memory_space=pltpu.HBM)
SMEM = pl.BlockSpec(memory_space=pltpu.SMEM)
NN = (((1,), (0,)), ((), ()))
NT = (((1,), (1,)), ((), ()))


def shape(dims, dtype):
    return jax.ShapeDtypeStruct(dims, dtype)


def dot(a, b, dims=NN):
    return lax.dot_general(a, b, dims, preferred_element_type=f32)


def call(kernel, outs, scalars, args, flops=0, moved=0, scratch=(), space=8, far=(), far_outs=()):
    specs = [SMEM] * scalars + [ANY if k in far else VMEM for k in range(scalars, len(args))]
    many = isinstance(outs, tuple)
    return pl.pallas_call(
        kernel,
        out_shape=outs,
        in_specs=specs,
        out_specs=tuple(ANY if k in far_outs else VMEM for k in range(len(outs))) if many else VMEM,
        scratch_shapes=list(scratch),
        compiler_params=pltpu.CompilerParams(vmem_limit_bytes=space * 1024 * 1024),
        cost_estimate=pl.CostEstimate(flops=flops, bytes_accessed=moved, transcendentals=0),
    )(*args)


def swap(value, axis):
    return lax.ppermute(value, axis, [(0, 1), (1, 0)])


def spread(value, axis):
    return lax.all_to_all(value, axis, split_axis=0, concat_axis=0, tiled=True)


def first_kernel(emb, src, rel, dst, neg, pieces, pack, rows, index, sems):
    copies = [pltpu.make_async_copy(emb, rows, sems.at[0])]
    for k, part in enumerate((src, rel, dst, neg)):
        copies.append(pltpu.make_async_copy(part, index.at[k], sems.at[k + 1]))
    for copy in copies:
        copy.start()
    for copy in copies:
        copy.wait()
    wide = jnp.concatenate([index[k] for k in range(4)], axis=0)
    high = wide // 256
    low = (wide - high * 256).astype(f32)
    both = jnp.concatenate([high.astype(f32), low], axis=0)
    pack[256:272, :] = jnp.concatenate([both[:, :256], both[:, 256:]], axis=0).astype(bf16)
    pack[0:256, :] = rows[...].astype(bf16)
    for h in range(2):
        half = rows[:, h * 128 : (h + 1) * 128]
        pieces[h * 32 : (h + 1) * 32] = half.reshape(32, 8, 128).astype(bf16)


def take_kernel(matching, arrived, routed):
    for d in range(64):
        piece = arrived[matching[d]]
        routed[d, 0] = piece
        routed[d, 1] = piece


def indices(part):
    part = part.astype(f32)
    both = jnp.concatenate([part[0:8], part[8:16]], axis=1)
    return both[0:4] * 256.0 + both[4:8]


def columns(value):
    return jnp.concatenate([value, value], axis=0).T


def lane_ids(rows, width):
    return lax.broadcasted_iota(jnp.int32, (rows, width), 1)


def row_ids(x, rows):
    ids = lane_ids(rows, 512)
    return (ids + jnp.where(ids >= 256, 768, 0) + x * 256).astype(f32)


def by_relation(kinds, rows):
    parts = [jnp.where(kinds == float(r), rows, 0.0).astype(bf16) for r in range(8)]
    return jnp.concatenate(parts, axis=1)


def trans_kernel(place, packs, rel, counts, known, *rest):
    outs, (trans, source, *rel_b), sems = rest[: len(rest) // 2], rest[len(rest) // 2 : -1], rest[-1]
    stack = jnp.concatenate([rel[r].astype(bf16) for r in range(8)], axis=1)
    copies = []
    if rel_b:
        for r in range(8):
            rel_b[0][r] = rel[r].astype(bf16)
        copies.append(pltpu.make_async_copy(rel_b[0], outs[2], sems.at[2]))
        copies[-1].start()
    ids = lane_ids(512, 256).astype(f32)
    wide = row_ids(place[2], 512)
    for s in range(2):
        index = indices(packs[s * 272 + 256 : s * 272 + 272, :])
        known[s * 4 : (s + 1) * 4, :] = index
        column = columns(index)
        hot = (column[:, 0:1] == ids).astype(f32).astype(bf16)
        rows = dot(hot, packs[s * 272 : s * 272 + 256, :])
        source[s * 512 : (s + 1) * 512, :] = rows.astype(bf16)
        trans[s * 512 : (s + 1) * 512, :] = dot(by_relation(column[:, 1:2], rows), stack, NT).astype(bf16)
        hits = (column[:, 3:4] == wide).astype(f32)
        counts[s : s + 1, :] = jnp.sum(hits, axis=0, keepdims=True)
    counts[2:8, :] = jnp.zeros((6, 512), f32)
    for k, held in enumerate((trans, source)):
        copies.append(pltpu.make_async_copy(held, outs[k], sems.at[k]))
        copies[-1].start()
    for copy in copies:
        copy.wait()


def score_kernel(
    place, rows_in, counts0, counts1, known0, known1, trans0, trans1, source0, source1,
    weight, g_trans, kept, given, rows, trans, source, sems
):
    copies = []
    for k, (part, held) in enumerate(
        ((trans0, trans), (trans1, trans), (source0, source), (source1, source))
    ):
        span = pl.ds((k % 2) * 1024, 1024)
        copies.append(pltpu.make_async_copy(part, held.at[span, :], sems.at[k]))
        copies[-1].start()
    core = place[0]
    for z in range(2):
        both = rows_in[:, z].reshape(2, 256, 128)
        rows[z * 256 : (z + 1) * 256, :] = jnp.concatenate([both[0], both[1]], axis=1)
    index = [known[s * 4 : (s + 1) * 4, :] for known in (known0, known1) for s in range(2)]
    ids = row_ids(place[2], 256)
    for b in range(8):
        if b % 4 == 0:
            copies[b // 4].wait()
        s = b // 2
        column = columns(index[s])[(b % 2) * 256 : (b % 2 + 1) * 256]
        span = slice(b * 256, (b + 1) * 256)
        score = dot(trans[span, :], rows[...], NT)
        sig = 1.0 / (1.0 + jnp.exp(-score))
        count = (counts0, counts1)[s // 2][s % 2 : s % 2 + 1, :]
        hit = column[:, 2:3] == ids
        part = jnp.where(hit, (count + 1.0) * sig - 1.0, count * sig).astype(bf16)
        weight[span, :] = part
        g_trans[span, :] = dot(part, rows[...]).astype(bf16)
    turned = g_trans[...].astype(f32).T
    kinds = jnp.concatenate([part[1:2] for part in index], axis=1)
    copies[2].wait()
    copies[3].wait()
    for r in range(8):
        wanted = r + 4 * core if r < 4 else r - 4 * core
        masked = jnp.where(kinds == wanted.astype(f32), turned, 0.0).astype(bf16)
        grad = dot(masked, source[...]).astype(bf16)
        if r < 4:
            kept[r * 256 : (r + 1) * 256, :] = grad
        else:
            given[(r - 4) * 256 : (r - 3) * 256, :] = grad


def back_kernel(
    place, weight, g_trans, known0, known1, trans0, trans1, rel_in, mine, theirs, own,
    trans, rel_b, sems
):
    copies = [pltpu.make_async_copy(rel_in, rel_b, sems.at[2])]
    for k, part in enumerate((trans0, trans1)):
        span = pl.ds(k * 1024, 1024)
        copies.append(pltpu.make_async_copy(part, trans.at[span, :], sems.at[k]))
    for copy in copies:
        copy.start()
    sub_ids = lax.broadcasted_iota(jnp.int32, (256, 512), 0).astype(f32)
    copies[0].wait()
    stack = rel_b[...].reshape(2048, 256)
    for s in range(4):
        index = (known0, known1)[s // 2][(s % 2) * 4 : (s % 2 + 1) * 4, :]
        grad = g_trans[s * 512 : (s + 1) * 512, :].astype(f32)
        total = dot(by_relation(columns(index)[:, 1:2], grad), stack)
        hot = (index[0:1, :] == sub_ids).astype(f32).astype(bf16)
        own[place[2] ^ s] = dot(hot, total.astype(bf16)).astype(bf16)
    copies[1].wait()
    copies[2].wait()
    turned = trans[...].astype(f32).T.astype(bf16)
    near = dot(turned, weight[:, 0:256]).T
    far = dot(turned, weight[:, 256:512]).T
    mine[...] = jnp.where(place[1] == 0, near, far)
    theirs[...] = jnp.where(place[1] == 0, far, near).astype(bf16)


def join_kernel(own, kept, came, out):
    for k in range(4):
        out[k, 0:256, :] = own[k]
        span = slice(k * 256, (k + 1) * 256)
        out[k, 256:512, :] = (kept[span, :].astype(f32) + came[span, :].astype(f32)).astype(bf16)


def upper(tiles):
    return lax.broadcasted_iota(jnp.int32, tiles, len(tiles) - 2) % 8 < 4


def pieces_kernel(got, mine, came, out, own_here):
    first = upper((32, 8, 128))
    for h in range(2):
        half = slice(h * 128, (h + 1) * 128)
        total = got[0, :, half].astype(f32)
        for k in range(1, 4):
            total = total + got[k, :, half].astype(f32)
        own_here[:, half] = total[0:256]
        rel = total[256:512].reshape(32, 8, 128)
        rows = (mine[:, half] + came[:, half].astype(f32)).reshape(32, 8, 128)
        span = slice(h * 32, (h + 1) * 32)
        out[span, 0] = jnp.where(first, rows, rel).astype(bf16)
        out[span, 1] = jnp.where(first, rel, rows).astype(bf16)


def route_kernel(place, matching, mid, out):
    rel = [jnp.zeros((8, 128), f32), jnp.zeros((8, 128), f32)]
    for d in range(64):
        rel[d % 2] = rel[d % 2] + (mid[d, 0].astype(f32) + mid[d, 1].astype(f32))
    near = upper((8, 128)) == (place[1] == 0)
    for d in range(64):
        target = matching[d]
        tail = jnp.where(target % 2 == 0, rel[0], rel[1])
        for z in range(2):
            out[target, z] = jnp.where(near, mid[d, z].astype(f32), tail).astype(bf16)


def rel_kernel(last, out):
    first = upper((32, 8, 128))
    for h in range(2):
        even = last[h * 32 : (h + 1) * 32, 0].astype(f32)
        odd = last[h * 32 : (h + 1) * 32, 1].astype(f32)
        part = jnp.where(first, odd, even).reshape(256, 128).astype(bf16)
        for k in range(4):
            out[k, :, h * 128 : (h + 1) * 128] = part


def to_row(column):
    return jnp.broadcast_to(column, (256, 128)).T[0:1]


def to_column(row):
    return jnp.broadcast_to(row, (128, 256)).T[:, 0:1]


def rows_kernel(emb, accum, own_here, last, new_emb, new_accum):
    first = upper((64, 8, 128))
    rows = jnp.where(first, last[:, 0].astype(f32), last[:, 1].astype(f32))
    halves = [rows[h * 32 : (h + 1) * 32].reshape(256, 128) for h in range(2)]
    grad = own_here[...] + jnp.concatenate(halves, axis=1)
    total = to_column(accum[...]) + jnp.mean(grad * grad, axis=1, keepdims=True)
    new_emb[...] = emb[...] - grad * (learn_rate / jnp.sqrt(total))
    new_accum[...] = to_row(total)


def update_kernel(place, rel, accum, grads, *rest):
    if len(rest) == 6:
        core, (seen, held, new_rel, new_accum, block, sem) = 1 - place[0], rest
    else:
        core, (new_rel, new_accum, block, sem) = place[0], rest
    old = jnp.concatenate([accum[...], accum[...]], axis=0)
    column = jnp.where(core == 0, old[0:8], old[4:12]).T
    totals = []
    for r in range(4):
        grad = grads[r].astype(f32)
        total = column[:, r : r + 1] + jnp.mean(grad * grad, axis=1, keepdims=True)
        block[r] = rel[4 * core + r] - grad * (learn_rate / jnp.sqrt(total))
        totals.append(total)
    copy = pltpu.make_async_copy(block, new_rel.at[pl.ds(4 * core, 4)], sem)
    copy.start()
    rows = jnp.concatenate(totals + totals, axis=1).T
    if len(rest) == 6:
        first = jnp.concatenate([held[...], held[...]], axis=0)
        mixed = jnp.concatenate([rows[0:4], first[0:4]], axis=0)
        turned = jnp.concatenate([first[0:4], rows[0:4]], axis=0)
        new_accum[...] = jnp.where(core == 0, mixed, turned)
    else:
        new_accum[...] = rows
    copy.wait()


def update_half(place, relations, rel_accum, grads, before=None):
    given = (place, relations, rel_accum, grads) + (before or ())
    specs = [SMEM, VMEM, VMEM, VMEM] + ([ANY, VMEM] if before else [])
    return pl.pallas_call(
        update_kernel,
        out_shape=(shape((8, 256, 256), f32), shape((8, 256), f32)),
        in_specs=specs,
        out_specs=(ANY, VMEM),
        scratch_shapes=[pltpu.VMEM((4, 256, 256), f32), pltpu.SemaphoreType.DMA],
        input_output_aliases={4: 0} if before else {},
        compiler_params=pltpu.CompilerParams(vmem_limit_bytes=62 * 1024 * 1024),
        cost_estimate=pl.CostEstimate(flops=0, bytes_accessed=3_000_000, transcendentals=0),
    )(*given)


def body(
    embeddings, row_accum, relations, rel_accum, matching, src_rows, dst_rows, rel_ids, neg_rows
):
    place = jnp.stack([lax.axis_index(name) for name in ("core", "zhi", "x")]).astype(jnp.int32)
    line = lambda v: v.reshape(1, 512)
    block = shape((1024, 256), bf16)
    pieces, pack = call(
        first_kernel,
        (shape((64, 8, 128), bf16), shape((272, 256), bf16)),
        0,
        (embeddings, line(src_rows), line(rel_ids), line(dst_rows), line(neg_rows)),
        moved=800_000,
        far=(0, 1, 2, 3, 4),
        space=62,
        scratch=[
            pltpu.VMEM((256, 256), f32),
            pltpu.VMEM((4, 1, 512), jnp.int32),
            pltpu.SemaphoreType.DMA((5,)),
        ],
    )
    arrived = spread(pieces, DOM)
    near = jnp.concatenate([pack, lax.ppermute(pack, "x", [(i, i ^ 1) for i in range(4)])], axis=0)
    near, arrived = lax.optimization_barrier((near, arrived))
    routed = call(take_kernel, shape((64, 2, 8, 128), bf16), 1, (matching, arrived), moved=400_000)
    rows_in = spread(routed.reshape(128, 8, 128), DOM_Z).reshape(64, 2, 8, 128)
    away = lax.ppermute(near, "x", [(i, i ^ 2) for i in range(4)])
    held = [pltpu.VMEM((1024, 256), bf16)] * 2
    counts0, known0, trans0, source0, rel_b = call(
        trans_kernel,
        (shape((8, 512), f32), shape((8, 512), f32), block, block, shape((8, 256, 256), bf16)),
        1,
        (place, near, relations),
        flops=1_300_000_000,
        moved=6_000_000,
        far_outs=(2, 3, 4),
        scratch=held + [pltpu.VMEM((8, 256, 256), bf16), pltpu.SemaphoreType.DMA((3,))],
        space=62,
    )
    counts1, known1, trans1, source1 = call(
        trans_kernel,
        (shape((8, 512), f32), shape((8, 512), f32), block, block),
        1,
        (place, away, relations),
        flops=1_300_000_000,
        moved=5_000_000,
        far_outs=(2, 3),
        scratch=held + [pltpu.SemaphoreType.DMA((2,))],
        space=62,
    )
    weight, g_trans, kept, given = call(
        score_kernel,
        (shape((2048, 512), bf16), shape((2048, 256), bf16), block, block),
        1,
        (place, rows_in, counts0, counts1, known0, known1, trans0, trans1, source0, source1),
        flops=3_200_000_000,
        moved=6_000_000,
        far=(6, 7, 8, 9),
        scratch=[
            pltpu.VMEM((512, 256), bf16),
            pltpu.VMEM((2048, 256), bf16),
            pltpu.VMEM((2048, 256), bf16),
            pltpu.SemaphoreType.DMA((4,)),
        ],
        space=56,
    )
    came = swap(given, "core")
    mine, theirs, own = call(
        back_kernel,
        (shape((256, 256), f32), shape((256, 256), bf16), shape((4, 256, 256), bf16)),
        1,
        (place, weight, g_trans, known0, known1, trans0, trans1, rel_b),
        flops=3_000_000_000,
        moved=6_000_000,
        far=(5, 6, 7),
        scratch=[
            pltpu.VMEM((2048, 256), bf16),
            pltpu.VMEM((8, 256, 256), bf16),
            pltpu.SemaphoreType.DMA((3,)),
        ],
        space=56,
    )
    rows_came = swap(theirs, "zhi")
    joined = call(join_kernel, shape((4, 512, 256), bf16), 0, (own, kept, came), moved=2_000_000)
    got = spread(joined, "x")
    out, own_here = call(
        pieces_kernel,
        (shape((64, 2, 8, 128), bf16), shape((256, 256), f32)),
        0,
        (got, mine, rows_came),
        moved=2_000_000,
    )
    mid = spread(out.reshape(128, 8, 128), DOM_Z).reshape(64, 2, 8, 128)
    routed_back = call(
        route_kernel, shape((64, 2, 8, 128), bf16), 2, (place, matching, mid), moved=512_000
    )
    last = spread(routed_back.reshape(128, 8, 128), DOM_Z).reshape(64, 2, 8, 128)
    rel_four = spread(
        call(rel_kernel, shape((4, 256, 256), bf16), 0, (last,), moved=512_000), "x"
    )
    new_embeddings, new_row_accum = call(
        rows_kernel,
        (shape((256, 256), f32), shape((1, 256), f32)),
        0,
        (embeddings, row_accum.reshape(1, 256), own_here, last),
        flops=1_000_000,
        moved=1_000_000,
    )
    new_embeddings, rel_four = lax.optimization_barrier((new_embeddings, rel_four))
    rel_rest = swap(rel_four, "core")
    half = update_half(place, relations, rel_accum, rel_four)
    new_relations, new_rel_accum = update_half(place, relations, rel_accum, rel_rest, half)
    return new_embeddings, new_row_accum.reshape(256), new_relations, new_rel_accum


def solution(mesh):
    fine = Mesh(mesh.devices.reshape(4, 8, 2, 2, 4), AXES)
    placed = (
        P(AXES, None),
        P(AXES),
        P(),
        P(),
        P(),
        P(AXES),
        P(AXES),
        P(AXES),
        P(AXES, None),
    )
    return jax.shard_map(
        body,
        mesh=fine,
        in_specs=placed,
        out_specs=(P(AXES, None), P(AXES), P(), P()),
        check_vma=False,
    )
```

```python
import jax
import jax.numpy as jnp
from jax import lax
from jax.experimental import pallas as pl
from jax.experimental.pallas import tpu as pltpu
from jax.sharding import Mesh, PartitionSpec as P

learn_rate = 0.1
AXES = ("zlo", "y", "core", "zhi", "x")
DOM = ("zlo", "y", "core")
DOM_Z = DOM + ("zhi",)
bf16 = jnp.bfloat16
f32 = jnp.float32
VMEM = pl.BlockSpec(memory_space=pltpu.VMEM)
ANY = pl.BlockSpec(memory_space=pltpu.HBM)
SMEM = pl.BlockSpec(memory_space=pltpu.SMEM)
NN = (((1,), (0,)), ((), ()))
NT = (((1,), (1,)), ((), ()))


def shape(dims, dtype):
    return jax.ShapeDtypeStruct(dims, dtype)


def dot(a, b, dims=NN):
    return lax.dot_general(a, b, dims, preferred_element_type=f32)


def call(kernel, outs, scalars, args, flops=0, moved=0, scratch=(), space=8, far=(), far_outs=()):
    specs = [SMEM] * scalars + [ANY if k in far else VMEM for k in range(scalars, len(args))]
    many = isinstance(outs, tuple)
    return pl.pallas_call(
        kernel,
        out_shape=outs,
        in_specs=specs,
        out_specs=tuple(ANY if k in far_outs else VMEM for k in range(len(outs))) if many else VMEM,
        scratch_shapes=list(scratch),
        compiler_params=pltpu.CompilerParams(vmem_limit_bytes=space * 1024 * 1024),
        cost_estimate=pl.CostEstimate(flops=flops, bytes_accessed=moved, transcendentals=0),
    )(*args)


def swap(value, axis):
    return lax.ppermute(value, axis, [(0, 1), (1, 0)])


def spread(value, axis):
    return lax.all_to_all(value, axis, split_axis=0, concat_axis=0, tiled=True)


def first_kernel(emb, src, rel, dst, neg, pieces, pack, rows, index, sems):
    copies = [pltpu.make_async_copy(emb, rows, sems.at[0])]
    for k, part in enumerate((src, rel, dst, neg)):
        copies.append(pltpu.make_async_copy(part, index.at[k], sems.at[k + 1]))
    for copy in copies:
        copy.start()
    for copy in copies:
        copy.wait()
    wide = jnp.concatenate([index[k] for k in range(4)], axis=0)
    high = wide // 256
    low = (wide - high * 256).astype(f32)
    both = jnp.concatenate([high.astype(f32), low], axis=0)
    pack[256:272, :] = jnp.concatenate([both[:, :256], both[:, 256:]], axis=0).astype(bf16)
    pack[0:256, :] = rows[...].astype(bf16)
    for h in range(2):
        half = rows[:, h * 128 : (h + 1) * 128]
        pieces[h * 32 : (h + 1) * 32] = half.reshape(32, 8, 128).astype(bf16)


def take_kernel(matching, arrived, routed):
    for d in range(64):
        piece = arrived[matching[d]]
        routed[d, 0] = piece
        routed[d, 1] = piece


def indices(part):
    part = part.astype(f32)
    both = jnp.concatenate([part[0:8], part[8:16]], axis=1)
    return both[0:4] * 256.0 + both[4:8]


def columns(value):
    return jnp.concatenate([value, value], axis=0).T


def lane_ids(rows, width):
    return lax.broadcasted_iota(jnp.int32, (rows, width), 1)


def row_ids(x, rows):
    ids = lane_ids(rows, 512)
    return (ids + jnp.where(ids >= 256, 768, 0) + x * 256).astype(f32)


def by_relation(kinds, rows):
    parts = [jnp.where(kinds == float(r), rows, 0.0).astype(bf16) for r in range(8)]
    return jnp.concatenate(parts, axis=1)


def trans_kernel(place, packs, rel, counts, known, trans, source, *rel_b):
    stack = jnp.concatenate([rel[r].astype(bf16) for r in range(8)], axis=1)
    for r in range(8) if rel_b else ():
        rel_b[0][r] = rel[r].astype(bf16)
    ids = lane_ids(512, 256).astype(f32)
    wide = row_ids(place[2], 512)
    for s in range(2):
        index = indices(packs[s * 272 + 256 : s * 272 + 272, :])
        known[s * 4 : (s + 1) * 4, :] = index
        column = columns(index)
        hot = (column[:, 0:1] == ids).astype(f32).astype(bf16)
        rows = dot(hot, packs[s * 272 : s * 272 + 256, :])
        source[s * 512 : (s + 1) * 512, :] = rows.astype(bf16)
        trans[s * 512 : (s + 1) * 512, :] = dot(by_relation(column[:, 1:2], rows), stack, NT).astype(bf16)
        hits = (column[:, 3:4] == wide).astype(f32)
        counts[s : s + 1, :] = jnp.sum(hits, axis=0, keepdims=True)
    counts[2:8, :] = jnp.zeros((6, 512), f32)


def score_kernel(
    place, rows_in, counts0, counts1, known0, known1, trans0, trans1, source0, source1,
    weight, g_trans, kept, given, rows
):
    core = place[0]
    for z in range(2):
        both = rows_in[:, z].reshape(2, 256, 128)
        rows[z * 256 : (z + 1) * 256, :] = jnp.concatenate([both[0], both[1]], axis=1)
    index = [known[s * 4 : (s + 1) * 4, :] for known in (known0, known1) for s in range(2)]
    ids = row_ids(place[2], 256)
    for b in range(8):
        s = b // 2
        column = columns(index[s])[(b % 2) * 256 : (b % 2 + 1) * 256]
        trans = (trans0, trans1)[b // 4][(b % 4) * 256 : (b % 4 + 1) * 256, :]
        span = slice(b * 256, (b + 1) * 256)
        score = dot(trans, rows[...], NT)
        sig = 1.0 / (1.0 + jnp.exp(-score))
        count = (counts0, counts1)[s // 2][s % 2 : s % 2 + 1, :]
        hit = column[:, 2:3] == ids
        part = jnp.where(hit, (count + 1.0) * sig - 1.0, count * sig).astype(bf16)
        weight[span, :] = part
        g_trans[span, :] = dot(part, rows[...]).astype(bf16)
    turned = g_trans[...].astype(f32).T
    kinds = jnp.concatenate([part[1:2] for part in index], axis=1)
    source = jnp.concatenate([source0[...], source1[...]], axis=0)
    for r in range(8):
        wanted = r + 4 * core if r < 4 else r - 4 * core
        masked = jnp.where(kinds == wanted.astype(f32), turned, 0.0).astype(bf16)
        grad = dot(masked, source).astype(bf16)
        if r < 4:
            kept[r] = grad
        else:
            given[r - 4] = grad


def partner_kernel(weight, trans0, trans1, g_rows):
    turned = jnp.concatenate([t[...].astype(f32).T.astype(bf16) for t in (trans0, trans1)], axis=1)
    for z in range(2):
        g_rows[z] = dot(turned, weight[:, z * 256 : (z + 1) * 256]).T.astype(bf16)


def own_kernel(g_trans, known0, known1, rel_b, own0, *others):
    sub_ids = lax.broadcasted_iota(jnp.int32, (256, 512), 0).astype(f32)
    stack = rel_b[...].reshape(2048, 256)
    for s in range(4):
        index = (known0, known1)[s // 2][(s % 2) * 4 : (s % 2 + 1) * 4, :]
        grad = g_trans[s * 512 : (s + 1) * 512, :].astype(f32)
        total = dot(by_relation(columns(index)[:, 1:2], grad), stack)
        hot = (index[0:1, :] == sub_ids).astype(f32).astype(bf16)
        mine = dot(hot, total.astype(bf16))
        if s == 0:
            own0[...] = mine
        else:
            others[s - 1][...] = mine.astype(bf16)


def join_kernel(kept, came, out):
    for k in range(4):
        out[k] = (kept[k].astype(f32) + came[k].astype(f32)).astype(bf16)


def pieces_kernel(got, g_rows, out):
    for h in range(2):
        half = slice(h * 128, (h + 1) * 128)
        rel = got[0, :, half].astype(f32)
        for k in range(1, 4):
            rel = rel + got[k, :, half].astype(f32)
        for p, part in enumerate((g_rows[0, :, half].astype(f32), g_rows[1, :, half].astype(f32), rel)):
            tiles = part.reshape(32, 8, 128)
            for z in range(2):
                out[h * 32 : (h + 1) * 32, z, p] = tiles[:, z * 4 : (z + 1) * 4].astype(bf16)


def route_kernel(matching, mid, out):
    rel = [jnp.zeros((4, 128), f32), jnp.zeros((4, 128), f32)]
    for d in range(64):
        rel[d % 2] = rel[d % 2] + (mid[d, 0, 2].astype(f32) + mid[d, 1, 2].astype(f32))
    for d in range(64):
        target = matching[d]
        tail = jnp.where(target % 2 == 0, rel[0], rel[1]).astype(bf16)
        for z in range(2):
            out[target, z, 0] = (mid[d, 0, z].astype(f32) + mid[d, 1, z].astype(f32)).astype(bf16)
            out[target, z, 1] = tail


def whole(last, h, p):
    span = slice(h * 32, (h + 1) * 32)
    parts = [last[span, z, p].astype(f32) for z in range(2)]
    return jnp.concatenate(parts, axis=1).reshape(256, 128)


def rel_kernel(last, out):
    for h in range(2):
        part = whole(last, h, 1).astype(bf16)
        for k in range(4):
            out[k, :, h * 128 : (h + 1) * 128] = part


def to_row(column):
    return jnp.broadcast_to(column, (256, 128)).T[0:1]


def to_column(row):
    return jnp.broadcast_to(row, (128, 256)).T[:, 0:1]


def rows_kernel(emb, accum, own0, own1, own2, own3, last, new_emb, new_accum):
    grad = own0[...] + jnp.concatenate([whole(last, 0, 0), whole(last, 1, 0)], axis=1)
    for own in (own1, own2, own3):
        grad = grad + own[...].astype(f32)
    total = to_column(accum[...]) + jnp.mean(grad * grad, axis=1, keepdims=True)
    new_emb[...] = emb[...] - grad * (learn_rate / jnp.sqrt(total))
    new_accum[...] = to_row(total)


def update_kernel(place, rel, accum, grads, *rest):
    if len(rest) == 6:
        core, (seen, held, new_rel, new_accum, block, sem) = 1 - place[0], rest
    else:
        core, (new_rel, new_accum, block, sem) = place[0], rest
    old = jnp.concatenate([accum[...], accum[...]], axis=0)
    column = jnp.where(core == 0, old[0:8], old[4:12]).T
    totals = []
    for r in range(4):
        grad = grads[r].astype(f32)
        total = column[:, r : r + 1] + jnp.mean(grad * grad, axis=1, keepdims=True)
        block[r] = rel[4 * core + r] - grad * (learn_rate / jnp.sqrt(total))
        totals.append(total)
    copy = pltpu.make_async_copy(block, new_rel.at[pl.ds(4 * core, 4)], sem)
    copy.start()
    rows = jnp.concatenate(totals + totals, axis=1).T
    if len(rest) == 6:
        first = jnp.concatenate([held[...], held[...]], axis=0)
        mixed = jnp.concatenate([rows[0:4], first[0:4]], axis=0)
        turned = jnp.concatenate([first[0:4], rows[0:4]], axis=0)
        new_accum[...] = jnp.where(core == 0, mixed, turned)
    else:
        new_accum[...] = rows
    copy.wait()


def update_half(place, relations, rel_accum, grads, before=None):
    given = (place, relations, rel_accum, grads) + (before or ())
    specs = [SMEM, VMEM, VMEM, VMEM] + ([ANY, VMEM] if before else [])
    return pl.pallas_call(
        update_kernel,
        out_shape=(shape((8, 256, 256), f32), shape((8, 256), f32)),
        in_specs=specs,
        out_specs=(ANY, VMEM),
        scratch_shapes=[pltpu.VMEM((4, 256, 256), f32), pltpu.SemaphoreType.DMA],
        input_output_aliases={4: 0} if before else {},
        compiler_params=pltpu.CompilerParams(vmem_limit_bytes=8 * 1024 * 1024),
        cost_estimate=pl.CostEstimate(flops=0, bytes_accessed=3_000_000, transcendentals=0),
    )(*given)


def body(
    embeddings, row_accum, relations, rel_accum, matching, src_rows, dst_rows, rel_ids, neg_rows
):
    place = jnp.stack([lax.axis_index(name) for name in ("core", "zhi", "x")]).astype(jnp.int32)
    line = lambda v: v.reshape(1, 512)
    block = shape((1024, 256), bf16)
    pieces, pack = call(
        first_kernel,
        (shape((64, 8, 128), bf16), shape((272, 256), bf16)),
        0,
        (embeddings, line(src_rows), line(rel_ids), line(dst_rows), line(neg_rows)),
        moved=800_000,
        far=(0, 1, 2, 3, 4),
        space=62,
        scratch=[
            pltpu.VMEM((256, 256), f32),
            pltpu.VMEM((4, 1, 512), jnp.int32),
            pltpu.SemaphoreType.DMA((5,)),
        ],
    )
    arrived = spread(pieces, DOM)
    near = jnp.concatenate([pack, lax.ppermute(pack, "x", [(i, i ^ 1) for i in range(4)])], axis=0)
    counts0, known0, trans0, source0, rel_b = call(
        trans_kernel,
        (shape((8, 512), f32), shape((8, 512), f32), block, block, shape((8, 256, 256), bf16)),
        1,
        (place, near, relations),
        flops=1_300_000_000,
        moved=6_000_000,
        space=16,
    )
    trans0, arrived = lax.optimization_barrier((trans0, arrived))
    routed = call(take_kernel, shape((64, 2, 8, 128), bf16), 1, (matching, arrived), moved=400_000)
    rows_in = spread(routed.reshape(128, 8, 128), DOM_Z).reshape(64, 2, 8, 128)
    away = lax.ppermute(near, "x", [(i, i ^ 2) for i in range(4)])
    counts1, known1, trans1, source1 = call(
        trans_kernel,
        (shape((8, 512), f32), shape((8, 512), f32), block, block),
        1,
        (place, away, relations),
        flops=1_300_000_000,
        moved=5_000_000,
        space=16,
    )
    four = shape((4, 256, 256), bf16)
    weight, g_trans, kept, given = call(
        score_kernel,
        (shape((2048, 512), bf16), shape((2048, 256), bf16), four, four),
        1,
        (place, rows_in, counts0, counts1, known0, known1, trans0, trans1, source0, source1),
        flops=3_200_000_000,
        moved=6_000_000,
        scratch=[pltpu.VMEM((512, 256), bf16)],
        space=20,
    )
    came = swap(given, "core")
    g_rows = call(
        partner_kernel,
        shape((2, 256, 256), bf16),
        0,
        (weight, trans0, trans1),
        flops=1_500_000_000,
        moved=4_000_000,
        space=16,
    )
    came, g_rows = lax.optimization_barrier((came, g_rows))
    got = spread(call(join_kernel, four, 0, (kept, came), moved=1_500_000), "x")
    one = shape((256, 256), bf16)
    own0, *others = call(
        own_kernel,
        (shape((256, 256), f32), one, one, one),
        0,
        (g_trans, known0, known1, rel_b),
        flops=3_000_000_000,
        moved=4_000_000,
        space=16,
    )
    *others, got = lax.optimization_barrier((*others, got))
    others = [
        lax.ppermute(part, "x", [(i, i ^ k) for i in range(4)]) for k, part in enumerate(others, 1)
    ]
    out = call(
        pieces_kernel, shape((64, 2, 3, 4, 128), bf16), 0, (got, g_rows), moved=2_000_000
    )
    mid = spread(out.reshape(128, 3, 4, 128), DOM_Z)
    *others, mid = lax.optimization_barrier((*others, mid))
    routed_back = call(
        route_kernel,
        shape((64, 2, 2, 4, 128), bf16),
        1,
        (matching, mid.reshape(64, 2, 3, 4, 128)),
        moved=512_000,
    )
    last = spread(routed_back.reshape(128, 2, 4, 128), DOM_Z).reshape(64, 2, 2, 4, 128)
    rel_four = spread(call(rel_kernel, four, 0, (last,), moved=512_000), "x")
    new_embeddings, new_row_accum = call(
        rows_kernel,
        (shape((256, 256), f32), shape((1, 256), f32)),
        0,
        (embeddings, row_accum.reshape(1, 256), own0, *others, last),
        flops=1_000_000,
        moved=1_000_000,
    )
    new_embeddings, rel_four = lax.optimization_barrier((new_embeddings, rel_four))
    rel_rest = swap(rel_four, "core")
    half = update_half(place, relations, rel_accum, rel_four)
    new_relations, new_rel_accum = update_half(place, relations, rel_accum, rel_rest, half)
    return new_embeddings, new_row_accum.reshape(256), new_relations, new_rel_accum


def solution(mesh):
    fine = Mesh(mesh.devices.reshape(4, 8, 2, 2, 4), AXES)
    placed = (
        P(AXES, None),
        P(AXES),
        P(),
        P(),
        P(),
        P(AXES),
        P(AXES),
        P(AXES),
        P(AXES, None),
    )
    return jax.shard_map(
        body,
        mesh=fine,
        in_specs=placed,
        out_specs=(P(AXES, None), P(AXES), P(), P()),
        check_vma=False,
    )
```

```python
import jax
import jax.numpy as jnp
from jax import lax
from jax.experimental import pallas as pl
from jax.experimental.pallas import tpu as pltpu
from jax.sharding import Mesh, PartitionSpec as P

learn_rate = 0.1
AXES = ("zlo", "y", "core", "zhi", "x")
DOM = ("zlo", "y", "core")
DOM_Z = DOM + ("zhi",)
bf16 = jnp.bfloat16
f32 = jnp.float32
VMEM = pl.BlockSpec(memory_space=pltpu.VMEM)
ANY = pl.BlockSpec(memory_space=pltpu.HBM)
SMEM = pl.BlockSpec(memory_space=pltpu.SMEM)
NN = (((1,), (0,)), ((), ()))
NT = (((1,), (1,)), ((), ()))


def shape(dims, dtype):
    return jax.ShapeDtypeStruct(dims, dtype)


def dot(a, b, dims=NN):
    return lax.dot_general(a, b, dims, preferred_element_type=f32)


def call(kernel, outs, scalars, args, flops=0, moved=0, scratch=(), space=8, far=(), far_outs=()):
    specs = [SMEM] * scalars + [ANY if k in far else VMEM for k in range(scalars, len(args))]
    many = isinstance(outs, tuple)
    return pl.pallas_call(
        kernel,
        out_shape=outs,
        in_specs=specs,
        out_specs=tuple(ANY if k in far_outs else VMEM for k in range(len(outs))) if many else VMEM,
        scratch_shapes=list(scratch),
        compiler_params=pltpu.CompilerParams(vmem_limit_bytes=space * 1024 * 1024),
        cost_estimate=pl.CostEstimate(flops=flops, bytes_accessed=moved, transcendentals=0),
    )(*args)


def swap(value, axis):
    return lax.ppermute(value, axis, [(0, 1), (1, 0)])


def spread(value, axis):
    return lax.all_to_all(value, axis, split_axis=0, concat_axis=0, tiled=True)


def first_kernel(emb, src, rel, dst, neg, pieces, pack, rows, index, sems):
    copies = [pltpu.make_async_copy(emb, rows, sems.at[0])]
    for k, part in enumerate((src, rel, dst, neg)):
        copies.append(pltpu.make_async_copy(part, index.at[k], sems.at[k + 1]))
    for copy in copies:
        copy.start()
    for copy in copies:
        copy.wait()
    wide = jnp.concatenate([index[k] for k in range(4)], axis=0)
    high = wide // 256
    low = (wide - high * 256).astype(f32)
    both = jnp.concatenate([high.astype(f32), low], axis=0)
    index_b = jnp.concatenate([both[:, :256], both[:, 256:]], axis=0).astype(bf16)
    for k in range(4):
        pack[k, 256:272, :] = index_b
        pack[k, 0:256, :] = rows[...].astype(bf16)
    for h in range(2):
        half = rows[:, h * 128 : (h + 1) * 128]
        pieces[h * 32 : (h + 1) * 32] = half.reshape(32, 8, 128).astype(bf16)


def take_kernel(matching, arrived, routed):
    for d in range(64):
        piece = arrived[matching[d]]
        routed[d, 0] = piece
        routed[d, 1] = piece


def indices(part):
    part = part.astype(f32)
    both = jnp.concatenate([part[0:8], part[8:16]], axis=1)
    return both[0:4] * 256.0 + both[4:8]


def columns(value):
    return jnp.concatenate([value, value], axis=0).T


def lane_ids(rows, width):
    return lax.broadcasted_iota(jnp.int32, (rows, width), 1)


def row_ids(x, rows):
    ids = lane_ids(rows, 512)
    return (ids + jnp.where(ids >= 256, 768, 0) + x * 256).astype(f32)


def by_relation(kinds, rows):
    parts = [jnp.where(kinds == float(r), rows, 0.0).astype(bf16) for r in range(8)]
    return jnp.concatenate(parts, axis=1)


def trans_kernel(place, packs, rel, counts, known, trans, source, rel_b):
    stack = jnp.concatenate([rel[r].astype(bf16) for r in range(8)], axis=1)
    for r in range(8):
        rel_b[r] = rel[r].astype(bf16)
    ids = lane_ids(512, 256).astype(f32)
    wide = row_ids(place[2], 512)
    for s in range(4):
        index = indices(packs[s, 256:272, :])
        known[s * 8 : (s + 1) * 8, :] = jnp.concatenate([index, index], axis=0)
        column = columns(index)
        hot = (column[:, 0:1] == ids).astype(f32).astype(bf16)
        rows = dot(hot, packs[s, 0:256, :])
        source[s * 512 : (s + 1) * 512, :] = rows.astype(bf16)
        trans[s * 512 : (s + 1) * 512, :] = dot(by_relation(column[:, 1:2], rows), stack, NT).astype(bf16)
        hits = (column[:, 3:4] == wide).astype(f32)
        counts[s : s + 1, :] = jnp.sum(hits, axis=0, keepdims=True)
    counts[4:8, :] = jnp.zeros((4, 512), f32)


def score_kernel(
    place, rows_in, counts, known, trans, source, weight, g_trans, kept, given, rows
):
    core = place[0]
    for z in range(2):
        both = rows_in[:, z].reshape(2, 256, 128)
        rows[z * 256 : (z + 1) * 256, :] = jnp.concatenate([both[0], both[1]], axis=1)
    index = [known[s * 8 : s * 8 + 4, :] for s in range(4)]
    ids = row_ids(place[2], 256)
    for b in range(8):
        s = b // 2
        column = columns(index[s])[(b % 2) * 256 : (b % 2 + 1) * 256]
        span = slice(b * 256, (b + 1) * 256)
        score = dot(trans[span, :], rows[...], NT)
        sig = 1.0 / (1.0 + jnp.exp(-score))
        count = counts[s : s + 1, :]
        hit = column[:, 2:3] == ids
        part = jnp.where(hit, (count + 1.0) * sig - 1.0, count * sig).astype(bf16)
        weight[span, :] = part
        g_trans[span, :] = dot(part, rows[...]).astype(bf16)
    turned = g_trans[...].astype(f32).T
    kinds = jnp.concatenate([part[1:2] for part in index], axis=1)
    for r in range(8):
        wanted = r + 4 * core if r < 4 else r - 4 * core
        masked = jnp.where(kinds == wanted.astype(f32), turned, 0.0).astype(bf16)
        grad = dot(masked, source[...]).astype(bf16)
        if r < 4:
            kept[r] = grad
        else:
            given[r - 4] = grad


def partner_kernel(weight, trans, g_rows):
    turned = trans[...].astype(f32).T.astype(bf16)
    for z in range(2):
        g_rows[z] = dot(turned, weight[:, z * 256 : (z + 1) * 256]).T.astype(bf16)


def own_kernel(place, g_trans, known, rel_b, own0, *others):
    sub_ids = lax.broadcasted_iota(jnp.int32, (256, 512), 0).astype(f32)
    stack = rel_b[...].reshape(2048, 256)
    for s in range(4):
        span = place[2] ^ s
        index = known[pl.ds(pl.multiple_of(span * 8, 8), 8), :]
        grad = g_trans[pl.ds(pl.multiple_of(span * 512, 512), 512), :].astype(f32)
        total = dot(by_relation(columns(index[0:4])[:, 1:2], grad), stack)
        hot = (index[0:1, :] == sub_ids).astype(f32).astype(bf16)
        mine = dot(hot, total.astype(bf16))
        if s == 0:
            own0[...] = mine
        else:
            others[s - 1][...] = mine.astype(bf16)


def join_kernel(kept, came, out):
    for k in range(4):
        out[k] = (kept[k].astype(f32) + came[k].astype(f32)).astype(bf16)


def pieces_kernel(got, g_rows, out):
    for h in range(2):
        half = slice(h * 128, (h + 1) * 128)
        rel = got[0, :, half].astype(f32)
        for k in range(1, 4):
            rel = rel + got[k, :, half].astype(f32)
        for p, part in enumerate((g_rows[0, :, half].astype(f32), g_rows[1, :, half].astype(f32), rel)):
            tiles = part.reshape(32, 8, 128)
            for z in range(2):
                out[h * 32 : (h + 1) * 32, z, p] = tiles[:, z * 4 : (z + 1) * 4].astype(bf16)


def route_kernel(matching, mid, out):
    rel = [jnp.zeros((4, 128), f32), jnp.zeros((4, 128), f32)]
    for d in range(64):
        rel[d % 2] = rel[d % 2] + (mid[d, 0, 2].astype(f32) + mid[d, 1, 2].astype(f32))
    for d in range(64):
        target = matching[d]
        tail = jnp.where(target % 2 == 0, rel[0], rel[1]).astype(bf16)
        for z in range(2):
            out[target, z, 0] = (mid[d, 0, z].astype(f32) + mid[d, 1, z].astype(f32)).astype(bf16)
            out[target, z, 1] = tail


def whole(last, h, p):
    span = slice(h * 32, (h + 1) * 32)
    parts = [last[span, z, p].astype(f32) for z in range(2)]
    return jnp.concatenate(parts, axis=1).reshape(256, 128)


def rel_kernel(last, out):
    for h in range(2):
        part = whole(last, h, 1).astype(bf16)
        for k in range(4):
            out[k, :, h * 128 : (h + 1) * 128] = part


def to_row(column):
    return jnp.broadcast_to(column, (256, 128)).T[0:1]


def to_column(row):
    return jnp.broadcast_to(row, (128, 256)).T[:, 0:1]


def rows_kernel(emb, accum, own0, own1, own2, own3, last, new_emb, new_accum):
    grad = own0[...] + jnp.concatenate([whole(last, 0, 0), whole(last, 1, 0)], axis=1)
    for own in (own1, own2, own3):
        grad = grad + own[...].astype(f32)
    total = to_column(accum[...]) + jnp.mean(grad * grad, axis=1, keepdims=True)
    new_emb[...] = emb[...] - grad * (learn_rate / jnp.sqrt(total))
    new_accum[...] = to_row(total)


def update_kernel(place, rel, accum, grads, *rest):
    if len(rest) == 6:
        core, (seen, held, new_rel, new_accum, block, sem) = 1 - place[0], rest
    else:
        core, (new_rel, new_accum, block, sem) = place[0], rest
    old = jnp.concatenate([accum[...], accum[...]], axis=0)
    column = jnp.where(core == 0, old[0:8], old[4:12]).T
    totals = []
    for r in range(4):
        grad = grads[r].astype(f32)
        total = column[:, r : r + 1] + jnp.mean(grad * grad, axis=1, keepdims=True)
        block[r] = rel[4 * core + r] - grad * (learn_rate / jnp.sqrt(total))
        totals.append(total)
    copy = pltpu.make_async_copy(block, new_rel.at[pl.ds(4 * core, 4)], sem)
    copy.start()
    rows = jnp.concatenate(totals + totals, axis=1).T
    if len(rest) == 6:
        first = jnp.concatenate([held[...], held[...]], axis=0)
        mixed = jnp.concatenate([rows[0:4], first[0:4]], axis=0)
        turned = jnp.concatenate([first[0:4], rows[0:4]], axis=0)
        new_accum[...] = jnp.where(core == 0, mixed, turned)
    else:
        new_accum[...] = rows
    copy.wait()


def update_half(place, relations, rel_accum, grads, before=None):
    given = (place, relations, rel_accum, grads) + (before or ())
    specs = [SMEM, VMEM, VMEM, VMEM] + ([ANY, VMEM] if before else [])
    return pl.pallas_call(
        update_kernel,
        out_shape=(shape((8, 256, 256), f32), shape((8, 256), f32)),
        in_specs=specs,
        out_specs=(ANY, VMEM),
        scratch_shapes=[pltpu.VMEM((4, 256, 256), f32), pltpu.SemaphoreType.DMA],
        input_output_aliases={4: 0} if before else {},
        compiler_params=pltpu.CompilerParams(vmem_limit_bytes=8 * 1024 * 1024),
        cost_estimate=pl.CostEstimate(flops=0, bytes_accessed=3_000_000, transcendentals=0),
    )(*given)


def body(
    embeddings, row_accum, relations, rel_accum, matching, src_rows, dst_rows, rel_ids, neg_rows
):
    place = jnp.stack([lax.axis_index(name) for name in ("core", "zhi", "x")]).astype(jnp.int32)
    line = lambda v: v.reshape(1, 512)
    pieces, pack = call(
        first_kernel,
        (shape((64, 8, 128), bf16), shape((4, 272, 256), bf16)),
        0,
        (embeddings, line(src_rows), line(rel_ids), line(dst_rows), line(neg_rows)),
        moved=800_000,
        far=(0, 1, 2, 3, 4),
        space=62,
        scratch=[
            pltpu.VMEM((256, 256), f32),
            pltpu.VMEM((4, 1, 512), jnp.int32),
            pltpu.SemaphoreType.DMA((5,)),
        ],
    )
    arrived = spread(pieces, DOM)
    packs = spread(pack, "x")
    routed = call(take_kernel, shape((64, 2, 8, 128), bf16), 1, (matching, arrived), moved=400_000)
    routed, packs = lax.optimization_barrier((routed, packs))
    rows_in = spread(routed.reshape(128, 8, 128), DOM_Z).reshape(64, 2, 8, 128)
    counts, known, trans, source, rel_b = call(
        trans_kernel,
        (
            shape((8, 512), f32),
            shape((32, 512), f32),
            shape((2048, 256), bf16),
            shape((2048, 256), bf16),
            shape((8, 256, 256), bf16),
        ),
        1,
        (place, packs, relations),
        flops=2_600_000_000,
        moved=6_000_000,
        space=16,
    )
    four = shape((4, 256, 256), bf16)
    weight, g_trans, kept, given = call(
        score_kernel,
        (shape((2048, 512), bf16), shape((2048, 256), bf16), four, four),
        1,
        (place, rows_in, counts, known, trans, source),
        flops=3_200_000_000,
        moved=6_000_000,
        scratch=[pltpu.VMEM((512, 256), bf16)],
        space=20,
    )
    came = swap(given, "core")
    g_rows = call(
        partner_kernel,
        shape((2, 256, 256), bf16),
        0,
        (weight, trans),
        flops=1_500_000_000,
        moved=4_000_000,
        space=16,
    )
    came, g_rows = lax.optimization_barrier((came, g_rows))
    got = spread(call(join_kernel, four, 0, (kept, came), moved=1_500_000), "x")
    one = shape((256, 256), bf16)
    own0, *others = call(
        own_kernel,
        (shape((256, 256), f32), one, one, one),
        1,
        (place, g_trans, known, rel_b),
        flops=3_000_000_000,
        moved=4_000_000,
        space=16,
    )
    *others, got = lax.optimization_barrier((*others, got))
    away = lambda part, k: lax.ppermute(part, "x", [(i, i ^ k) for i in range(4)])
    others[0], others[1] = away(others[0], 1), away(others[1], 2)
    out = call(
        pieces_kernel, shape((64, 2, 3, 4, 128), bf16), 0, (got, g_rows), moved=2_000_000
    )
    mid = spread(out.reshape(128, 3, 4, 128), DOM_Z)
    *others, mid = lax.optimization_barrier((*others, mid))
    routed_back = call(
        route_kernel,
        shape((64, 2, 2, 4, 128), bf16),
        1,
        (matching, mid.reshape(64, 2, 3, 4, 128)),
        moved=512_000,
    )
    others[2] = away(others[2], 3)
    last = spread(routed_back.reshape(128, 2, 4, 128), DOM_Z).reshape(64, 2, 2, 4, 128)
    others[2], last = lax.optimization_barrier((others[2], last))
    rel_four = spread(call(rel_kernel, four, 0, (last,), moved=512_000), "x")
    new_embeddings, new_row_accum = call(
        rows_kernel,
        (shape((256, 256), f32), shape((1, 256), f32)),
        0,
        (embeddings, row_accum.reshape(1, 256), own0, *others, last),
        flops=1_000_000,
        moved=1_000_000,
    )
    new_embeddings, rel_four = lax.optimization_barrier((new_embeddings, rel_four))
    rel_rest = swap(rel_four, "core")
    half = update_half(place, relations, rel_accum, rel_four)
    new_relations, new_rel_accum = update_half(place, relations, rel_accum, rel_rest, half)
    return new_embeddings, new_row_accum.reshape(256), new_relations, new_rel_accum


def solution(mesh):
    fine = Mesh(mesh.devices.reshape(4, 8, 2, 2, 4), AXES)
    placed = (
        P(AXES, None),
        P(AXES),
        P(),
        P(),
        P(),
        P(AXES),
        P(AXES),
        P(AXES),
        P(AXES, None),
    )
    return jax.shard_map(
        body,
        mesh=fine,
        in_specs=placed,
        out_specs=(P(AXES, None), P(AXES), P(), P()),
        check_vma=False,
    )
```

```python
import jax
import jax.numpy as jnp
from jax import lax
from jax.experimental import pallas as pl
from jax.experimental.pallas import tpu as pltpu
from jax.sharding import Mesh, PartitionSpec as P

learn_rate = 0.1
AXES = ("zlo", "y", "core", "zhi", "x")
DOM = ("zlo", "y", "core")
DOM_Z = DOM + ("zhi",)
bf16 = jnp.bfloat16
f32 = jnp.float32
VMEM = pl.BlockSpec(memory_space=pltpu.VMEM)
ANY = pl.BlockSpec(memory_space=pltpu.HBM)
SMEM = pl.BlockSpec(memory_space=pltpu.SMEM)
NN = (((1,), (0,)), ((), ()))
NT = (((1,), (1,)), ((), ()))


def shape(dims, dtype):
    return jax.ShapeDtypeStruct(dims, dtype)


def dot(a, b, dims=NN):
    return lax.dot_general(a, b, dims, preferred_element_type=f32)


def call(kernel, outs, scalars, args, flops=0, moved=0, scratch=(), space=8, far=(), far_outs=()):
    specs = [SMEM] * scalars + [ANY if k in far else VMEM for k in range(scalars, len(args))]
    many = isinstance(outs, tuple)
    return pl.pallas_call(
        kernel,
        out_shape=outs,
        in_specs=specs,
        out_specs=tuple(ANY if k in far_outs else VMEM for k in range(len(outs))) if many else VMEM,
        scratch_shapes=list(scratch),
        compiler_params=pltpu.CompilerParams(vmem_limit_bytes=space * 1024 * 1024),
        cost_estimate=pl.CostEstimate(flops=flops, bytes_accessed=moved, transcendentals=0),
    )(*args)


def swap(value, axis):
    return lax.ppermute(value, axis, [(0, 1), (1, 0)])


def spread(value, axis):
    return lax.all_to_all(value, axis, split_axis=0, concat_axis=0, tiled=True)


def first_kernel(emb, src, rel, dst, neg, pieces, pack, rows, index, sems):
    copies = [pltpu.make_async_copy(emb, rows, sems.at[0])]
    for k, part in enumerate((src, rel, dst, neg)):
        copies.append(pltpu.make_async_copy(part, index.at[k], sems.at[k + 1]))
    for copy in copies:
        copy.start()
    for copy in copies:
        copy.wait()
    wide = jnp.concatenate([index[k] for k in range(4)], axis=0)
    high = wide // 256
    low = (wide - high * 256).astype(f32)
    both = jnp.concatenate([high.astype(f32), low], axis=0)
    index_b = jnp.concatenate([both[:, :256], both[:, 256:]], axis=0).astype(bf16)
    for k in range(4):
        pack[k, 256:272, :] = index_b
        pack[k, 0:256, :] = rows[...].astype(bf16)
    for h in range(2):
        half = rows[:, h * 128 : (h + 1) * 128]
        pieces[h * 32 : (h + 1) * 32] = half.reshape(32, 8, 128).astype(bf16)


def take_kernel(matching, arrived, routed):
    for d in range(64):
        piece = arrived[matching[d]]
        routed[d, 0] = piece
        routed[d, 1] = piece


def indices(part):
    part = part.astype(f32)
    both = jnp.concatenate([part[0:8], part[8:16]], axis=1)
    return both[0:4] * 256.0 + both[4:8]


def columns(value):
    return jnp.concatenate([value, value], axis=0).T


def lane_ids(rows, width):
    return lax.broadcasted_iota(jnp.int32, (rows, width), 1)


def row_ids(x, rows):
    ids = lane_ids(rows, 512)
    return (ids + jnp.where(ids >= 256, 768, 0) + x * 256).astype(f32)


def by_relation(kinds, rows):
    wide = jnp.broadcast_to(kinds, rows.shape).astype(bf16)
    parts = [jnp.where(wide == bf16(r), rows, bf16(0)) for r in range(8)]
    return jnp.concatenate(parts, axis=1)


def cast_kernel(rel, rel_b):
    rel_b[...] = rel[...].astype(bf16)


def trans_kernel(place, packs, rel_b, counts, known, trans, source):
    stack = jnp.concatenate([rel_b[r] for r in range(8)], axis=1)
    ids = lane_ids(512, 256).astype(f32)
    wide = row_ids(place[2], 512)
    for s in range(4):
        index = indices(packs[s, 256:272, :])
        known[s * 8 : (s + 1) * 8, :] = jnp.concatenate([index, index], axis=0)
        column = columns(index)
        hot = (column[:, 0:1] == ids).astype(f32).astype(bf16)
        rows = dot(hot, packs[s, 0:256, :]).astype(bf16)
        source[s * 512 : (s + 1) * 512, :] = rows
        for h in range(0, 512, 128):
            part = by_relation(column[h : h + 128, 1:2], rows[h : h + 128])
            trans[s * 512 + h : s * 512 + h + 128, :] = dot(part, stack, NT).astype(bf16)
        hits = (column[:, 3:4] == wide).astype(f32)
        counts[s : s + 1, :] = jnp.sum(hits, axis=0, keepdims=True)
    counts[4:8, :] = jnp.zeros((4, 512), f32)


def score_kernel(
    place, rows_in, counts, known, trans, source, weight, g_trans, kept, given, rows
):
    core = place[0]
    for z in range(2):
        both = rows_in[:, z].reshape(2, 256, 128)
        rows[z * 256 : (z + 1) * 256, :] = jnp.concatenate([both[0], both[1]], axis=1)
    index = [known[s * 8 : s * 8 + 4, :] for s in range(4)]
    ids = row_ids(place[2], 256)
    for b in range(8):
        s = b // 2
        column = columns(index[s])[(b % 2) * 256 : (b % 2 + 1) * 256]
        span = slice(b * 256, (b + 1) * 256)
        score = dot(trans[span, :], rows[...], NT)
        sig = 1.0 / (1.0 + jnp.exp(-score))
        count = counts[s : s + 1, :]
        hit = column[:, 2:3] == ids
        part = jnp.where(hit, (count + 1.0) * sig - 1.0, count * sig).astype(bf16)
        weight[span, :] = part
        g_trans[span, :] = dot(part, rows[...]).astype(bf16)
    turned = g_trans[...].astype(f32).T
    kinds = jnp.concatenate([part[1:2] for part in index], axis=1)
    for r in range(8):
        wanted = r + 4 * core if r < 4 else r - 4 * core
        masked = jnp.where(kinds == wanted.astype(f32), turned, 0.0).astype(bf16)
        grad = dot(masked, source[...]).astype(bf16)
        if r < 4:
            kept[r] = grad
        else:
            given[r - 4] = grad


def partner_kernel(weight, trans, g_rows):
    turned = trans[...].astype(f32).T.astype(bf16)
    for z in range(2):
        g_rows[z] = dot(turned, weight[:, z * 256 : (z + 1) * 256]).T.astype(bf16)


def own_kernel(place, g_trans, known, rel_b, own0, own1, far):
    sub_ids = lax.broadcasted_iota(jnp.int32, (256, 512), 0).astype(f32)
    stack = rel_b[...].reshape(2048, 256)
    for s in range(4):
        span = place[2] ^ s
        index = known[pl.ds(pl.multiple_of(span * 8, 8), 8), :]
        grad = g_trans[pl.ds(pl.multiple_of(span * 512, 512), 512), :]
        kinds = columns(index[0:4])[:, 1:2]
        parts = [
            dot(by_relation(kinds[h : h + 128], grad[h : h + 128]), stack).astype(bf16)
            for h in range(0, 512, 128)
        ]
        hot = (index[0:1, :] == sub_ids).astype(f32).astype(bf16)
        mine = dot(hot, jnp.concatenate(parts, axis=0))
        if s < 2:
            (own0, own1)[s][...] = mine
        else:
            far[s - 2] = mine.astype(bf16)


def pass_kernel(own1, came, out):
    out[...] = (own1[...] + came[1].astype(f32)).astype(bf16)


def join_kernel(kept, came, out):
    for k in range(4):
        out[k] = (kept[k].astype(f32) + came[k].astype(f32)).astype(bf16)


def pieces_kernel(got, g_rows, out):
    for h in range(2):
        half = slice(h * 128, (h + 1) * 128)
        rel = got[0, :, half].astype(f32)
        for k in range(1, 4):
            rel = rel + got[k, :, half].astype(f32)
        for p, part in enumerate((g_rows[0, :, half].astype(f32), g_rows[1, :, half].astype(f32), rel)):
            tiles = part.reshape(32, 8, 128)
            for z in range(2):
                out[h * 32 : (h + 1) * 32, z, p] = tiles[:, z * 4 : (z + 1) * 4].astype(bf16)


def route_kernel(matching, mid, out):
    rel = [jnp.zeros((4, 128), f32), jnp.zeros((4, 128), f32)]
    for d in range(64):
        rel[d % 2] = rel[d % 2] + (mid[d, 0, 2].astype(f32) + mid[d, 1, 2].astype(f32))
    for d in range(64):
        target = matching[d]
        tail = jnp.where(target % 2 == 0, rel[0], rel[1]).astype(bf16)
        for z in range(2):
            out[target, z, 0] = (mid[d, 0, z].astype(f32) + mid[d, 1, z].astype(f32)).astype(bf16)
            out[target, z, 1] = tail


def whole(last, h, p):
    span = slice(h * 32, (h + 1) * 32)
    parts = [last[span, z, p].astype(f32) for z in range(2)]
    return jnp.concatenate(parts, axis=1).reshape(256, 128)


def rel_kernel(last, out):
    for h in range(2):
        part = whole(last, h, 1).astype(bf16)
        for k in range(4):
            out[k, :, h * 128 : (h + 1) * 128] = part


def to_row(column):
    return jnp.broadcast_to(column, (256, 128)).T[0:1]


def to_column(row):
    return jnp.broadcast_to(row, (128, 256)).T[:, 0:1]


def rows_kernel(emb, accum, own0, far, near, last, new_emb, new_accum):
    grad = own0[...] + far[0].astype(f32) + near[...].astype(f32)
    grad = grad + jnp.concatenate([whole(last, 0, 0), whole(last, 1, 0)], axis=1)
    total = to_column(accum[...]) + jnp.mean(grad * grad, axis=1, keepdims=True)
    new_emb[...] = emb[...] - grad * (learn_rate / jnp.sqrt(total))
    new_accum[...] = to_row(total)


def update_kernel(place, rel, accum, grads, *rest):
    if len(rest) == 6:
        core, (seen, held, new_rel, new_accum, block, sem) = 1 - place[0], rest
    else:
        core, (new_rel, new_accum, block, sem) = place[0], rest
    old = jnp.concatenate([accum[...], accum[...]], axis=0)
    column = jnp.where(core == 0, old[0:8], old[4:12]).T
    totals, copies = [], []
    for r in range(4):
        grad = grads[r].astype(f32)
        total = column[:, r : r + 1] + jnp.mean(grad * grad, axis=1, keepdims=True)
        block[r] = rel[4 * core + r] - grad * (learn_rate / jnp.sqrt(total))
        totals.append(total)
        copies.append(pltpu.make_async_copy(block.at[r], new_rel.at[4 * core + r], sem.at[r]))
        copies[r].start()
    rows = jnp.concatenate(totals + totals, axis=1).T
    if len(rest) == 6:
        first = jnp.concatenate([held[...], held[...]], axis=0)
        mixed = jnp.concatenate([rows[0:4], first[0:4]], axis=0)
        turned = jnp.concatenate([first[0:4], rows[0:4]], axis=0)
        new_accum[...] = jnp.where(core == 0, mixed, turned)
    else:
        new_accum[...] = rows
    for copy in copies:
        copy.wait()


def update_half(place, relations, rel_accum, grads, before=None):
    given = (place, relations, rel_accum, grads) + (before or ())
    specs = [SMEM, VMEM, VMEM, VMEM] + ([ANY, VMEM] if before else [])
    return pl.pallas_call(
        update_kernel,
        out_shape=(shape((8, 256, 256), f32), shape((8, 256), f32)),
        in_specs=specs,
        out_specs=(ANY, VMEM),
        scratch_shapes=[pltpu.VMEM((4, 256, 256), f32), pltpu.SemaphoreType.DMA((4,))],
        input_output_aliases={4: 0} if before else {},
        compiler_params=pltpu.CompilerParams(vmem_limit_bytes=8 * 1024 * 1024),
        cost_estimate=pl.CostEstimate(flops=0, bytes_accessed=3_000_000, transcendentals=0),
    )(*given)


def body(
    embeddings, row_accum, relations, rel_accum, matching, src_rows, dst_rows, rel_ids, neg_rows
):
    place = jnp.stack([lax.axis_index(name) for name in ("core", "zhi", "x")]).astype(jnp.int32)
    line = lambda v: v.reshape(1, 512)
    pieces, pack = call(
        first_kernel,
        (shape((64, 8, 128), bf16), shape((4, 272, 256), bf16)),
        0,
        (embeddings, line(src_rows), line(rel_ids), line(dst_rows), line(neg_rows)),
        moved=800_000,
        far=(0, 1, 2, 3, 4),
        space=62,
        scratch=[
            pltpu.VMEM((256, 256), f32),
            pltpu.VMEM((4, 1, 512), jnp.int32),
            pltpu.SemaphoreType.DMA((5,)),
        ],
    )
    arrived = spread(pieces, DOM)
    rel_b = call(
        cast_kernel, shape((8, 256, 256), bf16), 0, (relations,), moved=3_000_000, space=62
    )
    rel_b, arrived = lax.optimization_barrier((rel_b, arrived))
    packs = spread(pack, "x")
    routed = call(take_kernel, shape((64, 2, 8, 128), bf16), 1, (matching, arrived), moved=400_000)
    routed, packs = lax.optimization_barrier((routed, packs))
    rows_in = spread(routed.reshape(128, 8, 128), DOM_Z).reshape(64, 2, 8, 128)
    counts, known, trans, source = call(
        trans_kernel,
        (
            shape((8, 512), f32),
            shape((32, 512), f32),
            shape((2048, 256), bf16),
            shape((2048, 256), bf16),
        ),
        1,
        (place, packs, rel_b),
        flops=2_600_000_000,
        moved=6_000_000,
        space=16,
    )
    four = shape((4, 256, 256), bf16)
    weight, g_trans, kept, given = call(
        score_kernel,
        (shape((2048, 512), bf16), shape((2048, 256), bf16), four, four),
        1,
        (place, rows_in, counts, known, trans, source),
        flops=3_200_000_000,
        moved=6_000_000,
        scratch=[pltpu.VMEM((512, 256), bf16)],
        space=20,
    )
    came = swap(given, "core")
    g_rows = call(
        partner_kernel,
        shape((2, 256, 256), bf16),
        0,
        (weight, trans),
        flops=1_500_000_000,
        moved=4_000_000,
        space=16,
    )
    came, g_rows = lax.optimization_barrier((came, g_rows))
    got = spread(call(join_kernel, four, 0, (kept, came), moved=1_500_000), "x")
    own0, own1, far = call(
        own_kernel,
        (shape((256, 256), f32), shape((256, 256), f32), shape((2, 256, 256), bf16)),
        1,
        (place, g_trans, known, rel_b),
        flops=3_000_000_000,
        moved=4_000_000,
        space=16,
    )
    far, got = lax.optimization_barrier((far, got))
    far = lax.ppermute(far, "x", [(i, i ^ 2) for i in range(4)])
    out = call(
        pieces_kernel, shape((64, 2, 3, 4, 128), bf16), 0, (got, g_rows), moved=2_000_000
    )
    mid = spread(out.reshape(128, 3, 4, 128), DOM_Z)
    far, mid = lax.optimization_barrier((far, mid))
    routed_back = call(
        route_kernel,
        shape((64, 2, 2, 4, 128), bf16),
        1,
        (matching, mid.reshape(64, 2, 3, 4, 128)),
        moved=512_000,
    )
    near = call(pass_kernel, shape((256, 256), bf16), 0, (own1, far), moved=500_000)
    near = lax.ppermute(near, "x", [(i, i ^ 1) for i in range(4)])
    last = spread(routed_back.reshape(128, 2, 4, 128), DOM_Z).reshape(64, 2, 2, 4, 128)
    near, last = lax.optimization_barrier((near, last))
    rel_four = spread(call(rel_kernel, four, 0, (last,), moved=512_000), "x")
    new_embeddings, new_row_accum = call(
        rows_kernel,
        (shape((256, 256), f32), shape((1, 256), f32)),
        0,
        (embeddings, row_accum.reshape(1, 256), own0, far, near, last),
        flops=1_000_000,
        moved=1_000_000,
    )
    new_embeddings, rel_four = lax.optimization_barrier((new_embeddings, rel_four))
    rel_rest = swap(rel_four, "core")
    half = update_half(place, relations, rel_accum, rel_four)
    new_relations, new_rel_accum = update_half(place, relations, rel_accum, rel_rest, half)
    return new_embeddings, new_row_accum.reshape(256), new_relations, new_rel_accum


def solution(mesh):
    fine = Mesh(mesh.devices.reshape(4, 8, 2, 2, 4), AXES)
    placed = (
        P(AXES, None),
        P(AXES),
        P(),
        P(),
        P(),
        P(AXES),
        P(AXES),
        P(AXES),
        P(AXES, None),
    )
    return jax.shard_map(
        body,
        mesh=fine,
        in_specs=placed,
        out_specs=(P(AXES, None), P(AXES), P(), P()),
        check_vma=False,
    )
```

```python
import jax
import jax.numpy as jnp
from jax import lax
from jax.experimental import pallas as pl
from jax.experimental.pallas import tpu as pltpu
from jax.sharding import Mesh, PartitionSpec as P

learn_rate = 0.1
AXES = ("zlo", "y", "core", "zhi", "x")
DOM = ("zlo", "y", "core")
DOM_Z = DOM + ("zhi",)
bf16 = jnp.bfloat16
f32 = jnp.float32
VMEM = pl.BlockSpec(memory_space=pltpu.VMEM)
ANY = pl.BlockSpec(memory_space=pltpu.HBM)
SMEM = pl.BlockSpec(memory_space=pltpu.SMEM)
NN = (((1,), (0,)), ((), ()))
NT = (((1,), (1,)), ((), ()))


def shape(dims, dtype):
    return jax.ShapeDtypeStruct(dims, dtype)


def dot(a, b, dims=NN):
    return lax.dot_general(a, b, dims, preferred_element_type=f32)


def call(kernel, outs, scalars, args, flops=0, moved=0, scratch=(), space=8, far=(), far_outs=()):
    specs = [SMEM] * scalars + [ANY if k in far else VMEM for k in range(scalars, len(args))]
    many = isinstance(outs, tuple)
    return pl.pallas_call(
        kernel,
        out_shape=outs,
        in_specs=specs,
        out_specs=tuple(ANY if k in far_outs else VMEM for k in range(len(outs))) if many else (ANY if far_outs else VMEM),
        scratch_shapes=list(scratch),
        compiler_params=pltpu.CompilerParams(vmem_limit_bytes=space * 1024 * 1024),
        cost_estimate=pl.CostEstimate(flops=flops, bytes_accessed=moved, transcendentals=0),
    )(*args)


def swap(value, axis):
    return lax.ppermute(value, axis, [(0, 1), (1, 0)])


def spread(value, axis):
    return lax.all_to_all(value, axis, split_axis=0, concat_axis=0, tiled=True)


def first_kernel(emb, src, rel, dst, neg, pieces, pack, rows, index, sems):
    copies = [pltpu.make_async_copy(emb, rows, sems.at[0])]
    for k, part in enumerate((src, rel, dst, neg)):
        copies.append(pltpu.make_async_copy(part, index.at[k], sems.at[k + 1]))
    for copy in copies:
        copy.start()
    for copy in copies:
        copy.wait()
    wide = jnp.concatenate([index[k] for k in range(4)], axis=0)
    high = wide // 256
    low = (wide - high * 256).astype(f32)
    both = jnp.concatenate([high.astype(f32), low], axis=0)
    pack[256:272, :] = jnp.concatenate([both[:, :256], both[:, 256:]], axis=0).astype(bf16)
    pack[0:256, :] = rows[...].astype(bf16)
    for h in range(2):
        half = rows[:, h * 128 : (h + 1) * 128]
        pieces[h * 32 : (h + 1) * 32] = half.reshape(32, 8, 128).astype(bf16)


def take_kernel(matching, arrived, routed):
    for d in range(64):
        piece = arrived[matching[d]]
        routed[d, 0] = piece
        routed[d, 1] = piece


def indices(part):
    part = part.astype(f32)
    both = jnp.concatenate([part[0:8], part[8:16]], axis=1)
    return both[0:4] * 256.0 + both[4:8]


def columns(value):
    return jnp.concatenate([value, value], axis=0).T


def lane_ids(rows, width):
    return lax.broadcasted_iota(jnp.int32, (rows, width), 1)


def row_ids(x, rows):
    ids = lane_ids(rows, 512)
    return (ids + jnp.where(ids >= 256, 768, 0) + x * 256).astype(f32)


def by_relation(kinds, rows):
    wide = jnp.broadcast_to(kinds, rows.shape).astype(bf16)
    parts = [jnp.where(wide == bf16(r), rows, bf16(0)) for r in range(8)]
    return jnp.concatenate(parts, axis=1)


def cast_kernel(rel, rel_b, wide, narrow, sems):
    taken = [pltpu.make_async_copy(rel.at[r], wide.at[r], sems.at[r]) for r in range(8)]
    given = [pltpu.make_async_copy(narrow.at[r], rel_b.at[r], sems.at[8 + r]) for r in range(8)]
    for copy in taken:
        copy.start()
    for r in range(8):
        taken[r].wait()
        narrow[r] = wide[r].astype(bf16)
        given[r].start()
    for copy in given:
        copy.wait()


def trans_kernel(place, pack0, pack1, rel_b, counts, known, trans, source):
    stack = jnp.concatenate([rel_b[r] for r in range(8)], axis=1)
    ids = lane_ids(512, 256).astype(f32)
    wide = row_ids(place[2], 512)
    for s, pack in enumerate((pack0, pack1)):
        index = indices(pack[256:272, :])
        known[s * 8 : (s + 1) * 8, :] = jnp.concatenate([index, index], axis=0)
        column = columns(index)
        hot = (column[:, 0:1] == ids).astype(f32).astype(bf16)
        rows = dot(hot, pack[0:256, :]).astype(bf16)
        source[s * 512 : (s + 1) * 512, :] = rows
        part = by_relation(column[:, 1:2], rows)
        trans[s * 512 : (s + 1) * 512, :] = dot(part, stack, NT).astype(bf16)
        hits = (column[:, 3:4] == wide).astype(f32)
        counts[s : s + 1, :] = jnp.sum(hits, axis=0, keepdims=True)
    counts[2:8, :] = jnp.zeros((6, 512), f32)


def score_kernel(
    place, rows_in, counts0, counts1, known0, known1, trans0, trans1, source0, source1,
    weight, g_trans, kept, given, rows
):
    core = place[0]
    for z in range(2):
        both = rows_in[:, z].reshape(2, 256, 128)
        rows[z * 256 : (z + 1) * 256, :] = jnp.concatenate([both[0], both[1]], axis=1)
    index = [known[s * 8 : s * 8 + 4, :] for known in (known0, known1) for s in range(2)]
    ids = row_ids(place[2], 256)
    for b in range(8):
        s = b // 2
        column = columns(index[s])[(b % 2) * 256 : (b % 2 + 1) * 256]
        span = slice(b * 256, (b + 1) * 256)
        trans = (trans0, trans1)[b // 4][(b % 4) * 256 : (b % 4 + 1) * 256, :]
        score = dot(trans, rows[...], NT)
        sig = 1.0 / (1.0 + jnp.exp(-score))
        count = (counts0, counts1)[s // 2][s % 2 : s % 2 + 1, :]
        hit = column[:, 2:3] == ids
        part = jnp.where(hit, (count + 1.0) * sig - 1.0, count * sig).astype(bf16)
        weight[span, :] = part
        g_trans[span, :] = dot(part, rows[...]).astype(bf16)
    turned = g_trans[...].astype(f32).T
    kinds = jnp.concatenate([part[1:2] for part in index], axis=1)
    source = jnp.concatenate([source0[...], source1[...]], axis=0)
    for r in range(8):
        wanted = r + 4 * core if r < 4 else r - 4 * core
        masked = jnp.where(kinds == wanted.astype(f32), turned, 0.0).astype(bf16)
        grad = dot(masked, source).astype(bf16)
        if r < 4:
            kept[r] = grad
        else:
            given[r - 4] = grad


def partner_kernel(weight, trans0, trans1, g_rows):
    turned = jnp.concatenate([t[...].astype(f32).T.astype(bf16) for t in (trans0, trans1)], axis=1)
    for z in range(2):
        g_rows[z] = dot(turned, weight[:, z * 256 : (z + 1) * 256]).T.astype(bf16)


def own_kernel(g_trans, known0, known1, rel_b, own0, own1, far):
    sub_ids = lax.broadcasted_iota(jnp.int32, (256, 512), 0).astype(f32)
    stack = rel_b[...].reshape(2048, 256)
    for s in range(4):
        index = (known0, known1)[s // 2][(s % 2) * 8 : (s % 2 + 1) * 8, :]
        grad = g_trans[s * 512 : (s + 1) * 512, :]
        kinds = columns(index[0:4])[:, 1:2]
        parts = [
            dot(by_relation(kinds[h : h + 128], grad[h : h + 128]), stack).astype(bf16)
            for h in range(0, 512, 128)
        ]
        hot = (index[0:1, :] == sub_ids).astype(f32).astype(bf16)
        mine = dot(hot, jnp.concatenate(parts, axis=0))
        if s < 2:
            (own0, own1)[s][...] = mine
        else:
            far[s - 2] = mine.astype(bf16)


def pass_kernel(own1, came, out):
    out[...] = (own1[...] + came[1].astype(f32)).astype(bf16)


def join_kernel(kept, came, out):
    for k in range(4):
        out[k] = (kept[k].astype(f32) + came[k].astype(f32)).astype(bf16)


def pieces_kernel(got, g_rows, out):
    for h in range(2):
        half = slice(h * 128, (h + 1) * 128)
        rel = got[0, :, half].astype(f32)
        for k in range(1, 4):
            rel = rel + got[k, :, half].astype(f32)
        for p, part in enumerate((g_rows[0, :, half].astype(f32), g_rows[1, :, half].astype(f32), rel)):
            tiles = part.reshape(32, 8, 128)
            for z in range(2):
                out[h * 32 : (h + 1) * 32, z, p] = tiles[:, z * 4 : (z + 1) * 4].astype(bf16)


def route_kernel(matching, mid, out):
    rel = [jnp.zeros((4, 128), f32), jnp.zeros((4, 128), f32)]
    for d in range(64):
        rel[d % 2] = rel[d % 2] + (mid[d, 0, 2].astype(f32) + mid[d, 1, 2].astype(f32))
    for d in range(64):
        target = matching[d]
        tail = jnp.where(target % 2 == 0, rel[0], rel[1]).astype(bf16)
        for z in range(2):
            out[target, z, 0] = (mid[d, 0, z].astype(f32) + mid[d, 1, z].astype(f32)).astype(bf16)
            out[target, z, 1] = tail


def whole(last, h, p):
    span = slice(h * 32, (h + 1) * 32)
    parts = [last[span, z, p].astype(f32) for z in range(2)]
    return jnp.concatenate(parts, axis=1).reshape(256, 128)


def rel_kernel(last, out):
    for h in range(2):
        part = whole(last, h, 1).astype(bf16)
        for k in range(4):
            out[k, :, h * 128 : (h + 1) * 128] = part


def to_row(column):
    return jnp.broadcast_to(column, (256, 128)).T[0:1]


def to_column(row):
    return jnp.broadcast_to(row, (128, 256)).T[:, 0:1]


def rows_kernel(emb, accum, own0, far, near, last, new_emb, new_accum):
    grad = own0[...] + far[0].astype(f32) + near[...].astype(f32)
    grad = grad + jnp.concatenate([whole(last, 0, 0), whole(last, 1, 0)], axis=1)
    total = to_column(accum[...]) + jnp.mean(grad * grad, axis=1, keepdims=True)
    new_emb[...] = emb[...] - grad * (learn_rate / jnp.sqrt(total))
    new_accum[...] = to_row(total)


def update_kernel(place, rel, accum, grads, *rest):
    if len(rest) == 6:
        core, (seen, held, new_rel, new_accum, block, sem) = 1 - place[0], rest
    else:
        core, (new_rel, new_accum, block, sem) = place[0], rest
    old = jnp.concatenate([accum[...], accum[...]], axis=0)
    column = jnp.where(core == 0, old[0:8], old[4:12]).T
    totals, copies = [], []
    for r in range(4):
        grad = grads[r].astype(f32)
        total = column[:, r : r + 1] + jnp.mean(grad * grad, axis=1, keepdims=True)
        block[r] = rel[4 * core + r] - grad * (learn_rate / jnp.sqrt(total))
        totals.append(total)
        copies.append(pltpu.make_async_copy(block.at[r], new_rel.at[4 * core + r], sem.at[r]))
        copies[r].start()
    rows = jnp.concatenate(totals + totals, axis=1).T
    if len(rest) == 6:
        first = jnp.concatenate([held[...], held[...]], axis=0)
        mixed = jnp.concatenate([rows[0:4], first[0:4]], axis=0)
        turned = jnp.concatenate([first[0:4], rows[0:4]], axis=0)
        new_accum[...] = jnp.where(core == 0, mixed, turned)
    else:
        new_accum[...] = rows
    for copy in copies:
        copy.wait()


def update_half(place, relations, rel_accum, grads, before=None):
    given = (place, relations, rel_accum, grads) + (before or ())
    specs = [SMEM, VMEM, VMEM, VMEM] + ([ANY, VMEM] if before else [])
    return pl.pallas_call(
        update_kernel,
        out_shape=(shape((8, 256, 256), f32), shape((8, 256), f32)),
        in_specs=specs,
        out_specs=(ANY, VMEM),
        scratch_shapes=[pltpu.VMEM((4, 256, 256), f32), pltpu.SemaphoreType.DMA((4,))],
        input_output_aliases={4: 0} if before else {},
        compiler_params=pltpu.CompilerParams(vmem_limit_bytes=8 * 1024 * 1024),
        cost_estimate=pl.CostEstimate(flops=0, bytes_accessed=3_000_000, transcendentals=0),
    )(*given)


def body(
    embeddings, row_accum, relations, rel_accum, matching, src_rows, dst_rows, rel_ids, neg_rows
):
    place = jnp.stack([lax.axis_index(name) for name in ("core", "zhi", "x")]).astype(jnp.int32)
    line = lambda v: v.reshape(1, 512)
    pieces, pack = call(
        first_kernel,
        (shape((64, 8, 128), bf16), shape((272, 256), bf16)),
        0,
        (embeddings, line(src_rows), line(rel_ids), line(dst_rows), line(neg_rows)),
        moved=800_000,
        far=(0, 1, 2, 3, 4),
        space=62,
        scratch=[
            pltpu.VMEM((256, 256), f32),
            pltpu.VMEM((4, 1, 512), jnp.int32),
            pltpu.SemaphoreType.DMA((5,)),
        ],
    )
    arrived = spread(pieces, DOM)
    rel_b = call(
        cast_kernel,
        shape((8, 256, 256), bf16),
        0,
        (relations,),
        moved=3_000_000,
        far=(0,),
        far_outs=(0,),
        scratch=[
            pltpu.VMEM((8, 256, 256), f32),
            pltpu.VMEM((8, 256, 256), bf16),
            pltpu.SemaphoreType.DMA((16,)),
        ],
        space=62,
    )
    packs = [pack] + [
        lax.ppermute(pack, "x", [(i, i ^ k) for i in range(4)]) for k in range(1, 4)
    ]
    packs[1], rel_b, arrived = lax.optimization_barrier((packs[1], rel_b, arrived))
    routed = call(take_kernel, shape((64, 2, 8, 128), bf16), 1, (matching, arrived), moved=400_000)
    rows_in = spread(routed.reshape(128, 8, 128), DOM_Z).reshape(64, 2, 8, 128)
    block = shape((1024, 256), bf16)
    halves = [
        call(
            trans_kernel,
            (shape((8, 512), f32), shape((16, 512), f32), block, block),
            1,
            (place, packs[k], packs[k + 1], rel_b),
            flops=1_300_000_000,
            moved=3_000_000,
            space=16,
        )
        for k in (0, 2)
    ]
    counts, known, trans, source = zip(*halves)
    four = shape((4, 256, 256), bf16)
    weight, g_trans, kept, given = call(
        score_kernel,
        (shape((2048, 512), bf16), shape((2048, 256), bf16), four, four),
        1,
        (place, rows_in, *counts, *known, *trans, *source),
        flops=3_200_000_000,
        moved=6_000_000,
        scratch=[pltpu.VMEM((512, 256), bf16)],
        space=20,
    )
    came = swap(given, "core")
    g_rows = call(
        partner_kernel,
        shape((2, 256, 256), bf16),
        0,
        (weight, *trans),
        flops=1_500_000_000,
        moved=4_000_000,
        space=16,
    )
    came, g_rows = lax.optimization_barrier((came, g_rows))
    got = spread(call(join_kernel, four, 0, (kept, came), moved=1_500_000), "x")
    own0, own1, far = call(
        own_kernel,
        (shape((256, 256), f32), shape((256, 256), f32), shape((2, 256, 256), bf16)),
        0,
        (g_trans, *known, rel_b),
        flops=3_000_000_000,
        moved=4_000_000,
        space=16,
    )
    far, got = lax.optimization_barrier((far, got))
    far = lax.ppermute(far, "x", [(i, i ^ 2) for i in range(4)])
    out = call(
        pieces_kernel, shape((64, 2, 3, 4, 128), bf16), 0, (got, g_rows), moved=2_000_000
    )
    mid = spread(out.reshape(128, 3, 4, 128), DOM_Z)
    far, mid = lax.optimization_barrier((far, mid))
    routed_back = call(
        route_kernel,
        shape((64, 2, 2, 4, 128), bf16),
        1,
        (matching, mid.reshape(64, 2, 3, 4, 128)),
        moved=512_000,
    )
    near = call(pass_kernel, shape((256, 256), bf16), 0, (own1, far), moved=500_000)
    near = lax.ppermute(near, "x", [(i, i ^ 1) for i in range(4)])
    last = spread(routed_back.reshape(128, 2, 4, 128), DOM_Z).reshape(64, 2, 2, 4, 128)
    near, last = lax.optimization_barrier((near, last))
    rel_four = spread(call(rel_kernel, four, 0, (last,), moved=512_000), "x")
    new_embeddings, new_row_accum = call(
        rows_kernel,
        (shape((256, 256), f32), shape((1, 256), f32)),
        0,
        (embeddings, row_accum.reshape(1, 256), own0, far, near, last),
        flops=1_000_000,
        moved=1_000_000,
    )
    new_embeddings, rel_four = lax.optimization_barrier((new_embeddings, rel_four))
    rel_rest = swap(rel_four, "core")
    half = update_half(place, relations, rel_accum, rel_four)
    new_relations, new_rel_accum = update_half(place, relations, rel_accum, rel_rest, half)
    return new_embeddings, new_row_accum.reshape(256), new_relations, new_rel_accum


def solution(mesh):
    fine = Mesh(mesh.devices.reshape(4, 8, 2, 2, 4), AXES)
    placed = (
        P(AXES, None),
        P(AXES),
        P(),
        P(),
        P(),
        P(AXES),
        P(AXES),
        P(AXES),
        P(AXES, None),
    )
    return jax.shard_map(
        body,
        mesh=fine,
        in_specs=placed,
        out_specs=(P(AXES, None), P(AXES), P(), P()),
        check_vma=False,
    )
```

```python
import jax
import jax.numpy as jnp
from jax import lax
from jax.experimental import pallas as pl
from jax.experimental.pallas import tpu as pltpu
from jax.sharding import Mesh, PartitionSpec as P

learn_rate = 0.1
AXES = ("zlo", "y", "core", "zhi", "x")
DOM = ("zlo", "y", "core")
DOM_Z = DOM + ("zhi",)
bf16 = jnp.bfloat16
f32 = jnp.float32
VMEM = pl.BlockSpec(memory_space=pltpu.VMEM)
ANY = pl.BlockSpec(memory_space=pltpu.HBM)
SMEM = pl.BlockSpec(memory_space=pltpu.SMEM)
NN = (((1,), (0,)), ((), ()))
NT = (((1,), (1,)), ((), ()))


def shape(dims, dtype):
    return jax.ShapeDtypeStruct(dims, dtype)


def dot(a, b, dims=NN):
    return lax.dot_general(a, b, dims, preferred_element_type=f32)


def call(kernel, outs, scalars, args, flops=0, moved=0, scratch=(), space=8, far=(), far_outs=()):
    specs = [SMEM] * scalars + [ANY if k in far else VMEM for k in range(scalars, len(args))]
    many = isinstance(outs, tuple)
    return pl.pallas_call(
        kernel,
        out_shape=outs,
        in_specs=specs,
        out_specs=tuple(ANY if k in far_outs else VMEM for k in range(len(outs))) if many else (ANY if far_outs else VMEM),
        scratch_shapes=list(scratch),
        compiler_params=pltpu.CompilerParams(vmem_limit_bytes=space * 1024 * 1024),
        cost_estimate=pl.CostEstimate(flops=flops, bytes_accessed=moved, transcendentals=0),
    )(*args)


def swap(value, axis):
    return lax.ppermute(value, axis, [(0, 1), (1, 0)])


def spread(value, axis):
    return lax.all_to_all(value, axis, split_axis=0, concat_axis=0, tiled=True)


def first_kernel(emb, src, rel, dst, neg, pieces, pack, rows, index, sems):
    copies = [pltpu.make_async_copy(emb, rows, sems.at[0])]
    for k, part in enumerate((src, rel, dst, neg)):
        copies.append(pltpu.make_async_copy(part, index.at[k], sems.at[k + 1]))
    for copy in copies:
        copy.start()
    for copy in copies:
        copy.wait()
    wide = jnp.concatenate([index[k] for k in range(4)], axis=0)
    high = wide // 256
    low = (wide - high * 256).astype(f32)
    both = jnp.concatenate([high.astype(f32), low], axis=0)
    pack[256:272, :] = jnp.concatenate([both[:, :256], both[:, 256:]], axis=0).astype(bf16)
    pack[0:256, :] = rows[...].astype(bf16)
    for h in range(2):
        half = rows[:, h * 128 : (h + 1) * 128]
        pieces[h * 32 : (h + 1) * 32] = half.reshape(32, 8, 128).astype(bf16)


def take_kernel(matching, arrived, routed):
    for d in range(64):
        piece = arrived[matching[d]]
        routed[d, 0] = piece
        routed[d, 1] = piece


def indices(part):
    part = part.astype(f32)
    both = jnp.concatenate([part[0:8], part[8:16]], axis=1)
    return both[0:4] * 256.0 + both[4:8]


def columns(value):
    return jnp.concatenate([value, value], axis=0).T


def lane_ids(rows, width):
    return lax.broadcasted_iota(jnp.int32, (rows, width), 1)


def row_ids(x, rows):
    ids = lane_ids(rows, 512)
    return (ids + jnp.where(ids >= 256, 768, 0) + x * 256).astype(f32)


def by_relation(kinds, rows):
    wide = jnp.broadcast_to(kinds, rows.shape).astype(bf16)
    parts = [jnp.where(wide == bf16(r), rows, bf16(0)) for r in range(8)]
    return jnp.concatenate(parts, axis=1)


def cast_kernel(rel, rel_b, wide, narrow, sems):
    taken = [pltpu.make_async_copy(rel.at[r], wide.at[r], sems.at[r]) for r in range(8)]
    given = [pltpu.make_async_copy(narrow.at[r], rel_b.at[r], sems.at[8 + r]) for r in range(8)]
    for copy in taken:
        copy.start()
    for r in range(8):
        taken[r].wait()
        narrow[r] = wide[r].astype(bf16)
        given[r].start()
    for copy in given:
        copy.wait()


def span_work(x, pack, stack):
    index = indices(pack[256:272, :])
    column = columns(index)
    hot = (column[:, 0:1] == lane_ids(512, 256).astype(f32)).astype(f32).astype(bf16)
    rows = dot(hot, pack[0:256, :]).astype(bf16)
    turned = dot(by_relation(column[:, 1:2], rows), stack, NT).astype(bf16)
    hits = (column[:, 3:4] == row_ids(x, 512)).astype(f32)
    return index, rows, turned, jnp.sum(hits, axis=0, keepdims=True)


def trans_kernel(place, pack0, pack1, rel_b, counts, known, trans, source):
    stack = jnp.concatenate([rel_b[r] for r in range(8)], axis=1)
    for s, pack in enumerate((pack0, pack1)):
        index, rows, turned, count = span_work(place[2], pack, stack)
        known[s * 8 : (s + 1) * 8, :] = jnp.concatenate([index, index], axis=0)
        source[s * 512 : (s + 1) * 512, :] = rows
        trans[s * 512 : (s + 1) * 512, :] = turned
        counts[s : s + 1, :] = count
    counts[2:8, :] = jnp.zeros((6, 512), f32)


def score_kernel(
    place, rows_in, pack2, pack3, rel_b, counts, known, trans, source,
    weight, g_trans, kept, given, known1, trans1, rows, source1
):
    core = place[0]
    for z in range(2):
        both = rows_in[:, z].reshape(2, 256, 128)
        rows[z * 256 : (z + 1) * 256, :] = jnp.concatenate([both[0], both[1]], axis=1)
    index = [known[s * 8 : s * 8 + 4, :] for s in range(2)]
    count = [counts[s : s + 1, :] for s in range(2)]
    stack = jnp.concatenate([rel_b[r] for r in range(8)], axis=1)
    for s, pack in enumerate((pack2, pack3)):
        one, away, turned, many = span_work(place[2], pack, stack)
        known1[s * 8 : (s + 1) * 8, :] = jnp.concatenate([one, one], axis=0)
        source1[s * 512 : (s + 1) * 512, :] = away
        trans1[s * 512 : (s + 1) * 512, :] = turned
        index.append(one)
        count.append(many)
    ids = row_ids(place[2], 256)
    for b in range(8):
        s = b // 2
        column = columns(index[s])[(b % 2) * 256 : (b % 2 + 1) * 256]
        span = slice(b * 256, (b + 1) * 256)
        turned = (trans, trans1)[b // 4][(b % 4) * 256 : (b % 4 + 1) * 256, :]
        score = dot(turned, rows[...], NT)
        sig = 1.0 / (1.0 + jnp.exp(-score))
        hit = column[:, 2:3] == ids
        part = jnp.where(hit, (count[s] + 1.0) * sig - 1.0, count[s] * sig).astype(bf16)
        weight[span, :] = part
        g_trans[span, :] = dot(part, rows[...]).astype(bf16)
    turned = g_trans[...].astype(f32).T
    kinds = jnp.concatenate([part[1:2] for part in index], axis=1)
    every = jnp.concatenate([source[...], source1[...]], axis=0)
    for r in range(8):
        wanted = r + 4 * core if r < 4 else r - 4 * core
        masked = jnp.where(kinds == wanted.astype(f32), turned, 0.0).astype(bf16)
        grad = dot(masked, every).astype(bf16)
        if r < 4:
            kept[r] = grad
        else:
            given[r - 4] = grad


def partner_kernel(weight, trans0, trans1, g_rows):
    turned = jnp.concatenate([t[...].astype(f32).T.astype(bf16) for t in (trans0, trans1)], axis=1)
    for z in range(2):
        g_rows[z] = dot(turned, weight[:, z * 256 : (z + 1) * 256]).T.astype(bf16)


def own_kernel(g_trans, known0, known1, rel_b, own0, own1, far):
    sub_ids = lax.broadcasted_iota(jnp.int32, (256, 512), 0).astype(f32)
    stack = rel_b[...].reshape(2048, 256)
    for s in range(4):
        index = (known0, known1)[s // 2][(s % 2) * 8 : (s % 2 + 1) * 8, :]
        grad = g_trans[s * 512 : (s + 1) * 512, :]
        kinds = columns(index[0:4])[:, 1:2]
        parts = [
            dot(by_relation(kinds[h : h + 128], grad[h : h + 128]), stack).astype(bf16)
            for h in range(0, 512, 128)
        ]
        hot = (index[0:1, :] == sub_ids).astype(f32).astype(bf16)
        mine = dot(hot, jnp.concatenate(parts, axis=0))
        if s < 2:
            (own0, own1)[s][...] = mine
        else:
            far[s - 2] = mine.astype(bf16)


def pass_kernel(own1, came, out):
    out[...] = (own1[...] + came[1].astype(f32)).astype(bf16)


def join_kernel(kept, came, out):
    for k in range(4):
        out[k] = (kept[k].astype(f32) + came[k].astype(f32)).astype(bf16)


def pieces_kernel(got, g_rows, out):
    for h in range(2):
        half = slice(h * 128, (h + 1) * 128)
        rel = got[0, :, half].astype(f32)
        for k in range(1, 4):
            rel = rel + got[k, :, half].astype(f32)
        for p, part in enumerate((g_rows[0, :, half].astype(f32), g_rows[1, :, half].astype(f32), rel)):
            tiles = part.reshape(32, 8, 128)
            for z in range(2):
                out[h * 32 : (h + 1) * 32, z, p] = tiles[:, z * 4 : (z + 1) * 4].astype(bf16)


def route_kernel(matching, mid, out):
    rel = [jnp.zeros((4, 128), f32), jnp.zeros((4, 128), f32)]
    for d in range(64):
        rel[d % 2] = rel[d % 2] + (mid[d, 0, 2].astype(f32) + mid[d, 1, 2].astype(f32))
    for d in range(64):
        target = matching[d]
        tail = jnp.where(target % 2 == 0, rel[0], rel[1]).astype(bf16)
        for z in range(2):
            out[target, z, 0] = (mid[d, 0, z].astype(f32) + mid[d, 1, z].astype(f32)).astype(bf16)
            out[target, z, 1] = tail


def whole(last, h, p):
    span = slice(h * 32, (h + 1) * 32)
    parts = [last[span, z, p].astype(f32) for z in range(2)]
    return jnp.concatenate(parts, axis=1).reshape(256, 128)


def rel_kernel(last, out):
    for h in range(2):
        part = whole(last, h, 1).astype(bf16)
        for k in range(4):
            out[k, :, h * 128 : (h + 1) * 128] = part


def to_row(column):
    return jnp.broadcast_to(column, (256, 128)).T[0:1]


def to_column(row):
    return jnp.broadcast_to(row, (128, 256)).T[:, 0:1]


def rows_kernel(emb, accum, own0, far, near, last, new_emb, new_accum):
    grad = own0[...] + far[0].astype(f32) + near[...].astype(f32)
    grad = grad + jnp.concatenate([whole(last, 0, 0), whole(last, 1, 0)], axis=1)
    total = to_column(accum[...]) + jnp.mean(grad * grad, axis=1, keepdims=True)
    new_emb[...] = emb[...] - grad * (learn_rate / jnp.sqrt(total))
    new_accum[...] = to_row(total)


def update_kernel(place, rel, accum, grads, *rest):
    if len(rest) == 6:
        core, (seen, held, new_rel, new_accum, block, sem) = 1 - place[0], rest
    else:
        core, (new_rel, new_accum, block, sem) = place[0], rest
    old = jnp.concatenate([accum[...], accum[...]], axis=0)
    column = jnp.where(core == 0, old[0:8], old[4:12]).T
    totals, copies = [], []
    for r in range(4):
        grad = grads[r].astype(f32)
        total = column[:, r : r + 1] + jnp.mean(grad * grad, axis=1, keepdims=True)
        block[r] = rel[4 * core + r] - grad * (learn_rate / jnp.sqrt(total))
        totals.append(total)
        copies.append(pltpu.make_async_copy(block.at[r], new_rel.at[4 * core + r], sem.at[r]))
        copies[r].start()
    rows = jnp.concatenate(totals + totals, axis=1).T
    if len(rest) == 6:
        first = jnp.concatenate([held[...], held[...]], axis=0)
        mixed = jnp.concatenate([rows[0:4], first[0:4]], axis=0)
        turned = jnp.concatenate([first[0:4], rows[0:4]], axis=0)
        new_accum[...] = jnp.where(core == 0, mixed, turned)
    else:
        new_accum[...] = rows
    for copy in copies:
        copy.wait()


def update_half(place, relations, rel_accum, grads, before=None):
    given = (place, relations, rel_accum, grads) + (before or ())
    specs = [SMEM, VMEM, VMEM, VMEM] + ([ANY, VMEM] if before else [])
    return pl.pallas_call(
        update_kernel,
        out_shape=(shape((8, 256, 256), f32), shape((8, 256), f32)),
        in_specs=specs,
        out_specs=(ANY, VMEM),
        scratch_shapes=[pltpu.VMEM((4, 256, 256), f32), pltpu.SemaphoreType.DMA((4,))],
        input_output_aliases={4: 0} if before else {},
        compiler_params=pltpu.CompilerParams(vmem_limit_bytes=8 * 1024 * 1024),
        cost_estimate=pl.CostEstimate(flops=0, bytes_accessed=3_000_000, transcendentals=0),
    )(*given)


def body(
    embeddings, row_accum, relations, rel_accum, matching, src_rows, dst_rows, rel_ids, neg_rows
):
    place = jnp.stack([lax.axis_index(name) for name in ("core", "zhi", "x")]).astype(jnp.int32)
    line = lambda v: v.reshape(1, 512)
    pieces, pack = call(
        first_kernel,
        (shape((64, 8, 128), bf16), shape((272, 256), bf16)),
        0,
        (embeddings, line(src_rows), line(rel_ids), line(dst_rows), line(neg_rows)),
        moved=800_000,
        far=(0, 1, 2, 3, 4),
        space=62,
        scratch=[
            pltpu.VMEM((256, 256), f32),
            pltpu.VMEM((4, 1, 512), jnp.int32),
            pltpu.SemaphoreType.DMA((5,)),
        ],
    )
    arrived = spread(pieces, DOM)
    rel_b = call(
        cast_kernel,
        shape((8, 256, 256), bf16),
        0,
        (relations,),
        moved=3_000_000,
        far=(0,),
        far_outs=(0,),
        scratch=[
            pltpu.VMEM((8, 256, 256), f32),
            pltpu.VMEM((8, 256, 256), bf16),
            pltpu.SemaphoreType.DMA((16,)),
        ],
        space=62,
    )
    packs = [pack] + [
        lax.ppermute(pack, "x", [(i, i ^ k) for i in range(4)]) for k in range(1, 4)
    ]
    packs[1], rel_b, arrived = lax.optimization_barrier((packs[1], rel_b, arrived))
    routed = call(take_kernel, shape((64, 2, 8, 128), bf16), 1, (matching, arrived), moved=400_000)
    rows_in = spread(routed.reshape(128, 8, 128), DOM_Z).reshape(64, 2, 8, 128)
    block = shape((1024, 256), bf16)
    known_shape = shape((16, 512), f32)
    counts, known0, trans0, source0 = call(
        trans_kernel,
        (shape((8, 512), f32), known_shape, block, block),
        1,
        (place, packs[0], packs[1], rel_b),
        flops=1_300_000_000,
        moved=3_000_000,
        space=16,
    )
    four = shape((4, 256, 256), bf16)
    weight, g_trans, kept, given, known1, trans1 = call(
        score_kernel,
        (shape((2048, 512), bf16), shape((2048, 256), bf16), four, four, known_shape, block),
        1,
        (place, rows_in, packs[2], packs[3], rel_b, counts, known0, trans0, source0),
        flops=4_500_000_000,
        moved=6_000_000,
        scratch=[pltpu.VMEM((512, 256), bf16), pltpu.VMEM((1024, 256), bf16)],
        space=28,
    )
    came = swap(given, "core")
    g_rows = call(
        partner_kernel,
        shape((2, 256, 256), bf16),
        0,
        (weight, trans0, trans1),
        flops=1_500_000_000,
        moved=4_000_000,
        space=16,
    )
    came, g_rows = lax.optimization_barrier((came, g_rows))
    got = spread(call(join_kernel, four, 0, (kept, came), moved=1_500_000), "x")
    own0, own1, far = call(
        own_kernel,
        (shape((256, 256), f32), shape((256, 256), f32), shape((2, 256, 256), bf16)),
        0,
        (g_trans, known0, known1, rel_b),
        flops=3_000_000_000,
        moved=4_000_000,
        space=16,
    )
    far, got = lax.optimization_barrier((far, got))
    far = lax.ppermute(far, "x", [(i, i ^ 2) for i in range(4)])
    out = call(
        pieces_kernel, shape((64, 2, 3, 4, 128), bf16), 0, (got, g_rows), moved=2_000_000
    )
    mid = spread(out.reshape(128, 3, 4, 128), DOM_Z)
    far, mid = lax.optimization_barrier((far, mid))
    routed_back = call(
        route_kernel,
        shape((64, 2, 2, 4, 128), bf16),
        1,
        (matching, mid.reshape(64, 2, 3, 4, 128)),
        moved=512_000,
    )
    near = call(pass_kernel, shape((256, 256), bf16), 0, (own1, far), moved=500_000)
    near = lax.ppermute(near, "x", [(i, i ^ 1) for i in range(4)])
    last = spread(routed_back.reshape(128, 2, 4, 128), DOM_Z).reshape(64, 2, 2, 4, 128)
    near, last = lax.optimization_barrier((near, last))
    rel_four = spread(call(rel_kernel, four, 0, (last,), moved=512_000), "x")
    new_embeddings, new_row_accum = call(
        rows_kernel,
        (shape((256, 256), f32), shape((1, 256), f32)),
        0,
        (embeddings, row_accum.reshape(1, 256), own0, far, near, last),
        flops=1_000_000,
        moved=1_000_000,
    )
    new_embeddings, rel_four = lax.optimization_barrier((new_embeddings, rel_four))
    rel_rest = swap(rel_four, "core")
    half = update_half(place, relations, rel_accum, rel_four)
    new_relations, new_rel_accum = update_half(place, relations, rel_accum, rel_rest, half)
    return new_embeddings, new_row_accum.reshape(256), new_relations, new_rel_accum


def solution(mesh):
    fine = Mesh(mesh.devices.reshape(4, 8, 2, 2, 4), AXES)
    placed = (
        P(AXES, None),
        P(AXES),
        P(),
        P(),
        P(),
        P(AXES),
        P(AXES),
        P(AXES),
        P(AXES, None),
    )
    return jax.shard_map(
        body,
        mesh=fine,
        in_specs=placed,
        out_specs=(P(AXES, None), P(AXES), P(), P()),
        check_vma=False,
    )
```

```python
import jax
import jax.numpy as jnp
from jax import lax
from jax.experimental import pallas as pl
from jax.experimental.pallas import tpu as pltpu
from jax.sharding import Mesh, PartitionSpec as P

learn_rate = 0.1
AXES = ("zlo", "y", "core", "zhi", "x")
DOM = ("zlo", "y", "core")
DOM_Z = DOM + ("zhi",)
bf16 = jnp.bfloat16
f32 = jnp.float32
VMEM = pl.BlockSpec(memory_space=pltpu.VMEM)
ANY = pl.BlockSpec(memory_space=pltpu.HBM)
SMEM = pl.BlockSpec(memory_space=pltpu.SMEM)
NN = (((1,), (0,)), ((), ()))
NT = (((1,), (1,)), ((), ()))


def shape(dims, dtype):
    return jax.ShapeDtypeStruct(dims, dtype)


def dot(a, b, dims=NN):
    return lax.dot_general(a, b, dims, preferred_element_type=f32)


def call(kernel, outs, scalars, args, flops=0, moved=0, scratch=(), space=8, far=(), far_outs=()):
    specs = [SMEM] * scalars + [ANY if k in far else VMEM for k in range(scalars, len(args))]
    many = isinstance(outs, tuple)
    return pl.pallas_call(
        kernel,
        out_shape=outs,
        in_specs=specs,
        out_specs=tuple(ANY if k in far_outs else VMEM for k in range(len(outs))) if many else (ANY if far_outs else VMEM),
        scratch_shapes=list(scratch),
        compiler_params=pltpu.CompilerParams(vmem_limit_bytes=space * 1024 * 1024),
        cost_estimate=pl.CostEstimate(flops=flops, bytes_accessed=moved, transcendentals=0),
    )(*args)


def swap(value, axis):
    return lax.ppermute(value, axis, [(0, 1), (1, 0)])


def spread(value, axis):
    return lax.all_to_all(value, axis, split_axis=0, concat_axis=0, tiled=True)


def first_kernel(emb, src, rel, dst, neg, pieces, pack, rows, index, sems):
    copies = [pltpu.make_async_copy(emb, rows, sems.at[0])]
    for k, part in enumerate((src, rel, dst, neg)):
        copies.append(pltpu.make_async_copy(part, index.at[k], sems.at[k + 1]))
    for copy in copies:
        copy.start()
    for copy in copies:
        copy.wait()
    wide = jnp.concatenate([index[k] for k in range(4)], axis=0)
    high = wide // 256
    low = (wide - high * 256).astype(f32)
    both = jnp.concatenate([high.astype(f32), low], axis=0)
    pack[256:272, :] = jnp.concatenate([both[:, :256], both[:, 256:]], axis=0).astype(bf16)
    pack[0:256, :] = rows[...].astype(bf16)
    for h in range(2):
        half = rows[:, h * 128 : (h + 1) * 128]
        pieces[h * 32 : (h + 1) * 32] = half.reshape(32, 8, 128).astype(bf16)


def take_kernel(matching, arrived, routed):
    for d in range(64):
        piece = arrived[matching[d]]
        routed[d, 0] = piece
        routed[d, 1] = piece


def indices(part):
    part = part.astype(f32)
    both = jnp.concatenate([part[0:8], part[8:16]], axis=1)
    return both[0:4] * 256.0 + both[4:8]


def columns(value):
    return jnp.concatenate([value, value], axis=0).T


def lane_ids(rows, width):
    return lax.broadcasted_iota(jnp.int32, (rows, width), 1)


def row_ids(x, rows):
    ids = lane_ids(rows, 512)
    return (ids + jnp.where(ids >= 256, 768, 0) + x * 256).astype(f32)


def by_relation(kinds, rows):
    wide = jnp.broadcast_to(kinds, rows.shape).astype(bf16)
    parts = [jnp.where(wide == bf16(r), rows, bf16(0)) for r in range(8)]
    return jnp.concatenate(parts, axis=1)


def cast_kernel(rel, rel_b, wide, narrow, sems):
    taken = [pltpu.make_async_copy(rel.at[r], wide.at[r], sems.at[r]) for r in range(8)]
    given = [pltpu.make_async_copy(narrow.at[r], rel_b.at[r], sems.at[8 + r]) for r in range(8)]
    for copy in taken:
        copy.start()
    for r in range(8):
        taken[r].wait()
        narrow[r] = wide[r].astype(bf16)
        given[r].start()
    for copy in given:
        copy.wait()


def span_work(x, pack, stack):
    index = indices(pack[256:272, :])
    column = columns(index)
    hot = (column[:, 0:1] == lane_ids(512, 256).astype(f32)).astype(f32).astype(bf16)
    rows = dot(hot, pack[0:256, :]).astype(bf16)
    turned = dot(by_relation(column[:, 1:2], rows), stack, NT).astype(bf16)
    hits = (column[:, 3:4] == row_ids(x, 512)).astype(f32)
    return index, rows, turned, jnp.sum(hits, axis=0, keepdims=True)


def trans_kernel(place, pack0, pack1, rel_b, counts, known, trans, source):
    stack = jnp.concatenate([rel_b[r] for r in range(8)], axis=1)
    for s, pack in enumerate((pack0, pack1)):
        index, rows, turned, count = span_work(place[2], pack, stack)
        known[s * 8 : (s + 1) * 8, :] = jnp.concatenate([index, index], axis=0)
        source[s * 512 : (s + 1) * 512, :] = rows
        trans[s * 512 : (s + 1) * 512, :] = turned
        counts[s : s + 1, :] = count
    counts[2:8, :] = jnp.zeros((6, 512), f32)


def score_kernel(
    place, rows_in, pack2, pack3, rel_b, counts, known, trans, source,
    weight, g_trans, kept, given, known1, trans1, rows, source1
):
    core = place[0]
    for z in range(2):
        both = rows_in[:, z].reshape(2, 256, 128)
        rows[z * 256 : (z + 1) * 256, :] = jnp.concatenate([both[0], both[1]], axis=1)
    index = [known[s * 8 : s * 8 + 4, :] for s in range(2)]
    count = [counts[s : s + 1, :] for s in range(2)]
    stack = jnp.concatenate([rel_b[r] for r in range(8)], axis=1)
    for s, pack in enumerate((pack2, pack3)):
        one, away, turned, many = span_work(place[2], pack, stack)
        known1[s * 8 : (s + 1) * 8, :] = jnp.concatenate([one, one], axis=0)
        source1[s * 512 : (s + 1) * 512, :] = away
        trans1[s * 512 : (s + 1) * 512, :] = turned
        index.append(one)
        count.append(many)
    ids = row_ids(place[2], 256)
    for b in range(8):
        s = b // 2
        column = columns(index[s])[(b % 2) * 256 : (b % 2 + 1) * 256]
        span = slice(b * 256, (b + 1) * 256)
        turned = (trans, trans1)[b // 4][(b % 4) * 256 : (b % 4 + 1) * 256, :]
        score = dot(turned, rows[...], NT)
        sig = 1.0 / (1.0 + jnp.exp(-score))
        hit = column[:, 2:3] == ids
        part = jnp.where(hit, (count[s] + 1.0) * sig - 1.0, count[s] * sig).astype(bf16)
        weight[span, :] = part
        g_trans[span, :] = dot(part, rows[...]).astype(bf16)
    turned = g_trans[...].astype(f32).T
    kinds = jnp.concatenate([part[1:2] for part in index], axis=1)
    every = jnp.concatenate([source[...], source1[...]], axis=0)
    for r in range(8):
        wanted = r + 4 * core if r < 4 else r - 4 * core
        masked = jnp.where(kinds == wanted.astype(f32), turned, 0.0).astype(bf16)
        grad = dot(masked, every).astype(bf16)
        if r < 4:
            kept[r] = grad
        else:
            given[r - 4] = grad


def partner_kernel(weight, trans0, trans1, g_rows):
    turned = jnp.concatenate([t[...].astype(f32).T.astype(bf16) for t in (trans0, trans1)], axis=1)
    for z in range(2):
        g_rows[z] = dot(turned, weight[:, z * 256 : (z + 1) * 256]).T.astype(bf16)


def own_kernel(g_trans, known0, known1, rel_b, own0, own1, far):
    sub_ids = lax.broadcasted_iota(jnp.int32, (256, 512), 0).astype(f32)
    stack = rel_b[...].reshape(2048, 256)
    for s in range(4):
        index = (known0, known1)[s // 2][(s % 2) * 8 : (s % 2 + 1) * 8, :]
        grad = g_trans[s * 512 : (s + 1) * 512, :]
        kinds = columns(index[0:4])[:, 1:2]
        parts = [
            dot(by_relation(kinds[h : h + 128], grad[h : h + 128]), stack).astype(bf16)
            for h in range(0, 512, 128)
        ]
        hot = (index[0:1, :] == sub_ids).astype(f32).astype(bf16)
        mine = dot(hot, jnp.concatenate(parts, axis=0))
        if s < 2:
            (own0, own1)[s][...] = mine
        else:
            far[s - 2] = mine.astype(bf16)


def pass_kernel(own1, came, out):
    out[...] = (own1[...] + came[1].astype(f32)).astype(bf16)


def join_kernel(kept, came, out):
    for k in range(4):
        out[k] = (kept[k].astype(f32) + came[k].astype(f32)).astype(bf16)


def pieces_kernel(got, g_rows, out):
    for h in range(2):
        half = slice(h * 128, (h + 1) * 128)
        rel = got[0, :, half].astype(f32)
        for k in range(1, 4):
            rel = rel + got[k, :, half].astype(f32)
        for p, part in enumerate((g_rows[0, :, half].astype(f32), g_rows[1, :, half].astype(f32), rel)):
            tiles = part.reshape(32, 8, 128)
            for z in range(2):
                out[h * 32 : (h + 1) * 32, z, p] = tiles[:, z * 4 : (z + 1) * 4].astype(bf16)


def route_kernel(matching, mid, out):
    rel = [jnp.zeros((4, 128), f32), jnp.zeros((4, 128), f32)]
    for d in range(64):
        rel[d % 2] = rel[d % 2] + (mid[d, 0, 2].astype(f32) + mid[d, 1, 2].astype(f32))
    for d in range(64):
        target = matching[d]
        tail = jnp.where(target % 2 == 0, rel[0], rel[1]).astype(bf16)
        for z in range(2):
            out[target, z, 0] = (mid[d, 0, z].astype(f32) + mid[d, 1, z].astype(f32)).astype(bf16)
            out[target, z, 1] = tail


def whole(last, h, p):
    span = slice(h * 32, (h + 1) * 32)
    parts = [last[span, z, p].astype(f32) for z in range(2)]
    return jnp.concatenate(parts, axis=1).reshape(256, 128)


def rel_kernel(last, out):
    for h in range(2):
        part = whole(last, h, 1).astype(bf16)
        for k in range(4):
            out[k, :, h * 128 : (h + 1) * 128] = part


def to_row(column):
    return jnp.broadcast_to(column, (256, 128)).T[0:1]


def to_column(row):
    return jnp.broadcast_to(row, (128, 256)).T[:, 0:1]


def rows_kernel(emb, accum, own0, far, near, last, new_emb, new_accum):
    grad = own0[...] + far[0].astype(f32) + near[...].astype(f32)
    grad = grad + jnp.concatenate([whole(last, 0, 0), whole(last, 1, 0)], axis=1)
    total = to_column(accum[...]) + jnp.mean(grad * grad, axis=1, keepdims=True)
    new_emb[...] = emb[...] - grad * (learn_rate / jnp.sqrt(total))
    new_accum[...] = to_row(total)


def update_kernel(place, rel, accum, grads, *rest):
    if len(rest) == 6:
        core, (seen, held, new_rel, new_accum, block, sem) = 1 - place[0], rest
    else:
        core, (new_rel, new_accum, block, sem) = place[0], rest
    old = jnp.concatenate([accum[...], accum[...]], axis=0)
    column = jnp.where(core == 0, old[0:8], old[4:12]).T
    totals, copies = [], []
    for r in range(4):
        grad = grads[r].astype(f32)
        total = column[:, r : r + 1] + jnp.mean(grad * grad, axis=1, keepdims=True)
        block[r] = rel[4 * core + r] - grad * (learn_rate / jnp.sqrt(total))
        totals.append(total)
        copies.append(pltpu.make_async_copy(block.at[r], new_rel.at[4 * core + r], sem.at[r]))
        copies[r].start()
    rows = jnp.concatenate(totals + totals, axis=1).T
    if len(rest) == 6:
        first = jnp.concatenate([held[...], held[...]], axis=0)
        mixed = jnp.concatenate([rows[0:4], first[0:4]], axis=0)
        turned = jnp.concatenate([first[0:4], rows[0:4]], axis=0)
        new_accum[...] = jnp.where(core == 0, mixed, turned)
    else:
        new_accum[...] = rows
    for copy in copies:
        copy.wait()


def update_half(place, relations, rel_accum, grads, before=None):
    given = (place, relations, rel_accum, grads) + (before or ())
    specs = [SMEM, VMEM, VMEM, VMEM] + ([ANY, VMEM] if before else [])
    return pl.pallas_call(
        update_kernel,
        out_shape=(shape((8, 256, 256), f32), shape((8, 256), f32)),
        in_specs=specs,
        out_specs=(ANY, VMEM),
        scratch_shapes=[pltpu.VMEM((4, 256, 256), f32), pltpu.SemaphoreType.DMA((4,))],
        input_output_aliases={4: 0} if before else {},
        compiler_params=pltpu.CompilerParams(vmem_limit_bytes=8 * 1024 * 1024),
        cost_estimate=pl.CostEstimate(flops=0, bytes_accessed=3_000_000, transcendentals=0),
    )(*given)


def body(
    embeddings, row_accum, relations, rel_accum, matching, src_rows, dst_rows, rel_ids, neg_rows
):
    place = jnp.stack([lax.axis_index(name) for name in ("core", "zhi", "x")]).astype(jnp.int32)
    line = lambda v: v.reshape(1, 512)
    pieces, pack = call(
        first_kernel,
        (shape((64, 8, 128), bf16), shape((272, 256), bf16)),
        0,
        (embeddings, line(src_rows), line(rel_ids), line(dst_rows), line(neg_rows)),
        moved=800_000,
        far=(0, 1, 2, 3, 4),
        space=62,
        scratch=[
            pltpu.VMEM((256, 256), f32),
            pltpu.VMEM((4, 1, 512), jnp.int32),
            pltpu.SemaphoreType.DMA((5,)),
        ],
    )
    arrived = spread(pieces, DOM)
    rel_b = call(
        cast_kernel,
        shape((8, 256, 256), bf16),
        0,
        (relations,),
        moved=3_000_000,
        far=(0,),
        far_outs=(0,),
        scratch=[
            pltpu.VMEM((8, 256, 256), f32),
            pltpu.VMEM((8, 256, 256), bf16),
            pltpu.SemaphoreType.DMA((16,)),
        ],
        space=62,
    )
    packs = [pack] + [
        lax.ppermute(pack, "x", [(i, i ^ k) for i in range(4)]) for k in range(1, 4)
    ]
    packs[1], rel_b, arrived = lax.optimization_barrier((packs[1], rel_b, arrived))
    routed = call(take_kernel, shape((64, 2, 8, 128), bf16), 1, (matching, arrived), moved=400_000)
    rows_in = spread(routed.reshape(128, 8, 128), DOM_Z).reshape(64, 2, 8, 128)
    block = shape((1024, 256), bf16)
    known_shape = shape((16, 512), f32)
    counts, known0, trans0, source0 = call(
        trans_kernel,
        (shape((8, 512), f32), known_shape, block, block),
        1,
        (place, packs[0], packs[1], rel_b),
        flops=1_300_000_000,
        moved=3_000_000,
        space=16,
    )
    four = shape((4, 256, 256), bf16)
    weight, g_trans, kept, given, known1, trans1 = call(
        score_kernel,
        (shape((2048, 512), bf16), shape((2048, 256), bf16), four, four, known_shape, block),
        1,
        (place, rows_in, packs[2], packs[3], rel_b, counts, known0, trans0, source0),
        flops=4_500_000_000,
        moved=6_000_000,
        scratch=[pltpu.VMEM((512, 256), bf16), pltpu.VMEM((1024, 256), bf16)],
        space=28,
    )
    came = swap(given, "core")
    g_rows = call(
        partner_kernel,
        shape((2, 256, 256), bf16),
        0,
        (weight, trans0, trans1),
        flops=1_500_000_000,
        moved=4_000_000,
        space=16,
    )
    came, g_rows = lax.optimization_barrier((came, g_rows))
    got = spread(call(join_kernel, four, 0, (kept, came), moved=1_500_000), "x")
    own0, own1, far = call(
        own_kernel,
        (shape((256, 256), f32), shape((256, 256), f32), shape((2, 256, 256), bf16)),
        0,
        (g_trans, known0, known1, rel_b),
        flops=3_000_000_000,
        moved=4_000_000,
        space=16,
    )
    out = call(
        pieces_kernel, shape((64, 2, 3, 4, 128), bf16), 0, (got, g_rows), moved=2_000_000
    )
    mid = spread(out.reshape(128, 3, 4, 128), DOM_Z)
    far, mid = lax.optimization_barrier((far, mid))
    far = lax.ppermute(far, "x", [(i, i ^ 2) for i in range(4)])
    routed_back = call(
        route_kernel,
        shape((64, 2, 2, 4, 128), bf16),
        1,
        (matching, mid.reshape(64, 2, 3, 4, 128)),
        moved=512_000,
    )
    last = spread(routed_back.reshape(128, 2, 4, 128), DOM_Z).reshape(64, 2, 2, 4, 128)
    far, last = lax.optimization_barrier((far, last))
    near = call(pass_kernel, shape((256, 256), bf16), 0, (own1, far), moved=500_000)
    near = lax.ppermute(near, "x", [(i, i ^ 1) for i in range(4)])
    rel_four = spread(call(rel_kernel, four, 0, (last,), moved=512_000), "x")
    new_embeddings, new_row_accum = call(
        rows_kernel,
        (shape((256, 256), f32), shape((1, 256), f32)),
        0,
        (embeddings, row_accum.reshape(1, 256), own0, far, near, last),
        flops=1_000_000,
        moved=1_000_000,
    )
    new_embeddings, rel_four = lax.optimization_barrier((new_embeddings, rel_four))
    rel_rest = swap(rel_four, "core")
    half = update_half(place, relations, rel_accum, rel_four)
    new_relations, new_rel_accum = update_half(place, relations, rel_accum, rel_rest, half)
    return new_embeddings, new_row_accum.reshape(256), new_relations, new_rel_accum


def solution(mesh):
    fine = Mesh(mesh.devices.reshape(4, 8, 2, 2, 4), AXES)
    placed = (
        P(AXES, None),
        P(AXES),
        P(),
        P(),
        P(),
        P(AXES),
        P(AXES),
        P(AXES),
        P(AXES, None),
    )
    return jax.shard_map(
        body,
        mesh=fine,
        in_specs=placed,
        out_specs=(P(AXES, None), P(AXES), P(), P()),
        check_vma=False,
    )
```

```python
import jax
import jax.numpy as jnp
from jax import lax
from jax.experimental import pallas as pl
from jax.experimental.pallas import tpu as pltpu
from jax.sharding import Mesh, PartitionSpec as P

learn_rate = 0.1
AXES = ("zlo", "y", "core", "zhi", "x")
DOM = ("zlo", "y", "core")
DOM_Z = DOM + ("zhi",)
bf16 = jnp.bfloat16
f32 = jnp.float32
VMEM = pl.BlockSpec(memory_space=pltpu.VMEM)
ANY = pl.BlockSpec(memory_space=pltpu.HBM)
SMEM = pl.BlockSpec(memory_space=pltpu.SMEM)
NN = (((1,), (0,)), ((), ()))
NT = (((1,), (1,)), ((), ()))


def shape(dims, dtype):
    return jax.ShapeDtypeStruct(dims, dtype)


def dot(a, b, dims=NN):
    return lax.dot_general(a, b, dims, preferred_element_type=f32)


def call(kernel, outs, scalars, args, flops=0, moved=0, scratch=(), space=8, far=(), far_outs=()):
    specs = [SMEM] * scalars + [ANY if k in far else VMEM for k in range(scalars, len(args))]
    many = isinstance(outs, tuple)
    return pl.pallas_call(
        kernel,
        out_shape=outs,
        in_specs=specs,
        out_specs=tuple(ANY if k in far_outs else VMEM for k in range(len(outs))) if many else (ANY if far_outs else VMEM),
        scratch_shapes=list(scratch),
        compiler_params=pltpu.CompilerParams(vmem_limit_bytes=space * 1024 * 1024),
        cost_estimate=pl.CostEstimate(flops=flops, bytes_accessed=moved, transcendentals=0),
    )(*args)


def swap(value, axis):
    return lax.ppermute(value, axis, [(0, 1), (1, 0)])


def spread(value, axis):
    return lax.all_to_all(value, axis, split_axis=0, concat_axis=0, tiled=True)


def first_kernel(emb, src, rel, dst, neg, pieces, pack, rows, index, sems):
    copies = [pltpu.make_async_copy(emb, rows, sems.at[0])]
    for k, part in enumerate((src, rel, dst, neg)):
        copies.append(pltpu.make_async_copy(part, index.at[k], sems.at[k + 1]))
    for copy in copies:
        copy.start()
    for copy in copies:
        copy.wait()
    wide = jnp.concatenate([index[k] for k in range(4)], axis=0)
    high = wide // 256
    low = (wide - high * 256).astype(f32)
    both = jnp.concatenate([high.astype(f32), low], axis=0)
    pack[256:272, :] = jnp.concatenate([both[:, :256], both[:, 256:]], axis=0).astype(bf16)
    pack[0:256, :] = rows[...].astype(bf16)
    for h in range(2):
        half = rows[:, h * 128 : (h + 1) * 128]
        pieces[h * 32 : (h + 1) * 32] = half.reshape(32, 8, 128).astype(bf16)


def take_kernel(matching, arrived, routed):
    for d in range(64):
        piece = arrived[matching[d]]
        routed[d, 0] = piece
        routed[d, 1] = piece


def indices(part):
    part = part.astype(f32)
    both = jnp.concatenate([part[0:8], part[8:16]], axis=1)
    return both[0:4] * 256.0 + both[4:8]


def columns(value):
    return jnp.concatenate([value, value], axis=0).T


def lane_ids(rows, width):
    return lax.broadcasted_iota(jnp.int32, (rows, width), 1)


def row_ids(x, rows):
    ids = lane_ids(rows, 512)
    return (ids + jnp.where(ids >= 256, 768, 0) + x * 256).astype(f32)


def by_relation(kinds, rows):
    wide = jnp.broadcast_to(kinds, rows.shape).astype(bf16)
    parts = [jnp.where(wide == bf16(r), rows, bf16(0)) for r in range(8)]
    return jnp.concatenate(parts, axis=1)


def cast_kernel(rel, rel_b, wide, narrow, sems):
    taken = [pltpu.make_async_copy(rel.at[r], wide.at[r], sems.at[r]) for r in range(8)]
    given = [pltpu.make_async_copy(narrow.at[r], rel_b.at[r], sems.at[8 + r]) for r in range(8)]
    for copy in taken:
        copy.start()
    for r in range(8):
        taken[r].wait()
        narrow[r] = wide[r].astype(bf16)
        given[r].start()
    for copy in given:
        copy.wait()


def span_work(x, pack, stack):
    index = indices(pack[256:272, :])
    column = columns(index)
    hot = (column[:, 0:1] == lane_ids(512, 256).astype(f32)).astype(f32).astype(bf16)
    rows = dot(hot, pack[0:256, :]).astype(bf16)
    turned = dot(by_relation(column[:, 1:2], rows), stack, NT).astype(bf16)
    hits = (column[:, 3:4] == row_ids(x, 512)).astype(f32)
    return index, rows, turned, jnp.sum(hits, axis=0, keepdims=True)


def trans_kernel(place, pack0, pack1, rel_b, counts, known, trans, source):
    stack = jnp.concatenate([rel_b[r] for r in range(8)], axis=1)
    for s, pack in enumerate((pack0, pack1)):
        index, rows, turned, count = span_work(place[2], pack, stack)
        known[s * 8 : (s + 1) * 8, :] = jnp.concatenate([index, index], axis=0)
        source[s * 512 : (s + 1) * 512, :] = rows
        trans[s * 512 : (s + 1) * 512, :] = turned
        counts[s : s + 1, :] = count
    counts[2:8, :] = jnp.zeros((6, 512), f32)


def score_kernel(
    place, rows_in, pack2, pack3, rel_b, counts, known, trans, source,
    weight, g_trans, kept, given, known1, trans1, rows, source1
):
    core = place[0]
    for z in range(2):
        both = rows_in[:, z].reshape(2, 256, 128)
        rows[z * 256 : (z + 1) * 256, :] = jnp.concatenate([both[0], both[1]], axis=1)
    index = [known[s * 8 : s * 8 + 4, :] for s in range(2)]
    count = [counts[s : s + 1, :] for s in range(2)]
    stack = jnp.concatenate([rel_b[r] for r in range(8)], axis=1)
    for s, pack in enumerate((pack2, pack3)):
        one, away, turned, many = span_work(place[2], pack, stack)
        known1[s * 8 : (s + 1) * 8, :] = jnp.concatenate([one, one], axis=0)
        source1[s * 512 : (s + 1) * 512, :] = away
        trans1[s * 512 : (s + 1) * 512, :] = turned
        index.append(one)
        count.append(many)
    ids = row_ids(place[2], 256)
    for b in range(8):
        s = b // 2
        column = columns(index[s])[(b % 2) * 256 : (b % 2 + 1) * 256]
        span = slice(b * 256, (b + 1) * 256)
        turned = (trans, trans1)[b // 4][(b % 4) * 256 : (b % 4 + 1) * 256, :]
        score = dot(turned, rows[...], NT)
        sig = 1.0 / (1.0 + jnp.exp(-score))
        hit = column[:, 2:3] == ids
        part = jnp.where(hit, (count[s] + 1.0) * sig - 1.0, count[s] * sig).astype(bf16)
        weight[span, :] = part
        g_trans[span, :] = dot(part, rows[...]).astype(bf16)
    turned = g_trans[...].astype(f32).T
    kinds = jnp.concatenate([part[1:2] for part in index], axis=1)
    every = jnp.concatenate([source[...], source1[...]], axis=0)
    for r in range(8):
        wanted = r + 4 * core if r < 4 else r - 4 * core
        masked = jnp.where(kinds == wanted.astype(f32), turned, 0.0).astype(bf16)
        grad = dot(masked, every).astype(bf16)
        if r < 4:
            kept[r] = grad
        else:
            given[r - 4] = grad


def partner_kernel(weight, trans0, trans1, g_rows):
    turned = jnp.concatenate([t[...].astype(f32).T.astype(bf16) for t in (trans0, trans1)], axis=1)
    for z in range(2):
        g_rows[z] = dot(turned, weight[:, z * 256 : (z + 1) * 256]).T.astype(bf16)


def own_kernel(g_trans, known0, known1, rel_b, *owns):
    sub_ids = lax.broadcasted_iota(jnp.int32, (256, 512), 0).astype(f32)
    stack = rel_b[...].reshape(2048, 256)
    for s in range(4):
        index = (known0, known1)[s // 2][(s % 2) * 8 : (s % 2 + 1) * 8, :]
        grad = g_trans[s * 512 : (s + 1) * 512, :]
        kinds = columns(index[0:4])[:, 1:2]
        parts = [
            dot(by_relation(kinds[h : h + 128], grad[h : h + 128]), stack).astype(bf16)
            for h in range(0, 512, 128)
        ]
        hot = (index[0:1, :] == sub_ids).astype(f32).astype(bf16)
        mine = dot(hot, jnp.concatenate(parts, axis=0))
        owns[s][...] = mine.astype(owns[s].dtype)


def join_kernel(kept, came, out):
    for k in range(4):
        out[k] = (kept[k].astype(f32) + came[k].astype(f32)).astype(bf16)


def pieces_kernel(got, g_rows, out):
    for h in range(2):
        half = slice(h * 128, (h + 1) * 128)
        rel = got[0, :, half].astype(f32)
        for k in range(1, 4):
            rel = rel + got[k, :, half].astype(f32)
        for p, part in enumerate((g_rows[0, :, half].astype(f32), g_rows[1, :, half].astype(f32), rel)):
            tiles = part.reshape(32, 8, 128)
            for z in range(2):
                out[h * 32 : (h + 1) * 32, z, p] = tiles[:, z * 4 : (z + 1) * 4].astype(bf16)


def route_kernel(matching, mid, out):
    rel = [jnp.zeros((4, 128), f32), jnp.zeros((4, 128), f32)]
    for d in range(64):
        rel[d % 2] = rel[d % 2] + (mid[d, 0, 2].astype(f32) + mid[d, 1, 2].astype(f32))
    for d in range(64):
        target = matching[d]
        tail = jnp.where(target % 2 == 0, rel[0], rel[1]).astype(bf16)
        for z in range(2):
            out[target, z, 0] = (mid[d, 0, z].astype(f32) + mid[d, 1, z].astype(f32)).astype(bf16)
            out[target, z, 1] = tail


def whole(last, h, p):
    span = slice(h * 32, (h + 1) * 32)
    parts = [last[span, z, p].astype(f32) for z in range(2)]
    return jnp.concatenate(parts, axis=1).reshape(256, 128)


def rel_kernel(last, out):
    for h in range(2):
        part = whole(last, h, 1).astype(bf16)
        for k in range(4):
            out[k, :, h * 128 : (h + 1) * 128] = part


def to_row(column):
    return jnp.broadcast_to(column, (256, 128)).T[0:1]


def to_column(row):
    return jnp.broadcast_to(row, (128, 256)).T[:, 0:1]


def rows_kernel(emb, accum, own0, own1, own2, own3, last, new_emb, new_accum):
    grad = own0[...]
    for own in (own1, own2, own3):
        grad = grad + own[...].astype(f32)
    grad = grad + jnp.concatenate([whole(last, 0, 0), whole(last, 1, 0)], axis=1)
    total = to_column(accum[...]) + jnp.mean(grad * grad, axis=1, keepdims=True)
    new_emb[...] = emb[...] - grad * (learn_rate / jnp.sqrt(total))
    new_accum[...] = to_row(total)


def update_kernel(place, rel, accum, grads, *rest):
    if len(rest) == 6:
        core, (seen, held, new_rel, new_accum, block, sem) = 1 - place[0], rest
    else:
        core, (new_rel, new_accum, block, sem) = place[0], rest
    old = jnp.concatenate([accum[...], accum[...]], axis=0)
    column = jnp.where(core == 0, old[0:8], old[4:12]).T
    totals, copies = [], []
    for r in range(4):
        grad = grads[r].astype(f32)
        total = column[:, r : r + 1] + jnp.mean(grad * grad, axis=1, keepdims=True)
        block[r] = rel[4 * core + r] - grad * (learn_rate / jnp.sqrt(total))
        totals.append(total)
        copies.append(pltpu.make_async_copy(block.at[r], new_rel.at[4 * core + r], sem.at[r]))
        copies[r].start()
    rows = jnp.concatenate(totals + totals, axis=1).T
    if len(rest) == 6:
        first = jnp.concatenate([held[...], held[...]], axis=0)
        mixed = jnp.concatenate([rows[0:4], first[0:4]], axis=0)
        turned = jnp.concatenate([first[0:4], rows[0:4]], axis=0)
        new_accum[...] = jnp.where(core == 0, mixed, turned)
    else:
        new_accum[...] = rows
    for copy in copies:
        copy.wait()


def update_half(place, relations, rel_accum, grads, before=None):
    given = (place, relations, rel_accum, grads) + (before or ())
    specs = [SMEM, VMEM, VMEM, VMEM] + ([ANY, VMEM] if before else [])
    return pl.pallas_call(
        update_kernel,
        out_shape=(shape((8, 256, 256), f32), shape((8, 256), f32)),
        in_specs=specs,
        out_specs=(ANY, VMEM),
        scratch_shapes=[pltpu.VMEM((4, 256, 256), f32), pltpu.SemaphoreType.DMA((4,))],
        input_output_aliases={4: 0} if before else {},
        compiler_params=pltpu.CompilerParams(vmem_limit_bytes=8 * 1024 * 1024),
        cost_estimate=pl.CostEstimate(flops=0, bytes_accessed=3_000_000, transcendentals=0),
    )(*given)


def body(
    embeddings, row_accum, relations, rel_accum, matching, src_rows, dst_rows, rel_ids, neg_rows
):
    place = jnp.stack([lax.axis_index(name) for name in ("core", "zhi", "x")]).astype(jnp.int32)
    line = lambda v: v.reshape(1, 512)
    pieces, pack = call(
        first_kernel,
        (shape((64, 8, 128), bf16), shape((272, 256), bf16)),
        0,
        (embeddings, line(src_rows), line(rel_ids), line(dst_rows), line(neg_rows)),
        moved=800_000,
        far=(0, 1, 2, 3, 4),
        space=62,
        scratch=[
            pltpu.VMEM((256, 256), f32),
            pltpu.VMEM((4, 1, 512), jnp.int32),
            pltpu.SemaphoreType.DMA((5,)),
        ],
    )
    arrived = spread(pieces, DOM)
    rel_b = call(
        cast_kernel,
        shape((8, 256, 256), bf16),
        0,
        (relations,),
        moved=3_000_000,
        far=(0,),
        far_outs=(0,),
        scratch=[
            pltpu.VMEM((8, 256, 256), f32),
            pltpu.VMEM((8, 256, 256), bf16),
            pltpu.SemaphoreType.DMA((16,)),
        ],
        space=62,
    )
    packs = [pack] + [
        lax.ppermute(pack, "x", [(i, i ^ k) for i in range(4)]) for k in range(1, 4)
    ]
    packs[1], rel_b, arrived = lax.optimization_barrier((packs[1], rel_b, arrived))
    routed = call(take_kernel, shape((64, 2, 8, 128), bf16), 1, (matching, arrived), moved=400_000)
    rows_in = spread(routed.reshape(128, 8, 128), DOM_Z).reshape(64, 2, 8, 128)
    block = shape((1024, 256), bf16)
    known_shape = shape((16, 512), f32)
    counts, known0, trans0, source0 = call(
        trans_kernel,
        (shape((8, 512), f32), known_shape, block, block),
        1,
        (place, packs[0], packs[1], rel_b),
        flops=1_300_000_000,
        moved=3_000_000,
        space=16,
    )
    four = shape((4, 256, 256), bf16)
    weight, g_trans, kept, given, known1, trans1 = call(
        score_kernel,
        (shape((2048, 512), bf16), shape((2048, 256), bf16), four, four, known_shape, block),
        1,
        (place, rows_in, packs[2], packs[3], rel_b, counts, known0, trans0, source0),
        flops=4_500_000_000,
        moved=6_000_000,
        scratch=[pltpu.VMEM((512, 256), bf16), pltpu.VMEM((1024, 256), bf16)],
        space=28,
    )
    came = swap(given, "core")
    g_rows = call(
        partner_kernel,
        shape((2, 256, 256), bf16),
        0,
        (weight, trans0, trans1),
        flops=1_500_000_000,
        moved=4_000_000,
        space=16,
    )
    came, g_rows = lax.optimization_barrier((came, g_rows))
    got = spread(call(join_kernel, four, 0, (kept, came), moved=1_500_000), "x")
    one = shape((256, 256), bf16)
    owns = call(
        own_kernel,
        (shape((256, 256), f32), one, one, one),
        0,
        (g_trans, known0, known1, rel_b),
        flops=3_000_000_000,
        moved=4_000_000,
        space=16,
    )
    away = lambda part, k: lax.ppermute(part, "x", [(i, i ^ k) for i in range(4)])
    first = away(owns[1], 1)
    out = call(
        pieces_kernel, shape((64, 2, 3, 4, 128), bf16), 0, (got, g_rows), moved=2_000_000
    )
    mid = spread(out.reshape(128, 3, 4, 128), DOM_Z)
    first, *others, mid = lax.optimization_barrier((first, *owns[2:], mid))
    others = [away(part, k) for k, part in enumerate(others, 2)]
    routed_back = call(
        route_kernel,
        shape((64, 2, 2, 4, 128), bf16),
        1,
        (matching, mid.reshape(64, 2, 3, 4, 128)),
        moved=512_000,
    )
    last = spread(routed_back.reshape(128, 2, 4, 128), DOM_Z).reshape(64, 2, 2, 4, 128)
    *others, last = lax.optimization_barrier((*others, last))
    rel_four = spread(call(rel_kernel, four, 0, (last,), moved=512_000), "x")
    new_embeddings, new_row_accum = call(
        rows_kernel,
        (shape((256, 256), f32), shape((1, 256), f32)),
        0,
        (embeddings, row_accum.reshape(1, 256), owns[0], first, *others, last),
        flops=1_000_000,
        moved=1_000_000,
    )
    new_embeddings, rel_four = lax.optimization_barrier((new_embeddings, rel_four))
    rel_rest = swap(rel_four, "core")
    half = update_half(place, relations, rel_accum, rel_four)
    new_relations, new_rel_accum = update_half(place, relations, rel_accum, rel_rest, half)
    return new_embeddings, new_row_accum.reshape(256), new_relations, new_rel_accum


def solution(mesh):
    fine = Mesh(mesh.devices.reshape(4, 8, 2, 2, 4), AXES)
    placed = (
        P(AXES, None),
        P(AXES),
        P(),
        P(),
        P(),
        P(AXES),
        P(AXES),
        P(AXES),
        P(AXES, None),
    )
    return jax.shard_map(
        body,
        mesh=fine,
        in_specs=placed,
        out_specs=(P(AXES, None), P(AXES), P(), P()),
        check_vma=False,
    )
```

```python
import jax
import jax.numpy as jnp
from jax import lax
from jax.experimental import pallas as pl
from jax.experimental.pallas import tpu as pltpu
from jax.sharding import Mesh, PartitionSpec as P

learn_rate = 0.1
AXES = ("zlo", "y", "core", "zhi", "x")
DOM = ("zlo", "y", "core")
DOM_Z = DOM + ("zhi",)
bf16 = jnp.bfloat16
f32 = jnp.float32
VMEM = pl.BlockSpec(memory_space=pltpu.VMEM)
ANY = pl.BlockSpec(memory_space=pltpu.HBM)
SMEM = pl.BlockSpec(memory_space=pltpu.SMEM)
NN = (((1,), (0,)), ((), ()))
NT = (((1,), (1,)), ((), ()))


def shape(dims, dtype):
    return jax.ShapeDtypeStruct(dims, dtype)


def dot(a, b, dims=NN):
    return lax.dot_general(a, b, dims, preferred_element_type=f32)


def call(kernel, outs, scalars, args, flops=0, moved=0, scratch=(), space=8, far=(), far_outs=()):
    specs = [SMEM] * scalars + [ANY if k in far else VMEM for k in range(scalars, len(args))]
    many = isinstance(outs, tuple)
    return pl.pallas_call(
        kernel,
        out_shape=outs,
        in_specs=specs,
        out_specs=tuple(ANY if k in far_outs else VMEM for k in range(len(outs))) if many else (ANY if far_outs else VMEM),
        scratch_shapes=list(scratch),
        compiler_params=pltpu.CompilerParams(vmem_limit_bytes=space * 1024 * 1024),
        cost_estimate=pl.CostEstimate(flops=flops, bytes_accessed=moved, transcendentals=0),
    )(*args)


def swap(value, axis):
    return lax.ppermute(value, axis, [(0, 1), (1, 0)])


def spread(value, axis):
    return lax.all_to_all(value, axis, split_axis=0, concat_axis=0, tiled=True)


def first_kernel(emb, src, rel, dst, neg, pieces, pack, rows, index, sems):
    copies = [pltpu.make_async_copy(emb, rows, sems.at[0])]
    for k, part in enumerate((src, rel, dst, neg)):
        copies.append(pltpu.make_async_copy(part, index.at[k], sems.at[k + 1]))
    for copy in copies:
        copy.start()
    for copy in copies:
        copy.wait()
    wide = jnp.concatenate([index[k] for k in range(4)], axis=0)
    high = wide // 256
    low = (wide - high * 256).astype(f32)
    both = jnp.concatenate([high.astype(f32), low], axis=0)
    pack[256:272, :] = jnp.concatenate([both[:, :256], both[:, 256:]], axis=0).astype(bf16)
    pack[0:256, :] = rows[...].astype(bf16)
    for h in range(2):
        half = rows[:, h * 128 : (h + 1) * 128]
        pieces[h * 32 : (h + 1) * 32] = half.reshape(32, 8, 128).astype(bf16)


def take_kernel(matching, arrived, routed):
    for d in range(64):
        piece = arrived[matching[d]]
        routed[d, 0] = piece
        routed[d, 1] = piece


def indices(part):
    part = part.astype(f32)
    both = jnp.concatenate([part[0:8], part[8:16]], axis=1)
    return both[0:4] * 256.0 + both[4:8]


def columns(value):
    return jnp.concatenate([value, value], axis=0).T


def lane_ids(rows, width):
    return lax.broadcasted_iota(jnp.int32, (rows, width), 1)


def row_ids(x, rows):
    ids = lane_ids(rows, 512)
    return (ids + jnp.where(ids >= 256, 768, 0) + x * 256).astype(f32)


def by_relation(kinds, rows):
    wide = jnp.broadcast_to(kinds, rows.shape).astype(bf16)
    parts = [jnp.where(wide == bf16(r), rows, bf16(0)) for r in range(8)]
    return jnp.concatenate(parts, axis=1)


def cast_kernel(rel, rel_b, wide, narrow, sems):
    taken = [pltpu.make_async_copy(rel.at[r], wide.at[r], sems.at[r]) for r in range(8)]
    given = [pltpu.make_async_copy(narrow.at[r], rel_b.at[r], sems.at[8 + r]) for r in range(8)]
    for copy in taken:
        copy.start()
    for r in range(8):
        taken[r].wait()
        narrow[r] = wide[r].astype(bf16)
        given[r].start()
    for copy in given:
        copy.wait()


def span_work(x, pack, stack):
    index = indices(pack[256:272, :])
    column = columns(index)
    hot = (column[:, 0:1] == lane_ids(512, 256).astype(f32)).astype(f32).astype(bf16)
    rows = dot(hot, pack[0:256, :]).astype(bf16)
    turned = dot(by_relation(column[:, 1:2], rows), stack, NT).astype(bf16)
    hits = (column[:, 3:4] == row_ids(x, 512)).astype(f32)
    return index, rows, turned, jnp.sum(hits, axis=0, keepdims=True)


def trans_kernel(place, pack0, pack1, rel_b, counts, known, trans, source):
    stack = jnp.concatenate([rel_b[r] for r in range(8)], axis=1)
    for s, pack in enumerate((pack0, pack1)):
        index, rows, turned, count = span_work(place[2], pack, stack)
        known[s * 8 : (s + 1) * 8, :] = jnp.concatenate([index, index], axis=0)
        source[s * 512 : (s + 1) * 512, :] = rows
        trans[s * 512 : (s + 1) * 512, :] = turned
        counts[s : s + 1, :] = count
    counts[2:8, :] = jnp.zeros((6, 512), f32)


def score_kernel(
    place, rows_in, pack2, pack3, rel_b, counts, known, trans, source,
    weight, g_trans, kept, given, known1, trans1, rows, source1
):
    core = place[0]
    for z in range(2):
        both = rows_in[:, z].reshape(2, 256, 128)
        rows[z * 256 : (z + 1) * 256, :] = jnp.concatenate([both[0], both[1]], axis=1)
    index = [known[s * 8 : s * 8 + 4, :] for s in range(2)]
    count = [counts[s : s + 1, :] for s in range(2)]
    stack = jnp.concatenate([rel_b[r] for r in range(8)], axis=1)
    for s, pack in enumerate((pack2, pack3)):
        one, away, turned, many = span_work(place[2], pack, stack)
        known1[s * 8 : (s + 1) * 8, :] = jnp.concatenate([one, one], axis=0)
        source1[s * 512 : (s + 1) * 512, :] = away
        trans1[s * 512 : (s + 1) * 512, :] = turned
        index.append(one)
        count.append(many)
    ids = row_ids(place[2], 256)
    for b in range(8):
        s = b // 2
        column = columns(index[s])[(b % 2) * 256 : (b % 2 + 1) * 256]
        span = slice(b * 256, (b + 1) * 256)
        turned = (trans, trans1)[b // 4][(b % 4) * 256 : (b % 4 + 1) * 256, :]
        score = dot(turned, rows[...], NT)
        sig = 1.0 / (1.0 + jnp.exp(-score))
        hit = column[:, 2:3] == ids
        part = jnp.where(hit, (count[s] + 1.0) * sig - 1.0, count[s] * sig).astype(bf16)
        weight[span, :] = part
        g_trans[span, :] = dot(part, rows[...]).astype(bf16)
    turned = g_trans[...].astype(f32).T
    kinds = jnp.concatenate([part[1:2] for part in index], axis=1)
    every = jnp.concatenate([source[...], source1[...]], axis=0)
    for r in range(8):
        wanted = r + 4 * core if r < 4 else r - 4 * core
        masked = jnp.where(kinds == wanted.astype(f32), turned, 0.0).astype(bf16)
        grad = dot(masked, every).astype(bf16)
        if r < 4:
            kept[r] = grad
        else:
            given[r - 4] = grad


def partner_kernel(weight, trans0, trans1, g_rows):
    turned = jnp.concatenate([t[...].astype(f32).T.astype(bf16) for t in (trans0, trans1)], axis=1)
    for z in range(2):
        g_rows[z] = dot(turned, weight[:, z * 256 : (z + 1) * 256]).T.astype(bf16)


def own_kernel(g_trans, known0, known1, rel_b, *owns):
    sub_ids = lax.broadcasted_iota(jnp.int32, (256, 512), 0).astype(f32)
    stack = rel_b[...].reshape(2048, 256)
    for s in range(4):
        index = (known0, known1)[s // 2][(s % 2) * 8 : (s % 2 + 1) * 8, :]
        grad = g_trans[s * 512 : (s + 1) * 512, :]
        kinds = columns(index[0:4])[:, 1:2]
        parts = [
            dot(by_relation(kinds[h : h + 128], grad[h : h + 128]), stack).astype(bf16)
            for h in range(0, 512, 128)
        ]
        hot = (index[0:1, :] == sub_ids).astype(f32).astype(bf16)
        mine = dot(hot, jnp.concatenate(parts, axis=0))
        owns[s][...] = mine.astype(owns[s].dtype)


def join_kernel(place, kept, came, *outs):
    for k, out in enumerate(outs):
        target = place[2] ^ k
        out[...] = (kept[target].astype(f32) + came[target].astype(f32)).astype(bf16)


def pieces_kernel(got0, got1, got2, got3, g_rows, out):
    for h in range(2):
        half = slice(h * 128, (h + 1) * 128)
        rel = got0[:, half].astype(f32)
        for got in (got1, got2, got3):
            rel = rel + got[:, half].astype(f32)
        for p, part in enumerate((g_rows[0, :, half].astype(f32), g_rows[1, :, half].astype(f32), rel)):
            tiles = part.reshape(32, 8, 128)
            for z in range(2):
                out[h * 32 : (h + 1) * 32, z, p] = tiles[:, z * 4 : (z + 1) * 4].astype(bf16)


def route_kernel(matching, mid, out):
    rel = [jnp.zeros((4, 128), f32), jnp.zeros((4, 128), f32)]
    for d in range(64):
        rel[d % 2] = rel[d % 2] + (mid[d, 0, 2].astype(f32) + mid[d, 1, 2].astype(f32))
    for d in range(64):
        target = matching[d]
        tail = jnp.where(target % 2 == 0, rel[0], rel[1]).astype(bf16)
        for z in range(2):
            out[target, z, 0] = (mid[d, 0, z].astype(f32) + mid[d, 1, z].astype(f32)).astype(bf16)
            out[target, z, 1] = tail


def whole(last, h, p):
    span = slice(h * 32, (h + 1) * 32)
    parts = [last[span, z, p].astype(f32) for z in range(2)]
    return jnp.concatenate(parts, axis=1).reshape(256, 128)


def rel_kernel(last, out):
    for h in range(2):
        part = whole(last, h, 1).astype(bf16)
        for k in range(4):
            out[k, :, h * 128 : (h + 1) * 128] = part


def to_row(column):
    return jnp.broadcast_to(column, (256, 128)).T[0:1]


def to_column(row):
    return jnp.broadcast_to(row, (128, 256)).T[:, 0:1]


def rows_kernel(emb, accum, own0, own1, own2, own3, last, new_emb, new_accum):
    grad = own0[...]
    for own in (own1, own2, own3):
        grad = grad + own[...].astype(f32)
    grad = grad + jnp.concatenate([whole(last, 0, 0), whole(last, 1, 0)], axis=1)
    total = to_column(accum[...]) + jnp.mean(grad * grad, axis=1, keepdims=True)
    new_emb[...] = emb[...] - grad * (learn_rate / jnp.sqrt(total))
    new_accum[...] = to_row(total)


def update_kernel(place, rel, accum, grads, *rest):
    if len(rest) == 6:
        core, (seen, held, new_rel, new_accum, block, sem) = 1 - place[0], rest
    else:
        core, (new_rel, new_accum, block, sem) = place[0], rest
    old = jnp.concatenate([accum[...], accum[...]], axis=0)
    column = jnp.where(core == 0, old[0:8], old[4:12]).T
    totals, copies = [], []
    for r in range(4):
        grad = grads[r].astype(f32)
        total = column[:, r : r + 1] + jnp.mean(grad * grad, axis=1, keepdims=True)
        block[r] = rel[4 * core + r] - grad * (learn_rate / jnp.sqrt(total))
        totals.append(total)
        copies.append(pltpu.make_async_copy(block.at[r], new_rel.at[4 * core + r], sem.at[r]))
        copies[r].start()
    rows = jnp.concatenate(totals + totals, axis=1).T
    if len(rest) == 6:
        first = jnp.concatenate([held[...], held[...]], axis=0)
        mixed = jnp.concatenate([rows[0:4], first[0:4]], axis=0)
        turned = jnp.concatenate([first[0:4], rows[0:4]], axis=0)
        new_accum[...] = jnp.where(core == 0, mixed, turned)
    else:
        new_accum[...] = rows
    for copy in copies:
        copy.wait()


def update_half(place, relations, rel_accum, grads, before=None):
    given = (place, relations, rel_accum, grads) + (before or ())
    specs = [SMEM, VMEM, VMEM, VMEM] + ([ANY, VMEM] if before else [])
    return pl.pallas_call(
        update_kernel,
        out_shape=(shape((8, 256, 256), f32), shape((8, 256), f32)),
        in_specs=specs,
        out_specs=(ANY, VMEM),
        scratch_shapes=[pltpu.VMEM((4, 256, 256), f32), pltpu.SemaphoreType.DMA((4,))],
        input_output_aliases={4: 0} if before else {},
        compiler_params=pltpu.CompilerParams(vmem_limit_bytes=8 * 1024 * 1024),
        cost_estimate=pl.CostEstimate(flops=0, bytes_accessed=3_000_000, transcendentals=0),
    )(*given)


def body(
    embeddings, row_accum, relations, rel_accum, matching, src_rows, dst_rows, rel_ids, neg_rows
):
    place = jnp.stack([lax.axis_index(name) for name in ("core", "zhi", "x")]).astype(jnp.int32)
    line = lambda v: v.reshape(1, 512)
    pieces, pack = call(
        first_kernel,
        (shape((64, 8, 128), bf16), shape((272, 256), bf16)),
        0,
        (embeddings, line(src_rows), line(rel_ids), line(dst_rows), line(neg_rows)),
        moved=800_000,
        far=(0, 1, 2, 3, 4),
        space=62,
        scratch=[
            pltpu.VMEM((256, 256), f32),
            pltpu.VMEM((4, 1, 512), jnp.int32),
            pltpu.SemaphoreType.DMA((5,)),
        ],
    )
    arrived = spread(pieces, DOM)
    rel_b = call(
        cast_kernel,
        shape((8, 256, 256), bf16),
        0,
        (relations,),
        moved=3_000_000,
        far=(0,),
        far_outs=(0,),
        scratch=[
            pltpu.VMEM((8, 256, 256), f32),
            pltpu.VMEM((8, 256, 256), bf16),
            pltpu.SemaphoreType.DMA((16,)),
        ],
        space=62,
    )
    packs = [pack] + [
        lax.ppermute(pack, "x", [(i, i ^ k) for i in range(4)]) for k in range(1, 4)
    ]
    packs[1], rel_b, arrived = lax.optimization_barrier((packs[1], rel_b, arrived))
    routed = call(take_kernel, shape((64, 2, 8, 128), bf16), 1, (matching, arrived), moved=400_000)
    rows_in = spread(routed.reshape(128, 8, 128), DOM_Z).reshape(64, 2, 8, 128)
    block = shape((1024, 256), bf16)
    known_shape = shape((16, 512), f32)
    counts, known0, trans0, source0 = call(
        trans_kernel,
        (shape((8, 512), f32), known_shape, block, block),
        1,
        (place, packs[0], packs[1], rel_b),
        flops=1_300_000_000,
        moved=3_000_000,
        space=16,
    )
    four = shape((4, 256, 256), bf16)
    weight, g_trans, kept, given, known1, trans1 = call(
        score_kernel,
        (shape((2048, 512), bf16), shape((2048, 256), bf16), four, four, known_shape, block),
        1,
        (place, rows_in, packs[2], packs[3], rel_b, counts, known0, trans0, source0),
        flops=4_500_000_000,
        moved=6_000_000,
        scratch=[pltpu.VMEM((512, 256), bf16), pltpu.VMEM((1024, 256), bf16)],
        space=28,
    )
    came = swap(given, "core")
    g_rows = call(
        partner_kernel,
        shape((2, 256, 256), bf16),
        0,
        (weight, trans0, trans1),
        flops=1_500_000_000,
        moved=4_000_000,
        space=16,
    )
    came, g_rows = lax.optimization_barrier((came, g_rows))
    one = shape((256, 256), bf16)
    away = lambda part, k: lax.ppermute(part, "x", [(i, i ^ k) for i in range(4)])
    joined = call(join_kernel, (one,) * 4, 1, (place, kept, came), moved=1_500_000)
    got = list(joined[:1]) + [away(joined[k], k) for k in range(1, 4)]
    owns = call(
        own_kernel,
        (shape((256, 256), f32), one, one, one),
        0,
        (g_trans, known0, known1, rel_b),
        flops=3_000_000_000,
        moved=4_000_000,
        space=16,
    )
    first = away(owns[1], 1)
    out = call(
        pieces_kernel, shape((64, 2, 3, 4, 128), bf16), 0, (*got, g_rows), moved=2_000_000
    )
    mid = spread(out.reshape(128, 3, 4, 128), DOM_Z)
    first, *others, mid = lax.optimization_barrier((first, *owns[2:], mid))
    others = [away(part, k) for k, part in enumerate(others, 2)]
    routed_back = call(
        route_kernel,
        shape((64, 2, 2, 4, 128), bf16),
        1,
        (matching, mid.reshape(64, 2, 3, 4, 128)),
        moved=512_000,
    )
    last = spread(routed_back.reshape(128, 2, 4, 128), DOM_Z).reshape(64, 2, 2, 4, 128)
    *others, last = lax.optimization_barrier((*others, last))
    rel_four = spread(call(rel_kernel, four, 0, (last,), moved=512_000), "x")
    new_embeddings, new_row_accum = call(
        rows_kernel,
        (shape((256, 256), f32), shape((1, 256), f32)),
        0,
        (embeddings, row_accum.reshape(1, 256), owns[0], first, *others, last),
        flops=1_000_000,
        moved=1_000_000,
    )
    new_embeddings, rel_four = lax.optimization_barrier((new_embeddings, rel_four))
    rel_rest = swap(rel_four, "core")
    half = update_half(place, relations, rel_accum, rel_four)
    new_relations, new_rel_accum = update_half(place, relations, rel_accum, rel_rest, half)
    return new_embeddings, new_row_accum.reshape(256), new_relations, new_rel_accum


def solution(mesh):
    fine = Mesh(mesh.devices.reshape(4, 8, 2, 2, 4), AXES)
    placed = (
        P(AXES, None),
        P(AXES),
        P(),
        P(),
        P(),
        P(AXES),
        P(AXES),
        P(AXES),
        P(AXES, None),
    )
    return jax.shard_map(
        body,
        mesh=fine,
        in_specs=placed,
        out_specs=(P(AXES, None), P(AXES), P(), P()),
        check_vma=False,
    )
```

```python
import jax
import jax.numpy as jnp
from jax import lax
from jax.experimental import pallas as pl
from jax.experimental.pallas import tpu as pltpu
from jax.sharding import Mesh, PartitionSpec as P

learn_rate = 0.1
AXES = ("zlo", "y", "core", "zhi", "x")
DOM = ("zlo", "y", "core")
DOM_Z = DOM + ("zhi",)
bf16 = jnp.bfloat16
f32 = jnp.float32
VMEM = pl.BlockSpec(memory_space=pltpu.VMEM)
ANY = pl.BlockSpec(memory_space=pltpu.HBM)
SMEM = pl.BlockSpec(memory_space=pltpu.SMEM)
NN = (((1,), (0,)), ((), ()))
NT = (((1,), (1,)), ((), ()))


def shape(dims, dtype):
    return jax.ShapeDtypeStruct(dims, dtype)


def dot(a, b, dims=NN):
    return lax.dot_general(a, b, dims, preferred_element_type=f32)


def call(kernel, outs, scalars, args, flops=0, moved=0, scratch=(), space=8, far=(), far_outs=()):
    specs = [SMEM] * scalars + [ANY if k in far else VMEM for k in range(scalars, len(args))]
    many = isinstance(outs, tuple)
    return pl.pallas_call(
        kernel,
        out_shape=outs,
        in_specs=specs,
        out_specs=tuple(ANY if k in far_outs else VMEM for k in range(len(outs))) if many else (ANY if far_outs else VMEM),
        scratch_shapes=list(scratch),
        compiler_params=pltpu.CompilerParams(vmem_limit_bytes=space * 1024 * 1024),
        cost_estimate=pl.CostEstimate(flops=flops, bytes_accessed=moved, transcendentals=0),
    )(*args)


def swap(value, axis):
    return lax.ppermute(value, axis, [(0, 1), (1, 0)])


def spread(value, axis):
    return lax.all_to_all(value, axis, split_axis=0, concat_axis=0, tiled=True)


def copy_out(source, target, sem):
    copy = pltpu.make_async_copy(source, target, sem)
    copy.start()
    return copy


def first_kernel(emb, src, rel, dst, neg, pieces_out, pack_out, rows, index, pieces, pack, sems):
    halves = [
        copy_out(emb.at[pl.ds(k * 128, 128), :], rows.at[pl.ds(k * 128, 128), :], sems.at[k])
        for k in range(2)
    ]
    parts = [copy_out(part, index.at[k], sems.at[2 + k]) for k, part in enumerate((src, rel, dst, neg))]
    sent = []
    for k in range(2):
        halves[k].wait()
        block = rows[k * 128 : (k + 1) * 128, :]
        for h in range(2):
            span = slice(h * 32 + k * 16, h * 32 + (k + 1) * 16)
            pieces[span] = block[:, h * 128 : (h + 1) * 128].reshape(16, 8, 128).astype(bf16)
            place = pl.ds(h * 32 + k * 16, 16)
            sent.append(copy_out(pieces.at[place], pieces_out.at[place], sems.at[6 + 2 * k + h]))
        pack[k * 128 : (k + 1) * 128, :] = block.astype(bf16)
    for part in parts:
        part.wait()
    wide = jnp.concatenate([index[k] for k in range(4)], axis=0)
    high = wide // 256
    low = (wide - high * 256).astype(f32)
    both = jnp.concatenate([high.astype(f32), low], axis=0)
    pack[256:272, :] = jnp.concatenate([both[:, :256], both[:, 256:]], axis=0).astype(bf16)
    sent.append(copy_out(pack, pack_out, sems.at[10]))
    for copy in sent:
        copy.wait()


def take_kernel(matching, arrived, out, routed, sems):
    sent = []
    for k in range(4):
        for d in range(k * 16, (k + 1) * 16):
            piece = arrived[matching[d]]
            routed[d, 0] = piece
            routed[d, 1] = piece
        span = pl.ds(k * 16, 16)
        sent.append(copy_out(routed.at[span], out.at[span], sems.at[k]))
    for copy in sent:
        copy.wait()


def indices(part):
    part = part.astype(f32)
    both = jnp.concatenate([part[0:8], part[8:16]], axis=1)
    return both[0:4] * 256.0 + both[4:8]


def columns(value):
    return jnp.concatenate([value, value], axis=0).T


def lane_ids(rows, width):
    return lax.broadcasted_iota(jnp.int32, (rows, width), 1)


def row_ids(x, rows):
    ids = lane_ids(rows, 512)
    return (ids + jnp.where(ids >= 256, 768, 0) + x * 256).astype(f32)


def by_relation(kinds, rows):
    wide = jnp.broadcast_to(kinds, rows.shape).astype(bf16)
    parts = [jnp.where(wide == bf16(r), rows, bf16(0)) for r in range(8)]
    return jnp.concatenate(parts, axis=1)


def cast_kernel(rel, rel_b, wide, narrow, sems):
    taken = [pltpu.make_async_copy(rel.at[r], wide.at[r], sems.at[r]) for r in range(8)]
    given = [pltpu.make_async_copy(narrow.at[r], rel_b.at[r], sems.at[8 + r]) for r in range(8)]
    for copy in taken:
        copy.start()
    for r in range(8):
        taken[r].wait()
        narrow[r] = wide[r].astype(bf16)
        given[r].start()
    for copy in given:
        copy.wait()


def span_work(x, pack, stack):
    index = indices(pack[256:272, :])
    column = columns(index)
    hot = (column[:, 0:1] == lane_ids(512, 256).astype(f32)).astype(f32).astype(bf16)
    rows = dot(hot, pack[0:256, :]).astype(bf16)
    turned = dot(by_relation(column[:, 1:2], rows), stack, NT).astype(bf16)
    hits = (column[:, 3:4] == row_ids(x, 512)).astype(f32)
    return index, rows, turned, jnp.sum(hits, axis=0, keepdims=True)


def trans_kernel(place, pack0, pack1, rel_b, counts, known, trans, source):
    stack = jnp.concatenate([rel_b[r] for r in range(8)], axis=1)
    for s, pack in enumerate((pack0, pack1)):
        index, rows, turned, count = span_work(place[2], pack, stack)
        known[s * 8 : (s + 1) * 8, :] = jnp.concatenate([index, index], axis=0)
        source[s * 512 : (s + 1) * 512, :] = rows
        trans[s * 512 : (s + 1) * 512, :] = turned
        counts[s : s + 1, :] = count
    counts[2:8, :] = jnp.zeros((6, 512), f32)


def score_kernel(
    place, rows_in, pack2, pack3, rel_b, counts, known, trans, source,
    weight, g_trans, kept, given, known1, trans1, rows, source1
):
    core = place[0]
    for z in range(2):
        both = rows_in[:, z].reshape(2, 256, 128)
        rows[z * 256 : (z + 1) * 256, :] = jnp.concatenate([both[0], both[1]], axis=1)
    index = [known[s * 8 : s * 8 + 4, :] for s in range(2)]
    count = [counts[s : s + 1, :] for s in range(2)]
    stack = jnp.concatenate([rel_b[r] for r in range(8)], axis=1)
    for s, pack in enumerate((pack2, pack3)):
        one, away, turned, many = span_work(place[2], pack, stack)
        known1[s * 8 : (s + 1) * 8, :] = jnp.concatenate([one, one], axis=0)
        source1[s * 512 : (s + 1) * 512, :] = away
        trans1[s * 512 : (s + 1) * 512, :] = turned
        index.append(one)
        count.append(many)
    ids = row_ids(place[2], 256)
    for b in range(8):
        s = b // 2
        column = columns(index[s])[(b % 2) * 256 : (b % 2 + 1) * 256]
        span = slice(b * 256, (b + 1) * 256)
        turned = (trans, trans1)[b // 4][(b % 4) * 256 : (b % 4 + 1) * 256, :]
        score = dot(turned, rows[...], NT)
        sig = 1.0 / (1.0 + jnp.exp(-score))
        hit = column[:, 2:3] == ids
        part = jnp.where(hit, (count[s] + 1.0) * sig - 1.0, count[s] * sig).astype(bf16)
        weight[span, :] = part
        g_trans[span, :] = dot(part, rows[...]).astype(bf16)
    turned = g_trans[...].astype(f32).T
    kinds = jnp.concatenate([part[1:2] for part in index], axis=1)
    every = jnp.concatenate([source[...], source1[...]], axis=0)
    for r in range(8):
        wanted = r + 4 * core if r < 4 else r - 4 * core
        masked = jnp.where(kinds == wanted.astype(f32), turned, 0.0).astype(bf16)
        grad = dot(masked, every).astype(bf16)
        if r < 4:
            kept[r] = grad
        else:
            given[r - 4] = grad


def partner_kernel(weight, trans0, trans1, g_rows):
    turned = jnp.concatenate([t[...].astype(f32).T.astype(bf16) for t in (trans0, trans1)], axis=1)
    for z in range(2):
        g_rows[z] = dot(turned, weight[:, z * 256 : (z + 1) * 256]).T.astype(bf16)


def own_kernel(g_trans, known0, known1, rel_b, *owns):
    sub_ids = lax.broadcasted_iota(jnp.int32, (256, 512), 0).astype(f32)
    stack = rel_b[...].reshape(2048, 256)
    for s in range(4):
        index = (known0, known1)[s // 2][(s % 2) * 8 : (s % 2 + 1) * 8, :]
        grad = g_trans[s * 512 : (s + 1) * 512, :]
        kinds = columns(index[0:4])[:, 1:2]
        parts = [
            dot(by_relation(kinds[h : h + 128], grad[h : h + 128]), stack).astype(bf16)
            for h in range(0, 512, 128)
        ]
        hot = (index[0:1, :] == sub_ids).astype(f32).astype(bf16)
        mine = dot(hot, jnp.concatenate(parts, axis=0))
        owns[s][...] = mine.astype(owns[s].dtype)


def join_kernel(kept, came, out):
    for k in range(4):
        out[k] = (kept[k].astype(f32) + came[k].astype(f32)).astype(bf16)


def pieces_kernel(got, g_rows, out, tiles_out, sems):
    sent = []
    for h in range(2):
        half = slice(h * 128, (h + 1) * 128)
        rel = got[0, :, half].astype(f32)
        for k in range(1, 4):
            rel = rel + got[k, :, half].astype(f32)
        for p, part in enumerate((g_rows[0, :, half].astype(f32), g_rows[1, :, half].astype(f32), rel)):
            tiles = part.reshape(32, 8, 128)
            for z in range(2):
                tiles_out[h * 32 : (h + 1) * 32, z, p] = tiles[:, z * 4 : (z + 1) * 4].astype(bf16)
        span = pl.ds(h * 32, 32)
        sent.append(copy_out(tiles_out.at[span], out.at[span], sems.at[h]))
    for copy in sent:
        copy.wait()


def route_kernel(matching, mid, out):
    parts = mid[:, :, 2].astype(f32).reshape(32, 2, 2, 4, 128)
    for c in range(2):
        tail = jnp.sum(jnp.sum(parts[:, c], axis=1), axis=0).astype(bf16)
        for d in range(c, 64, 2):
            for z in range(2):
                out[d, z, 1] = tail
    rows = (mid[:, 0, 0:2].astype(f32) + mid[:, 1, 0:2].astype(f32)).astype(bf16)
    for d in range(64):
        target = matching[d]
        for z in range(2):
            out[target, z, 0] = rows[d, z]


def whole(last, h, p):
    span = slice(h * 32, (h + 1) * 32)
    parts = [last[span, z, p].astype(f32) for z in range(2)]
    return jnp.concatenate(parts, axis=1).reshape(256, 128)


def rel_kernel(last, out, held, sems):
    for h in range(2):
        held[:, h * 128 : (h + 1) * 128] = whole(last, h, 1).astype(bf16)
    for copy in [copy_out(held, out.at[k], sems.at[k]) for k in range(4)]:
        copy.wait()


def to_row(column):
    return jnp.broadcast_to(column, (256, 128)).T[0:1]


def to_column(row):
    return jnp.broadcast_to(row, (128, 256)).T[:, 0:1]


def rows_kernel(emb, accum, own0, own1, own2, own3, last, new_emb, new_accum):
    grad = own0[...]
    for own in (own1, own2, own3):
        grad = grad + own[...].astype(f32)
    grad = grad + jnp.concatenate([whole(last, 0, 0), whole(last, 1, 0)], axis=1)
    total = to_column(accum[...]) + jnp.mean(grad * grad, axis=1, keepdims=True)
    new_emb[...] = emb[...] - grad * (learn_rate / jnp.sqrt(total))
    new_accum[...] = to_row(total)


def update_kernel(place, rel, accum, grads, *rest):
    if len(rest) == 6:
        core, (seen, held, new_rel, new_accum, block, sem) = 1 - place[0], rest
    else:
        core, (new_rel, new_accum, block, sem) = place[0], rest
    old = jnp.concatenate([accum[...], accum[...]], axis=0)
    column = jnp.where(core == 0, old[0:8], old[4:12]).T
    totals, copies = [], []
    for r in range(4):
        grad = grads[r].astype(f32)
        total = column[:, r : r + 1] + jnp.mean(grad * grad, axis=1, keepdims=True)
        block[r] = rel[4 * core + r] - grad * (learn_rate / jnp.sqrt(total))
        totals.append(total)
        copies.append(pltpu.make_async_copy(block.at[r], new_rel.at[4 * core + r], sem.at[r]))
        copies[r].start()
    rows = jnp.concatenate(totals + totals, axis=1).T
    if len(rest) == 6:
        first = jnp.concatenate([held[...], held[...]], axis=0)
        mixed = jnp.concatenate([rows[0:4], first[0:4]], axis=0)
        turned = jnp.concatenate([first[0:4], rows[0:4]], axis=0)
        new_accum[...] = jnp.where(core == 0, mixed, turned)
    else:
        new_accum[...] = rows
    for copy in copies:
        copy.wait()


def update_half(place, relations, rel_accum, grads, before=None):
    given = (place, relations, rel_accum, grads) + (before or ())
    specs = [SMEM, VMEM, VMEM, VMEM] + ([ANY, VMEM] if before else [])
    return pl.pallas_call(
        update_kernel,
        out_shape=(shape((8, 256, 256), f32), shape((8, 256), f32)),
        in_specs=specs,
        out_specs=(ANY, VMEM),
        scratch_shapes=[pltpu.VMEM((4, 256, 256), f32), pltpu.SemaphoreType.DMA((4,))],
        input_output_aliases={4: 0} if before else {},
        compiler_params=pltpu.CompilerParams(vmem_limit_bytes=8 * 1024 * 1024),
        cost_estimate=pl.CostEstimate(flops=0, bytes_accessed=3_000_000, transcendentals=0),
    )(*given)


def body(
    embeddings, row_accum, relations, rel_accum, matching, src_rows, dst_rows, rel_ids, neg_rows
):
    place = jnp.stack([lax.axis_index(name) for name in ("core", "zhi", "x")]).astype(jnp.int32)
    line = lambda v: v.reshape(1, 512)
    pieces, pack = call(
        first_kernel,
        (shape((64, 8, 128), bf16), shape((272, 256), bf16)),
        0,
        (embeddings, line(src_rows), line(rel_ids), line(dst_rows), line(neg_rows)),
        moved=800_000,
        far=(0, 1, 2, 3, 4),
        far_outs=(0, 1),
        space=62,
        scratch=[
            pltpu.VMEM((256, 256), f32),
            pltpu.VMEM((4, 1, 512), jnp.int32),
            pltpu.VMEM((64, 8, 128), bf16),
            pltpu.VMEM((272, 256), bf16),
            pltpu.SemaphoreType.DMA((11,)),
        ],
    )
    arrived = spread(pieces, DOM)
    rel_b = call(
        cast_kernel,
        shape((8, 256, 256), bf16),
        0,
        (relations,),
        moved=3_000_000,
        far=(0,),
        far_outs=(0,),
        scratch=[
            pltpu.VMEM((8, 256, 256), f32),
            pltpu.VMEM((8, 256, 256), bf16),
            pltpu.SemaphoreType.DMA((16,)),
        ],
        space=62,
    )
    packs = [pack] + [
        lax.ppermute(pack, "x", [(i, i ^ k) for i in range(4)]) for k in range(1, 4)
    ]
    packs[1], rel_b, arrived = lax.optimization_barrier((packs[1], rel_b, arrived))
    routed = call(
        take_kernel,
        shape((64, 2, 8, 128), bf16),
        1,
        (matching, arrived),
        moved=400_000,
        far_outs=(0,),
        scratch=[pltpu.VMEM((64, 2, 8, 128), bf16), pltpu.SemaphoreType.DMA((4,))],
    )
    rows_in = spread(routed.reshape(128, 8, 128), DOM_Z).reshape(64, 2, 8, 128)
    block = shape((1024, 256), bf16)
    known_shape = shape((16, 512), f32)
    counts, known0, trans0, source0 = call(
        trans_kernel,
        (shape((8, 512), f32), known_shape, block, block),
        1,
        (place, packs[0], packs[1], rel_b),
        flops=1_300_000_000,
        moved=3_000_000,
        space=16,
    )
    four = shape((4, 256, 256), bf16)
    weight, g_trans, kept, given, known1, trans1 = call(
        score_kernel,
        (shape((2048, 512), bf16), shape((2048, 256), bf16), four, four, known_shape, block),
        1,
        (place, rows_in, packs[2], packs[3], rel_b, counts, known0, trans0, source0),
        flops=4_500_000_000,
        moved=6_000_000,
        scratch=[pltpu.VMEM((512, 256), bf16), pltpu.VMEM((1024, 256), bf16)],
        space=28,
    )
    came = swap(given, "core")
    g_rows = call(
        partner_kernel,
        shape((2, 256, 256), bf16),
        0,
        (weight, trans0, trans1),
        flops=1_500_000_000,
        moved=4_000_000,
        space=16,
    )
    came, g_rows = lax.optimization_barrier((came, g_rows))
    got = spread(call(join_kernel, four, 0, (kept, came), moved=1_500_000), "x")
    one = shape((256, 256), bf16)
    owns = call(
        own_kernel,
        (shape((256, 256), f32), one, one, one),
        0,
        (g_trans, known0, known1, rel_b),
        flops=3_000_000_000,
        moved=4_000_000,
        space=16,
    )
    away = lambda part, k: lax.ppermute(part, "x", [(i, i ^ k) for i in range(4)])
    first = away(owns[1], 1)
    out = call(
        pieces_kernel,
        shape((64, 2, 3, 4, 128), bf16),
        0,
        (got, g_rows),
        moved=2_000_000,
        far_outs=(0,),
        scratch=[pltpu.VMEM((64, 2, 3, 4, 128), bf16), pltpu.SemaphoreType.DMA((2,))],
    )
    mid = spread(out.reshape(128, 3, 4, 128), DOM_Z)
    first, *others, mid = lax.optimization_barrier((first, *owns[2:], mid))
    others = [away(part, k) for k, part in enumerate(others, 2)]
    routed_back = call(
        route_kernel,
        shape((64, 2, 2, 4, 128), bf16),
        1,
        (matching, mid.reshape(64, 2, 3, 4, 128)),
        moved=512_000,
    )
    last = spread(routed_back.reshape(128, 2, 4, 128), DOM_Z).reshape(64, 2, 2, 4, 128)
    *others, last = lax.optimization_barrier((*others, last))
    rel_four = spread(call(
            rel_kernel,
            four,
            0,
            (last,),
            moved=512_000,
            far_outs=(0,),
            scratch=[pltpu.VMEM((256, 256), bf16), pltpu.SemaphoreType.DMA((4,))],
        ),
        "x",
    )
    new_embeddings, new_row_accum = call(
        rows_kernel,
        (shape((256, 256), f32), shape((1, 256), f32)),
        0,
        (embeddings, row_accum.reshape(1, 256), owns[0], first, *others, last),
        flops=1_000_000,
        moved=1_000_000,
    )
    new_embeddings, rel_four = lax.optimization_barrier((new_embeddings, rel_four))
    rel_rest = swap(rel_four, "core")
    half = update_half(place, relations, rel_accum, rel_four)
    new_relations, new_rel_accum = update_half(place, relations, rel_accum, rel_rest, half)
    return new_embeddings, new_row_accum.reshape(256), new_relations, new_rel_accum


def solution(mesh):
    fine = Mesh(mesh.devices.reshape(4, 8, 2, 2, 4), AXES)
    placed = (
        P(AXES, None),
        P(AXES),
        P(),
        P(),
        P(),
        P(AXES),
        P(AXES),
        P(AXES),
        P(AXES, None),
    )
    return jax.shard_map(
        body,
        mesh=fine,
        in_specs=placed,
        out_specs=(P(AXES, None), P(AXES), P(), P()),
        check_vma=False,
    )
```

```python
import jax
import jax.numpy as jnp
from jax import lax
from jax.experimental import pallas as pl
from jax.experimental.pallas import tpu as pltpu
from jax.sharding import Mesh, PartitionSpec as P

learn_rate = 0.1
AXES = ("zlo", "y", "core", "zhi", "x")
DOM = ("zlo", "y", "core")
DOM_Z = DOM + ("zhi",)
bf16 = jnp.bfloat16
f32 = jnp.float32
VMEM = pl.BlockSpec(memory_space=pltpu.VMEM)
ANY = pl.BlockSpec(memory_space=pltpu.HBM)
SMEM = pl.BlockSpec(memory_space=pltpu.SMEM)
NN = (((1,), (0,)), ((), ()))
NT = (((1,), (1,)), ((), ()))


def shape(dims, dtype):
    return jax.ShapeDtypeStruct(dims, dtype)


def dot(a, b, dims=NN):
    return lax.dot_general(a, b, dims, preferred_element_type=f32)


def call(kernel, outs, scalars, args, flops=0, moved=0, scratch=(), space=8, far=(), far_outs=()):
    specs = [SMEM] * scalars + [ANY if k in far else VMEM for k in range(scalars, len(args))]
    many = isinstance(outs, tuple)
    return pl.pallas_call(
        kernel,
        out_shape=outs,
        in_specs=specs,
        out_specs=tuple(ANY if k in far_outs else VMEM for k in range(len(outs))) if many else (ANY if far_outs else VMEM),
        scratch_shapes=list(scratch),
        compiler_params=pltpu.CompilerParams(vmem_limit_bytes=space * 1024 * 1024),
        cost_estimate=pl.CostEstimate(flops=flops, bytes_accessed=moved, transcendentals=0),
    )(*args)


def swap(value, axis):
    return lax.ppermute(value, axis, [(0, 1), (1, 0)])


def spread(value, axis):
    return lax.all_to_all(value, axis, split_axis=0, concat_axis=0, tiled=True)


def first_kernel(emb, src, rel, dst, neg, pieces, pack, rows, index, sems):
    copies = [pltpu.make_async_copy(emb, rows, sems.at[0])]
    for k, part in enumerate((src, rel, dst, neg)):
        copies.append(pltpu.make_async_copy(part, index.at[k], sems.at[k + 1]))
    for copy in copies:
        copy.start()
    for copy in copies:
        copy.wait()
    wide = jnp.concatenate([index[k] for k in range(4)], axis=0)
    high = wide // 256
    low = (wide - high * 256).astype(f32)
    both = jnp.concatenate([high.astype(f32), low], axis=0)
    pack[256:272, :] = jnp.concatenate([both[:, :256], both[:, 256:]], axis=0).astype(bf16)
    pack[0:256, :] = rows[...].astype(bf16)
    for h in range(2):
        half = rows[:, h * 128 : (h + 1) * 128]
        pieces[h * 32 : (h + 1) * 32] = half.reshape(32, 8, 128).astype(bf16)


def take_kernel(matching, arrived, routed):
    for d in range(64):
        piece = arrived[matching[d]]
        routed[d, 0] = piece
        routed[d, 1] = piece


def indices(part):
    part = part.astype(f32)
    both = jnp.concatenate([part[0:8], part[8:16]], axis=1)
    return both[0:4] * 256.0 + both[4:8]


def columns(value):
    return jnp.concatenate([value, value], axis=0).T


def lane_ids(rows, width):
    return lax.broadcasted_iota(jnp.int32, (rows, width), 1)


def row_ids(x, rows):
    ids = lane_ids(rows, 512)
    return (ids + jnp.where(ids >= 256, 768, 0) + x * 256).astype(f32)


def by_relation(kinds, rows):
    wide = jnp.broadcast_to(kinds, rows.shape).astype(bf16)
    parts = [jnp.where(wide == bf16(r), rows, bf16(0)) for r in range(8)]
    return jnp.concatenate(parts, axis=1)


def cast_kernel(rel, rel_b, wide, narrow, sems):
    taken = [pltpu.make_async_copy(rel.at[r], wide.at[r], sems.at[r]) for r in range(8)]
    given = [pltpu.make_async_copy(narrow.at[r], rel_b.at[r], sems.at[8 + r]) for r in range(8)]
    for copy in taken:
        copy.start()
    for r in range(8):
        taken[r].wait()
        narrow[r] = wide[r].astype(bf16)
        given[r].start()
    for copy in given:
        copy.wait()


def span_work(x, pack, stack):
    index = indices(pack[256:272, :])
    column = columns(index)
    hot = (column[:, 0:1] == lane_ids(512, 256).astype(f32)).astype(f32).astype(bf16)
    rows = dot(hot, pack[0:256, :]).astype(bf16)
    turned = dot(by_relation(column[:, 1:2], rows), stack, NT).astype(bf16)
    hits = (column[:, 3:4] == row_ids(x, 512)).astype(f32)
    return index, rows, turned, jnp.sum(hits, axis=0, keepdims=True)


def trans_kernel(place, pack0, pack1, rel_b, counts, known, trans, source):
    stack = jnp.concatenate([rel_b[r] for r in range(8)], axis=1)
    for s, pack in enumerate((pack0, pack1)):
        index, rows, turned, count = span_work(place[2], pack, stack)
        known[s * 8 : (s + 1) * 8, :] = jnp.concatenate([index, index], axis=0)
        source[s * 512 : (s + 1) * 512, :] = rows
        trans[s * 512 : (s + 1) * 512, :] = turned
        counts[s : s + 1, :] = count
    counts[2:8, :] = jnp.zeros((6, 512), f32)


def score_kernel(
    place, rows_in, pack2, pack3, rel_b, counts, known, trans, source,
    weight, g_trans, given, known1, trans1, source1, rows
):
    for z in range(2):
        both = rows_in[:, z].reshape(2, 256, 128)
        rows[z * 256 : (z + 1) * 256, :] = jnp.concatenate([both[0], both[1]], axis=1)
    index = [known[s * 8 : s * 8 + 4, :] for s in range(2)]
    count = [counts[s : s + 1, :] for s in range(2)]
    stack = jnp.concatenate([rel_b[r] for r in range(8)], axis=1)
    for s, pack in enumerate((pack2, pack3)):
        one, away, turned, many = span_work(place[2], pack, stack)
        known1[s * 8 : (s + 1) * 8, :] = jnp.concatenate([one, one], axis=0)
        source1[s * 512 : (s + 1) * 512, :] = away
        trans1[s * 512 : (s + 1) * 512, :] = turned
        index.append(one)
        count.append(many)
    ids = row_ids(place[2], 256)
    for b in range(8):
        s = b // 2
        column = columns(index[s])[(b % 2) * 256 : (b % 2 + 1) * 256]
        span = slice(b * 256, (b + 1) * 256)
        turned = (trans, trans1)[b // 4][(b % 4) * 256 : (b % 4 + 1) * 256, :]
        score = dot(turned, rows[...], NT)
        sig = 1.0 / (1.0 + jnp.exp(-score))
        hit = column[:, 2:3] == ids
        part = jnp.where(hit, (count[s] + 1.0) * sig - 1.0, count[s] * sig).astype(bf16)
        weight[span, :] = part
        g_trans[span, :] = dot(part, rows[...]).astype(bf16)
    relation_part(1 - place[0], g_trans, index, source, source1, given)


def relation_part(core, g_trans, index, source0, source1, out):
    turned = g_trans[...].astype(f32).T
    kinds = jnp.concatenate([part[1:2] for part in index], axis=1)
    every = jnp.concatenate([source0[...], source1[...]], axis=0)
    for r in range(4):
        masked = jnp.where(kinds == (r + 4 * core).astype(f32), turned, 0.0).astype(bf16)
        out[r] = dot(masked, every).astype(bf16)


def partner_kernel(
    place, weight, trans0, trans1, g_trans, known0, known1, source0, source1, g_rows, kept
):
    turned = jnp.concatenate([t[...].astype(f32).T.astype(bf16) for t in (trans0, trans1)], axis=1)
    for z in range(2):
        g_rows[z] = dot(turned, weight[:, z * 256 : (z + 1) * 256]).T.astype(bf16)
    index = [known[s * 8 : s * 8 + 4, :] for known in (known0, known1) for s in range(2)]
    relation_part(place[0], g_trans, index, source0, source1, kept)


def own_kernel(g_trans, known0, known1, rel_b, *owns):
    sub_ids = lax.broadcasted_iota(jnp.int32, (256, 512), 0).astype(f32)
    stack = rel_b[...].reshape(2048, 256)
    for s in range(4):
        index = (known0, known1)[s // 2][(s % 2) * 8 : (s % 2 + 1) * 8, :]
        grad = g_trans[s * 512 : (s + 1) * 512, :]
        kinds = columns(index[0:4])[:, 1:2]
        parts = [
            dot(by_relation(kinds[h : h + 128], grad[h : h + 128]), stack).astype(bf16)
            for h in range(0, 512, 128)
        ]
        hot = (index[0:1, :] == sub_ids).astype(f32).astype(bf16)
        mine = dot(hot, jnp.concatenate(parts, axis=0))
        owns[s][...] = mine.astype(owns[s].dtype)


def join_kernel(kept, came, out):
    for k in range(4):
        out[k] = (kept[k].astype(f32) + came[k].astype(f32)).astype(bf16)


def pieces_kernel(got, g_rows, out):
    for h in range(2):
        half = slice(h * 128, (h + 1) * 128)
        rel = got[0, :, half].astype(f32)
        for k in range(1, 4):
            rel = rel + got[k, :, half].astype(f32)
        for p, part in enumerate((g_rows[0, :, half].astype(f32), g_rows[1, :, half].astype(f32), rel)):
            tiles = part.reshape(32, 8, 128)
            for z in range(2):
                out[h * 32 : (h + 1) * 32, z, p] = tiles[:, z * 4 : (z + 1) * 4].astype(bf16)


def route_kernel(matching, mid, out):
    rel = [jnp.zeros((4, 128), f32), jnp.zeros((4, 128), f32)]
    for d in range(64):
        rel[d % 2] = rel[d % 2] + (mid[d, 0, 2].astype(f32) + mid[d, 1, 2].astype(f32))
    for d in range(64):
        target = matching[d]
        tail = jnp.where(target % 2 == 0, rel[0], rel[1]).astype(bf16)
        for z in range(2):
            out[target, z, 0] = (mid[d, 0, z].astype(f32) + mid[d, 1, z].astype(f32)).astype(bf16)
            out[target, z, 1] = tail


def whole(last, h, p):
    span = slice(h * 32, (h + 1) * 32)
    parts = [last[span, z, p].astype(f32) for z in range(2)]
    return jnp.concatenate(parts, axis=1).reshape(256, 128)


def rel_kernel(last, out):
    for h in range(2):
        part = whole(last, h, 1).astype(bf16)
        for k in range(4):
            out[k, :, h * 128 : (h + 1) * 128] = part


def to_row(column):
    return jnp.broadcast_to(column, (256, 128)).T[0:1]


def to_column(row):
    return jnp.broadcast_to(row, (128, 256)).T[:, 0:1]


def rows_kernel(emb, accum, own0, own1, own2, own3, last, new_emb, new_accum):
    grad = own0[...]
    for own in (own1, own2, own3):
        grad = grad + own[...].astype(f32)
    grad = grad + jnp.concatenate([whole(last, 0, 0), whole(last, 1, 0)], axis=1)
    total = to_column(accum[...]) + jnp.mean(grad * grad, axis=1, keepdims=True)
    new_emb[...] = emb[...] - grad * (learn_rate / jnp.sqrt(total))
    new_accum[...] = to_row(total)


def update_kernel(place, rel, accum, grads, *rest):
    if len(rest) == 6:
        core, (seen, held, new_rel, new_accum, block, sem) = 1 - place[0], rest
    else:
        core, (new_rel, new_accum, block, sem) = place[0], rest
    old = jnp.concatenate([accum[...], accum[...]], axis=0)
    column = jnp.where(core == 0, old[0:8], old[4:12]).T
    totals, copies = [], []
    for r in range(4):
        grad = grads[r].astype(f32)
        total = column[:, r : r + 1] + jnp.mean(grad * grad, axis=1, keepdims=True)
        block[r] = rel[4 * core + r] - grad * (learn_rate / jnp.sqrt(total))
        totals.append(total)
        copies.append(pltpu.make_async_copy(block.at[r], new_rel.at[4 * core + r], sem.at[r]))
        copies[r].start()
    rows = jnp.concatenate(totals + totals, axis=1).T
    if len(rest) == 6:
        first = jnp.concatenate([held[...], held[...]], axis=0)
        mixed = jnp.concatenate([rows[0:4], first[0:4]], axis=0)
        turned = jnp.concatenate([first[0:4], rows[0:4]], axis=0)
        new_accum[...] = jnp.where(core == 0, mixed, turned)
    else:
        new_accum[...] = rows
    for copy in copies:
        copy.wait()


def update_half(place, relations, rel_accum, grads, before=None):
    given = (place, relations, rel_accum, grads) + (before or ())
    specs = [SMEM, VMEM, VMEM, VMEM] + ([ANY, VMEM] if before else [])
    return pl.pallas_call(
        update_kernel,
        out_shape=(shape((8, 256, 256), f32), shape((8, 256), f32)),
        in_specs=specs,
        out_specs=(ANY, VMEM),
        scratch_shapes=[pltpu.VMEM((4, 256, 256), f32), pltpu.SemaphoreType.DMA((4,))],
        input_output_aliases={4: 0} if before else {},
        compiler_params=pltpu.CompilerParams(vmem_limit_bytes=8 * 1024 * 1024),
        cost_estimate=pl.CostEstimate(flops=0, bytes_accessed=3_000_000, transcendentals=0),
    )(*given)


def body(
    embeddings, row_accum, relations, rel_accum, matching, src_rows, dst_rows, rel_ids, neg_rows
):
    place = jnp.stack([lax.axis_index(name) for name in ("core", "zhi", "x")]).astype(jnp.int32)
    line = lambda v: v.reshape(1, 512)
    pieces, pack = call(
        first_kernel,
        (shape((64, 8, 128), bf16), shape((272, 256), bf16)),
        0,
        (embeddings, line(src_rows), line(rel_ids), line(dst_rows), line(neg_rows)),
        moved=800_000,
        far=(0, 1, 2, 3, 4),
        space=62,
        scratch=[
            pltpu.VMEM((256, 256), f32),
            pltpu.VMEM((4, 1, 512), jnp.int32),
            pltpu.SemaphoreType.DMA((5,)),
        ],
    )
    arrived = spread(pieces, DOM)
    rel_b = call(
        cast_kernel,
        shape((8, 256, 256), bf16),
        0,
        (relations,),
        moved=3_000_000,
        far=(0,),
        far_outs=(0,),
        scratch=[
            pltpu.VMEM((8, 256, 256), f32),
            pltpu.VMEM((8, 256, 256), bf16),
            pltpu.SemaphoreType.DMA((16,)),
        ],
        space=62,
    )
    packs = [pack] + [
        lax.ppermute(pack, "x", [(i, i ^ k) for i in range(4)]) for k in range(1, 4)
    ]
    packs[1], rel_b, arrived = lax.optimization_barrier((packs[1], rel_b, arrived))
    routed = call(take_kernel, shape((64, 2, 8, 128), bf16), 1, (matching, arrived), moved=400_000)
    rows_in = spread(routed.reshape(128, 8, 128), DOM_Z).reshape(64, 2, 8, 128)
    block = shape((1024, 256), bf16)
    known_shape = shape((16, 512), f32)
    counts, known0, trans0, source0 = call(
        trans_kernel,
        (shape((8, 512), f32), known_shape, block, block),
        1,
        (place, packs[0], packs[1], rel_b),
        flops=1_300_000_000,
        moved=3_000_000,
        space=16,
    )
    four = shape((4, 256, 256), bf16)
    weight, g_trans, given, known1, trans1, source1 = call(
        score_kernel,
        (shape((2048, 512), bf16), shape((2048, 256), bf16), four, known_shape, block, block),
        1,
        (place, rows_in, packs[2], packs[3], rel_b, counts, known0, trans0, source0),
        flops=4_500_000_000,
        moved=6_000_000,
        scratch=[pltpu.VMEM((512, 256), bf16)],
        space=28,
    )
    came = swap(given, "core")
    g_rows, kept = call(
        partner_kernel,
        (shape((2, 256, 256), bf16), four),
        1,
        (place, weight, trans0, trans1, g_trans, known0, known1, source0, source1),
        flops=2_500_000_000,
        moved=4_000_000,
        space=16,
    )
    came, g_rows = lax.optimization_barrier((came, g_rows))
    got = spread(call(join_kernel, four, 0, (kept, came), moved=1_500_000), "x")
    one = shape((256, 256), bf16)
    owns = call(
        own_kernel,
        (shape((256, 256), f32), one, one, one),
        0,
        (g_trans, known0, known1, rel_b),
        flops=3_000_000_000,
        moved=4_000_000,
        space=16,
    )
    away = lambda part, k: lax.ppermute(part, "x", [(i, i ^ k) for i in range(4)])
    first = away(owns[1], 1)
    out = call(
        pieces_kernel, shape((64, 2, 3, 4, 128), bf16), 0, (got, g_rows), moved=2_000_000
    )
    mid = spread(out.reshape(128, 3, 4, 128), DOM_Z)
    first, *others, mid = lax.optimization_barrier((first, *owns[2:], mid))
    others = [away(part, k) for k, part in enumerate(others, 2)]
    routed_back = call(
        route_kernel,
        shape((64, 2, 2, 4, 128), bf16),
        1,
        (matching, mid.reshape(64, 2, 3, 4, 128)),
        moved=512_000,
    )
    last = spread(routed_back.reshape(128, 2, 4, 128), DOM_Z).reshape(64, 2, 2, 4, 128)
    *others, last = lax.optimization_barrier((*others, last))
    rel_four = spread(call(rel_kernel, four, 0, (last,), moved=512_000), "x")
    new_embeddings, new_row_accum = call(
        rows_kernel,
        (shape((256, 256), f32), shape((1, 256), f32)),
        0,
        (embeddings, row_accum.reshape(1, 256), owns[0], first, *others, last),
        flops=1_000_000,
        moved=1_000_000,
    )
    new_embeddings, rel_four = lax.optimization_barrier((new_embeddings, rel_four))
    rel_rest = swap(rel_four, "core")
    half = update_half(place, relations, rel_accum, rel_four)
    new_relations, new_rel_accum = update_half(place, relations, rel_accum, rel_rest, half)
    return new_embeddings, new_row_accum.reshape(256), new_relations, new_rel_accum


def solution(mesh):
    fine = Mesh(mesh.devices.reshape(4, 8, 2, 2, 4), AXES)
    placed = (
        P(AXES, None),
        P(AXES),
        P(),
        P(),
        P(),
        P(AXES),
        P(AXES),
        P(AXES),
        P(AXES, None),
    )
    return jax.shard_map(
        body,
        mesh=fine,
        in_specs=placed,
        out_specs=(P(AXES, None), P(AXES), P(), P()),
        check_vma=False,
    )
```

```python
import jax
import jax.numpy as jnp
from jax import lax
from jax.experimental import pallas as pl
from jax.experimental.pallas import tpu as pltpu
from jax.sharding import Mesh, PartitionSpec as P

learn_rate = 0.1
AXES = ("zlo", "y", "core", "zhi", "x")
DOM = ("zlo", "y", "core")
DOM_Z = DOM + ("zhi",)
bf16 = jnp.bfloat16
f32 = jnp.float32
VMEM = pl.BlockSpec(memory_space=pltpu.VMEM)
ANY = pl.BlockSpec(memory_space=pltpu.HBM)
SMEM = pl.BlockSpec(memory_space=pltpu.SMEM)
NN = (((1,), (0,)), ((), ()))
NT = (((1,), (1,)), ((), ()))


def shape(dims, dtype):
    return jax.ShapeDtypeStruct(dims, dtype)


def dot(a, b, dims=NN):
    return lax.dot_general(a, b, dims, preferred_element_type=f32)


def call(kernel, outs, scalars, args, flops=0, moved=0, scratch=(), space=8, far=(), far_outs=()):
    specs = [SMEM] * scalars + [ANY if k in far else VMEM for k in range(scalars, len(args))]
    many = isinstance(outs, tuple)
    return pl.pallas_call(
        kernel,
        out_shape=outs,
        in_specs=specs,
        out_specs=tuple(ANY if k in far_outs else VMEM for k in range(len(outs))) if many else (ANY if far_outs else VMEM),
        scratch_shapes=list(scratch),
        compiler_params=pltpu.CompilerParams(vmem_limit_bytes=space * 1024 * 1024),
        cost_estimate=pl.CostEstimate(flops=flops, bytes_accessed=moved, transcendentals=0),
    )(*args)


def swap(value, axis):
    return lax.ppermute(value, axis, [(0, 1), (1, 0)])


def spread(value, axis):
    return lax.all_to_all(value, axis, split_axis=0, concat_axis=0, tiled=True)


def first_kernel(emb, src, rel, dst, neg, pieces, pack, rows, index, sems):
    copies = [pltpu.make_async_copy(emb, rows, sems.at[0])]
    for k, part in enumerate((src, rel, dst, neg)):
        copies.append(pltpu.make_async_copy(part, index.at[k], sems.at[k + 1]))
    for copy in copies:
        copy.start()
    for copy in copies:
        copy.wait()
    wide = jnp.concatenate([index[k] for k in range(4)], axis=0)
    high = wide // 256
    low = (wide - high * 256).astype(f32)
    both = jnp.concatenate([high.astype(f32), low], axis=0)
    pack[256:272, :] = jnp.concatenate([both[:, :256], both[:, 256:]], axis=0).astype(bf16)
    pack[0:256, :] = rows[...].astype(bf16)
    for h in range(2):
        half = rows[:, h * 128 : (h + 1) * 128]
        pieces[h * 32 : (h + 1) * 32] = half.reshape(32, 8, 128).astype(bf16)


def take_kernel(matching, arrived, routed):
    for d in range(64):
        piece = arrived[matching[d]]
        routed[d, 0] = piece
        routed[d, 1] = piece


def indices(part):
    part = part.astype(f32)
    both = jnp.concatenate([part[0:8], part[8:16]], axis=1)
    return both[0:4] * 256.0 + both[4:8]


def columns(value):
    return jnp.concatenate([value, value], axis=0).T


def lane_ids(rows, width):
    return lax.broadcasted_iota(jnp.int32, (rows, width), 1)


def row_ids(x, rows):
    ids = lane_ids(rows, 512)
    return (ids + jnp.where(ids >= 256, 768, 0) + x * 256).astype(f32)


def by_relation(kinds, rows):
    wide = jnp.broadcast_to(kinds, rows.shape).astype(bf16)
    parts = [jnp.where(wide == bf16(r), rows, bf16(0)) for r in range(8)]
    return jnp.concatenate(parts, axis=1)


def cast_kernel(rel, rel_b, wide, narrow, sems):
    taken = [pltpu.make_async_copy(rel.at[r], wide.at[r], sems.at[r]) for r in range(8)]
    given = [pltpu.make_async_copy(narrow.at[r], rel_b.at[r], sems.at[8 + r]) for r in range(8)]
    for copy in taken:
        copy.start()
    for r in range(8):
        taken[r].wait()
        narrow[r] = wide[r].astype(bf16)
        given[r].start()
    for copy in given:
        copy.wait()


def span_work(x, pack, stack):
    index = indices(pack[256:272, :])
    column = columns(index)
    hot = (column[:, 0:1] == lane_ids(512, 256).astype(f32)).astype(f32).astype(bf16)
    rows = dot(hot, pack[0:256, :]).astype(bf16)
    turned = dot(by_relation(column[:, 1:2], rows), stack, NT).astype(bf16)
    hits = (column[:, 3:4] == row_ids(x, 512)).astype(f32)
    return index, rows, turned, jnp.sum(hits, axis=0, keepdims=True)


def trans_kernel(place, pack0, pack1, rel_b, counts, known, trans, source):
    stack = jnp.concatenate([rel_b[r] for r in range(8)], axis=1)
    for s, pack in enumerate((pack0, pack1)):
        index, rows, turned, count = span_work(place[2], pack, stack)
        known[s * 8 : (s + 1) * 8, :] = jnp.concatenate([index, index], axis=0)
        source[s * 512 : (s + 1) * 512, :] = rows
        trans[s * 512 : (s + 1) * 512, :] = turned
        counts[s : s + 1, :] = count
    counts[2:8, :] = jnp.zeros((6, 512), f32)


def score_kernel(
    place, rows_in, pack2, pack3, rel_b, counts, known, trans, source,
    weight, g_trans, kept, given, known1, trans1, rows, source1
):
    core = place[0]
    for z in range(2):
        both = rows_in[:, z].reshape(2, 256, 128)
        rows[z * 256 : (z + 1) * 256, :] = jnp.concatenate([both[0], both[1]], axis=1)
    index = [known[s * 8 : s * 8 + 4, :] for s in range(2)]
    count = [counts[s : s + 1, :] for s in range(2)]
    stack = jnp.concatenate([rel_b[r] for r in range(8)], axis=1)
    for s, pack in enumerate((pack2, pack3)):
        one, away, turned, many = span_work(place[2], pack, stack)
        known1[s * 8 : (s + 1) * 8, :] = jnp.concatenate([one, one], axis=0)
        source1[s * 512 : (s + 1) * 512, :] = away
        trans1[s * 512 : (s + 1) * 512, :] = turned
        index.append(one)
        count.append(many)
    ids = row_ids(place[2], 256)
    for b in range(8):
        s = b // 2
        column = columns(index[s])[(b % 2) * 256 : (b % 2 + 1) * 256]
        span = slice(b * 256, (b + 1) * 256)
        turned = (trans, trans1)[b // 4][(b % 4) * 256 : (b % 4 + 1) * 256, :]
        score = dot(turned, rows[...], NT)
        sig = 1.0 / (1.0 + jnp.exp(-score))
        hit = column[:, 2:3] == ids
        part = jnp.where(hit, (count[s] + 1.0) * sig - 1.0, count[s] * sig).astype(bf16)
        weight[span, :] = part
        g_trans[span, :] = dot(part, rows[...]).astype(bf16)
    turned = g_trans[...].astype(f32).T
    kinds = jnp.concatenate([part[1:2] for part in index], axis=1)
    every = jnp.concatenate([source[...], source1[...]], axis=0)
    for r in range(8):
        wanted = r + 4 * core if r < 4 else r - 4 * core
        masked = jnp.where(kinds == wanted.astype(f32), turned, 0.0).astype(bf16)
        grad = dot(masked, every).astype(bf16)
        if r < 4:
            kept[r] = grad
        else:
            given[r - 4] = grad


def partner_kernel(weight, trans0, trans1, g_rows):
    turned = jnp.concatenate([t[...].astype(f32).T.astype(bf16) for t in (trans0, trans1)], axis=1)
    for z in range(2):
        g_rows[z] = dot(turned, weight[:, z * 256 : (z + 1) * 256]).T.astype(bf16)


def own_kernel(g_trans, known0, known1, rel_b, *owns):
    sub_ids = lax.broadcasted_iota(jnp.int32, (256, 512), 0).astype(f32)
    stack = rel_b[...].reshape(2048, 256)
    for s in range(4):
        index = (known0, known1)[s // 2][(s % 2) * 8 : (s % 2 + 1) * 8, :]
        grad = g_trans[s * 512 : (s + 1) * 512, :]
        kinds = columns(index[0:4])[:, 1:2]
        parts = [
            dot(by_relation(kinds[h : h + 128], grad[h : h + 128]), stack).astype(bf16)
            for h in range(0, 512, 128)
        ]
        hot = (index[0:1, :] == sub_ids).astype(f32).astype(bf16)
        mine = dot(hot, jnp.concatenate(parts, axis=0))
        owns[s][...] = mine.astype(owns[s].dtype)


def join_kernel(kept, came, out):
    for k in range(4):
        out[k] = (kept[k].astype(f32) + came[k].astype(f32)).astype(bf16)


def pieces_kernel(got, g_rows, out):
    for h in range(2):
        half = slice(h * 128, (h + 1) * 128)
        rel = got[0, :, half].astype(f32)
        for k in range(1, 4):
            rel = rel + got[k, :, half].astype(f32)
        for p, part in enumerate((g_rows[0, :, half].astype(f32), g_rows[1, :, half].astype(f32), rel)):
            tiles = part.reshape(32, 8, 128)
            for z in range(2):
                out[h * 32 : (h + 1) * 32, z, p] = tiles[:, z * 4 : (z + 1) * 4].astype(bf16)


def route_kernel(matching, mid, out):
    rel = [jnp.zeros((4, 128), f32), jnp.zeros((4, 128), f32)]
    for d in range(64):
        rel[d % 2] = rel[d % 2] + (mid[d, 0, 2].astype(f32) + mid[d, 1, 2].astype(f32))
    for d in range(64):
        target = matching[d]
        tail = jnp.where(target % 2 == 0, rel[0], rel[1]).astype(bf16)
        for z in range(2):
            out[target, z, 0] = (mid[d, 0, z].astype(f32) + mid[d, 1, z].astype(f32)).astype(bf16)
            out[target, z, 1] = tail


def whole(last, h, p):
    span = slice(h * 32, (h + 1) * 32)
    parts = [last[span, z, p].astype(f32) for z in range(2)]
    return jnp.concatenate(parts, axis=1).reshape(256, 128)


def rel_kernel(last, out):
    for h in range(2):
        part = whole(last, h, 1).astype(bf16)
        for k in range(4):
            out[k, :, h * 128 : (h + 1) * 128] = part


def to_row(column):
    return jnp.broadcast_to(column, (256, 128)).T[0:1]


def to_column(row):
    return jnp.broadcast_to(row, (128, 256)).T[:, 0:1]


def rows_kernel(emb, accum, own0, own1, own2, own3, last, new_emb, new_accum):
    grad = own0[...]
    for own in (own1, own2, own3):
        grad = grad + own[...].astype(f32)
    grad = grad + jnp.concatenate([whole(last, 0, 0), whole(last, 1, 0)], axis=1)
    total = to_column(accum[...]) + jnp.mean(grad * grad, axis=1, keepdims=True)
    new_emb[...] = emb[...] - grad * (learn_rate / jnp.sqrt(total))
    new_accum[...] = to_row(total)


def update_kernel(place, rel, accum, grads, *rest):
    if len(rest) == 6:
        core, (seen, held, new_rel, new_accum, block, sem) = 1 - place[0], rest
    else:
        core, (new_rel, new_accum, block, sem) = place[0], rest
    old = jnp.concatenate([accum[...], accum[...]], axis=0)
    column = jnp.where(core == 0, old[0:8], old[4:12]).T
    totals, copies = [], []
    for r in range(4):
        grad = grads[r].astype(f32)
        total = column[:, r : r + 1] + jnp.mean(grad * grad, axis=1, keepdims=True)
        block[r] = rel[4 * core + r] - grad * (learn_rate / jnp.sqrt(total))
        totals.append(total)
        copies.append(pltpu.make_async_copy(block.at[r], new_rel.at[4 * core + r], sem.at[r]))
        copies[r].start()
    rows = jnp.concatenate(totals + totals, axis=1).T
    if len(rest) == 6:
        first = jnp.concatenate([held[...], held[...]], axis=0)
        mixed = jnp.concatenate([rows[0:4], first[0:4]], axis=0)
        turned = jnp.concatenate([first[0:4], rows[0:4]], axis=0)
        new_accum[...] = jnp.where(core == 0, mixed, turned)
    else:
        new_accum[...] = rows
    for copy in copies:
        copy.wait()


def update_half(place, relations, rel_accum, grads, before=None):
    given = (place, relations, rel_accum, grads) + (before or ())
    specs = [SMEM, VMEM, VMEM, VMEM] + ([ANY, VMEM] if before else [])
    return pl.pallas_call(
        update_kernel,
        out_shape=(shape((8, 256, 256), f32), shape((8, 256), f32)),
        in_specs=specs,
        out_specs=(ANY, VMEM),
        scratch_shapes=[pltpu.VMEM((4, 256, 256), f32), pltpu.SemaphoreType.DMA((4,))],
        input_output_aliases={4: 0} if before else {},
        compiler_params=pltpu.CompilerParams(vmem_limit_bytes=8 * 1024 * 1024),
        cost_estimate=pl.CostEstimate(flops=0, bytes_accessed=3_000_000, transcendentals=0),
    )(*given)


def body(
    embeddings, row_accum, relations, rel_accum, matching, src_rows, dst_rows, rel_ids, neg_rows
):
    place = jnp.stack([lax.axis_index(name) for name in ("core", "zhi", "x")]).astype(jnp.int32)
    line = lambda v: v.reshape(1, 512)
    pieces, pack = call(
        first_kernel,
        (shape((64, 8, 128), bf16), shape((272, 256), bf16)),
        0,
        (embeddings, line(src_rows), line(rel_ids), line(dst_rows), line(neg_rows)),
        moved=800_000,
        far=(0, 1, 2, 3, 4),
        space=62,
        scratch=[
            pltpu.VMEM((256, 256), f32),
            pltpu.VMEM((4, 1, 512), jnp.int32),
            pltpu.SemaphoreType.DMA((5,)),
        ],
    )
    arrived = spread(pieces, DOM)
    rel_b = call(
        cast_kernel,
        shape((8, 256, 256), bf16),
        0,
        (relations,),
        moved=3_000_000,
        far=(0,),
        far_outs=(0,),
        scratch=[
            pltpu.VMEM((8, 256, 256), f32),
            pltpu.VMEM((8, 256, 256), bf16),
            pltpu.SemaphoreType.DMA((16,)),
        ],
        space=62,
    )
    packs = [pack] + [
        lax.ppermute(pack, "x", [(i, i ^ k) for i in range(4)]) for k in range(1, 4)
    ]
    rel_b, arrived = lax.optimization_barrier((rel_b, arrived))
    routed = call(take_kernel, shape((64, 2, 8, 128), bf16), 1, (matching, arrived), moved=400_000)
    rows_in = spread(routed.reshape(128, 8, 128), DOM_Z).reshape(64, 2, 8, 128)
    block = shape((1024, 256), bf16)
    known_shape = shape((16, 512), f32)
    counts, known0, trans0, source0 = call(
        trans_kernel,
        (shape((8, 512), f32), known_shape, block, block),
        1,
        (place, packs[0], packs[1], rel_b),
        flops=1_300_000_000,
        moved=3_000_000,
        space=16,
    )
    four = shape((4, 256, 256), bf16)
    weight, g_trans, kept, given, known1, trans1 = call(
        score_kernel,
        (shape((2048, 512), bf16), shape((2048, 256), bf16), four, four, known_shape, block),
        1,
        (place, rows_in, packs[2], packs[3], rel_b, counts, known0, trans0, source0),
        flops=4_500_000_000,
        moved=6_000_000,
        scratch=[pltpu.VMEM((512, 256), bf16), pltpu.VMEM((1024, 256), bf16)],
        space=28,
    )
    came = swap(given, "core")
    g_rows = call(
        partner_kernel,
        shape((2, 256, 256), bf16),
        0,
        (weight, trans0, trans1),
        flops=1_500_000_000,
        moved=4_000_000,
        space=16,
    )
    came, g_rows = lax.optimization_barrier((came, g_rows))
    got = spread(call(join_kernel, four, 0, (kept, came), moved=1_500_000), "x")
    one = shape((256, 256), bf16)
    owns = call(
        own_kernel,
        (shape((256, 256), f32), one, one, one),
        0,
        (g_trans, known0, known1, rel_b),
        flops=3_000_000_000,
        moved=4_000_000,
        space=16,
    )
    away = lambda part, k: lax.ppermute(part, "x", [(i, i ^ k) for i in range(4)])
    first = away(owns[1], 1)
    out = call(
        pieces_kernel, shape((64, 2, 3, 4, 128), bf16), 0, (got, g_rows), moved=2_000_000
    )
    mid = spread(out.reshape(128, 3, 4, 128), DOM_Z)
    first, *others, mid = lax.optimization_barrier((first, *owns[2:], mid))
    others = [away(part, k) for k, part in enumerate(others, 2)]
    routed_back = call(
        route_kernel,
        shape((64, 2, 2, 4, 128), bf16),
        1,
        (matching, mid.reshape(64, 2, 3, 4, 128)),
        moved=512_000,
    )
    last = spread(routed_back.reshape(128, 2, 4, 128), DOM_Z).reshape(64, 2, 2, 4, 128)
    *others, last = lax.optimization_barrier((*others, last))
    rel_four = spread(call(rel_kernel, four, 0, (last,), moved=512_000), "x")
    new_embeddings, new_row_accum = call(
        rows_kernel,
        (shape((256, 256), f32), shape((1, 256), f32)),
        0,
        (embeddings, row_accum.reshape(1, 256), owns[0], first, *others, last),
        flops=1_000_000,
        moved=1_000_000,
    )
    new_embeddings, rel_four = lax.optimization_barrier((new_embeddings, rel_four))
    rel_rest = swap(rel_four, "core")
    half = update_half(place, relations, rel_accum, rel_four)
    new_relations, new_rel_accum = update_half(place, relations, rel_accum, rel_rest, half)
    return new_embeddings, new_row_accum.reshape(256), new_relations, new_rel_accum


def solution(mesh):
    fine = Mesh(mesh.devices.reshape(4, 8, 2, 2, 4), AXES)
    placed = (
        P(AXES, None),
        P(AXES),
        P(),
        P(),
        P(),
        P(AXES),
        P(AXES),
        P(AXES),
        P(AXES, None),
    )
    return jax.shard_map(
        body,
        mesh=fine,
        in_specs=placed,
        out_specs=(P(AXES, None), P(AXES), P(), P()),
        check_vma=False,
    )
```
